32 devices in a mesh: groups: 2 (over x), dp: 16 (over z, y, core).
Axes of the slice: x: 2, y: 2, z: 4, core: 2. Of those that a mesh axis runs over, the one named last changes fastest.
Arguments:
- activations: bfloat16 [12288, 8192], P(('groups', 'dp')), parts along dimension 0, may hold values from -6 to 6
- out_grads: bfloat16 [12288, 4096], P(('groups', 'dp')), parts along dimension 0, may hold values from -0.109375 to 0.109375
- projector: bfloat16 [16384, 512], P(('groups', 'dp')), parts along dimension 0, may hold values from -0.0625 to 0.0625
- first_moment: float32 [8192, 512], P(('groups', 'dp')), parts along dimension 0, may hold values from -6 to 6
- second_moment: float32 [8192, 512], P(('groups', 'dp')), parts along dimension 0, may hold values from 0.02 to 0.5
Outputs:
- update: bfloat16 [8192, 8192], P('groups', 'dp'), parts along dimension 0
- new_first: float32 [8192, 512], P(('groups', 'dp')), parts along dimension 0
- new_second: float32 [8192, 512], P(('groups', 'dp')), parts along dimension 0
The draws below stay inside these ranges and needn't reach their ends.
There are 2 independent parts, one for each index of `groups`. The reference program is written for one: setup_inputs(seed, part) draws one part's arguments, and reference() takes and returns one part's arrays. A program takes and returns all parts, laid end to end along the dimension named above; each array names one. Nothing has to cross between parts.
All inputs are finite; a program needn't handle non-finite values.
Results may differ from the reference program's by a relative error of at most 0.005.
Values may be sent and summed in bfloat16 or wider, within the bound.
No kernel may reach another device: no remote copies, remote signals or barrier semaphores. Data moves between devices by JAX's collectives and lax.ppermute only.
A program may use at most 128 MiB of HBM per device.

```python
import math
import jax
import jax.numpy as jnp
from jax import lax

D = 8192
RANK = 512
STEP = 100
NQ = 4096
TOKENS = 6144


def spiked(result, rng, source, target, shards_of, factor):
    def block_of(axis_at):
        return (jnp.arange(result.shape[axis_at]) // (result.shape[axis_at] // shards_of)).reshape((-1,) + (1,) * (result.ndim - 1 - axis_at))

    near = jax.random.permutation(rng, shards_of)[block_of(target)]
    second = (block_of(target) + shards_of // 2) % shards_of
    return jnp.where((block_of(source) == near) | (block_of(source) == second), factor * result, result)


def block_scale(own_key, extent, pieces, low, top_value):
    level, own = 1.0, jax.random.fold_in(own_key, 6)
    for position, parts in pieces:
        draws = jnp.exp(jax.random.uniform(jax.random.fold_in(own, position), (parts,), jnp.float32, low / len(pieces), top_value / len(pieces)))
        level = level * jnp.repeat(draws, extent[position] // parts).reshape([-1 if axis == position else 1 for axis in range(len(extent))])
    return level


def centred(key, extent, spread, limit, split=(), held_as=jnp.bfloat16):
    entries = spread * jax.random.normal(key, extent, jnp.float32)
    if split:
        entries = entries * block_scale(key, extent, split, -0.22, 0.18)
    return jnp.clip(entries, -limit, limit).astype(held_as)


def bell_draw_with(key, dims, deviation, limit, cuts, heavy, dtype=jnp.bfloat16):
    entries = deviation * jax.random.normal(key, dims, jnp.float32)
    if cuts:
        entries = entries * block_scale(key, dims, cuts, -0.22, 0.18)
    return jnp.clip(spiked(entries, jax.random.fold_in(key, 3), *heavy), -limit, limit).astype(dtype)


def setup_inputs(seed: int = 0, part: int = 0) -> dict:
    key_of = jax.random.split(jax.random.key(seed), 6)
    part_keys = jax.random.split(jax.random.fold_in(key_of[5], part), 6)
    activations = centred(part_keys[0], (TOKENS, D), 1.0, 6.0, ((0, 16),))
    out_grads = bell_draw_with(part_keys[1], (TOKENS, NQ), TOKENS ** -0.5, 0.109375, ((0, 16),), (0, 1, 16, 2.0))
    projector = centred(part_keys[2], (D, RANK), D ** -0.5, 0.0625, ((0, 16),))
    first_moment = centred(part_keys[3], (NQ, RANK), 1.0, 6.0, ((0, 16),), jnp.float32)
    second_moment = jnp.clip(jnp.exp(math.log(0.5) - 3.218876 * jax.random.uniform(part_keys[4], (NQ, RANK), jnp.float32) ** block_scale(part_keys[4], (NQ, RANK), ((0, 16),), -0.2, 0.2)), 0.02, 0.5)
    return dict(activations=activations, out_grads=out_grads, projector=projector, first_moment=first_moment, second_moment=second_moment)


decay_first = 0.9
decay_second = 0.999
epsilon = 1e-08

def reference(activations, out_grads, projector, first_moment, second_moment):
    projected = jnp.dot(activations, projector, preferred_element_type=jnp.float32).astype(jnp.bfloat16)
    reduced = lax.dot_general(out_grads, projected, (((0,), (0,)), ((), ())), preferred_element_type=jnp.float32)
    new_first = decay_first * first_moment + (1.0 - decay_first) * reduced
    new_second = decay_second * second_moment + (1.0 - decay_second) * reduced * reduced
    first_fix = 1.0 - decay_first ** STEP
    second_fix = 1.0 - decay_second ** STEP
    direction = (new_first / first_fix / (jnp.sqrt(new_second / second_fix) + epsilon)).astype(jnp.bfloat16)
    update = lax.dot_general(direction, projector, (((1,), (1,)), ((), ())), preferred_element_type=jnp.float32).astype(jnp.bfloat16)
    return (update, new_first, new_second)
```

```python
import functools
import jax
import jax.numpy as jnp
from jax import lax
from jax.experimental import pallas as pl
from jax.experimental.pallas import tpu as pltpu
from jax.sharding import PartitionSpec as P

STEP = 100

decay_first = 0.9
decay_second = 0.999
epsilon = 1e-08

CHUNKS = 2
F32, BF16 = jnp.float32, jnp.bfloat16
VMEM_LIMIT = 40 * 1024 * 1024


def adam(reduced, first_moment, second_moment):
    new_first = decay_first * first_moment + (1.0 - decay_first) * reduced
    new_second = decay_second * second_moment + (1.0 - decay_second) * reduced * reduced
    first_fix = 1.0 - decay_first**STEP
    second_fix = 1.0 - decay_second**STEP
    direction = (new_first / first_fix / (jnp.sqrt(new_second / second_fix) + epsilon)).astype(BF16)
    return new_first, new_second, direction


def plain(activations, out_grads, projector, first_moment, second_moment):
    projected = jnp.dot(
        activations,
        lax.all_gather(projector, "dp", axis=0, tiled=True),
        preferred_element_type=F32,
    ).astype(BF16)
    reduced = lax.psum_scatter(
        lax.dot_general(out_grads, projected, (((0,), (0,)), ((), ())), preferred_element_type=F32),
        "dp",
        scatter_dimension=0,
        tiled=True,
    )
    new_first, new_second, direction = adam(reduced, first_moment, second_moment)
    update = lax.dot_general(
        lax.all_gather(direction, "dp", axis=0, tiled=True),
        projector,
        (((1,), (1,)), ((), ())),
        preferred_element_type=F32,
    ).astype(BF16)
    return update, new_first, new_second


def params():
    return pltpu.CompilerParams(vmem_limit_bytes=VMEM_LIMIT)


def cost(flops, moved):
    return pl.CostEstimate(flops=flops, bytes_accessed=moved, transcendentals=0)


def pick(array, at, width):
    rows, many = array.shape[0], at.shape[0]

    def kernel(at_ref, in_ref, out_ref):
        out_ref[...] = in_ref[...]

    return pl.pallas_call(
        kernel,
        grid_spec=pltpu.PrefetchScalarGridSpec(
            num_scalar_prefetch=1,
            grid=(many,),
            in_specs=[pl.BlockSpec((rows, width), lambda j, at_ref: (0, at_ref[j]))],
            out_specs=pl.BlockSpec((rows, width), lambda j, at_ref: (0, j)),
        ),
        out_shape=jax.ShapeDtypeStruct((rows, many * width), array.dtype),
        compiler_params=params(),
        cost_estimate=cost(0, 4 * rows * many * width),
        name="pick",
    )(at, array)


def project(activations, sibling, at, blocks):
    many, (depth, cols), rows = len(blocks), blocks[0].shape, activations.shape[0]

    def kernel(at_ref, own_ref, sib_ref, *refs):
        out_ref = refs[-1]
        for j in range(many):

            @pl.when(pl.program_id(0) == j)
            def _(j=j):
                block = refs[j][...]
                own = jnp.dot(own_ref[...], block, preferred_element_type=F32)
                sib = jnp.dot(sib_ref[...], block, preferred_element_type=F32)
                if j == 0:
                    out_ref[:rows, :] = own
                    out_ref[rows:, :] = sib
                else:
                    out_ref[:rows, :] += own
                    out_ref[rows:, :] += sib

    whole = pl.BlockSpec((depth, cols), lambda j, at_ref: (0, 0))
    return pl.pallas_call(
        kernel,
        grid_spec=pltpu.PrefetchScalarGridSpec(
            num_scalar_prefetch=1,
            grid=(many,),
            in_specs=[
                pl.BlockSpec((rows, depth), lambda j, at_ref: (0, at_ref[j])),
                pl.BlockSpec((rows, depth), lambda j, at_ref: (0, j)),
            ]
            + [whole] * many,
            out_specs=pl.BlockSpec((2 * rows, cols), lambda j, at_ref: (0, 0)),
        ),
        out_shape=jax.ShapeDtypeStruct((2 * rows, cols), F32),
        compiler_params=params(),
        cost_estimate=cost(4 * rows * depth * many * cols, 4 * rows * depth * many + 2 * depth * many * cols),
        name="project",
    )(at, activations, sibling, *blocks)


def outer(out_grads, sibling, at, mine, theirs, width):
    many, rows, cols = at.shape[0], out_grads.shape[0], mine.shape[1]
    half = many // 2
    dims = (((0,), (0,)), ((), ()))

    def kernel(at_ref, own_ref, sib_ref, mine_ref, theirs_ref, send_ref, keep_ref, held):
        j = pl.program_id(0)

        @pl.when(j == 0)
        def _():
            held[:rows, :] = (mine_ref[:rows, :] + theirs_ref[rows:, :]).astype(BF16)
            held[rows:, :] = (mine_ref[rows:, :] + theirs_ref[:rows, :]).astype(BF16)

        term = lax.dot_general(own_ref[...], held[:rows, :], dims, preferred_element_type=F32)
        term += lax.dot_general(sib_ref[...], held[rows:, :], dims, preferred_element_type=F32)

        @pl.when(j < half)
        def _():
            send_ref[0] = term.astype(BF16)

        @pl.when(j >= half)
        def _():
            keep_ref[0] = term

    whole = pl.BlockSpec((2 * rows, cols), lambda j, at_ref: (0, 0))
    return pl.pallas_call(
        kernel,
        grid_spec=pltpu.PrefetchScalarGridSpec(
            num_scalar_prefetch=1,
            grid=(many,),
            in_specs=[
                pl.BlockSpec((rows, width), lambda j, at_ref: (0, at_ref[j])),
                pl.BlockSpec((rows, width), lambda j, at_ref: (0, j)),
                whole,
                whole,
            ],
            out_specs=[
                pl.BlockSpec((1, width, cols), lambda j, at_ref: (jnp.minimum(j, half - 1), 0, 0)),
                pl.BlockSpec((1, width, cols), lambda j, at_ref: (jnp.maximum(j - half, 0), 0, 0)),
            ],
            scratch_shapes=[pltpu.VMEM((2 * rows, cols), BF16)],
        ),
        out_shape=[
            jax.ShapeDtypeStruct((half, width, cols), BF16),
            jax.ShapeDtypeStruct((half, width, cols), F32),
        ],
        compiler_params=params(),
        cost_estimate=cost(4 * rows * width * many * cols, 4 * rows * width * many + 6 * half * width * cols),
        name="outer",
    )(at, out_grads, sibling, mine, theirs)


def back(blocks, projector, at):
    many, chunks = len(blocks), len(blocks[0])
    (rows, cols), width = blocks[0][0].shape, projector.shape[0]
    flat = [part for block in blocks for part in block]

    def kernel(at_ref, projector_ref, *refs):
        out_ref = refs[-1]
        for j in range(many):

            @pl.when(pl.program_id(0) == j)
            def _(j=j):
                total = None
                for i in range(chunks):
                    term = lax.dot_general(
                        refs[j * chunks + i][...],
                        projector_ref[:, i * cols : (i + 1) * cols],
                        (((1,), (1,)), ((), ())),
                        preferred_element_type=F32,
                    )
                    total = term if total is None else total + term
                out_ref[...] = total.astype(BF16)

    return pl.pallas_call(
        kernel,
        grid_spec=pltpu.PrefetchScalarGridSpec(
            num_scalar_prefetch=1,
            grid=(many,),
            in_specs=[pl.BlockSpec(projector.shape, lambda j, at_ref: (0, 0))]
            + [pl.BlockSpec((rows, cols), lambda j, at_ref: (0, 0))] * len(flat),
            out_specs=pl.BlockSpec((rows, width), lambda j, at_ref: (at_ref[j], 0)),
        ),
        out_shape=jax.ShapeDtypeStruct((many * rows, width), BF16),
        compiler_params=params(),
        cost_estimate=cost(2 * many * rows * width * cols * chunks, 2 * many * rows * (width + cols * chunks)),
        name="back",
    )(at, projector, *flat)


def levels(activations, out_grads, projector, first_moment, second_moment, *, nz):
    me = lax.axis_index("dp")
    z, y, core = me // 4, me // 2 % 2, me % 2
    grid = [(a, b, c) for a in range(nz) for b in range(2) for c in range(2)]

    def pairs(to):
        return [((a * 2 + b) * 2 + c, (to(a, b, c)[0] * 2 + to(a, b, c)[1]) * 2 + to(a, b, c)[2]) for a, b, c in grid]

    def swap_core(x):
        return lax.ppermute(x, "dp", pairs(lambda a, b, c: (a, b, 1 - c)))

    def swap_y(x):
        return lax.ppermute(x, "dp", pairs(lambda a, b, c: (a, 1 - b, c)))

    def shift_z(x, k):
        return lax.ppermute(x, "dp", pairs(lambda a, b, c: ((a + k) % nz, b, c)))

    def index(k, dy, dc):
        return (lax.rem(z + nz + k, nz) * 2 + (1 - y if dy else y)) * 2 + (1 - core if dc else core)

    def named(*order):
        return jnp.stack([index(*o) for o in order]).astype(jnp.int32)

    ks = sorted(range(1, nz), key=lambda k: min(k, nz - k))
    depth, rank = projector.shape
    width = first_moment.shape[0]
    cols = rank // CHUNKS

    gathered = []
    for i in range(CHUNKS):
        own = projector[:, i * cols : (i + 1) * cols]
        line = [own] + [shift_z(own, k) for k in ks]
        gathered.append(line + [swap_y(x) for x in line])
    order_in = [(-k, dy) for dy in (0, 1) for k in [0] + ks]
    order_out = [(k, dy) for dy in (1, 0) for k in [0] + ks]
    a_sibling = swap_core(pick(activations, named(*[(k, dy, 1) for k, dy in order_in]), depth))
    g_sibling = swap_core(pick(out_grads, named(*[(k, dy, 1) for k, dy in order_out]), width))
    at_in = named(*[(k, dy, 0) for k, dy in order_in])
    at_out = named(*[(k, dy, 0) for k, dy in order_out])

    firsts, seconds, directions = [], [], []
    for i in range(CHUNKS):
        mine = project(activations, a_sibling, at_in, gathered[i])
        send, keep = outer(out_grads, g_sibling, at_out, mine, swap_core(mine), width)
        line = keep + swap_y(send).astype(F32)
        reduced = line[0]
        for at, k in enumerate(ks):
            reduced = reduced + shift_z(line[1 + at].astype(BF16), k).astype(F32)
        part = slice(i * cols, (i + 1) * cols)
        new_first, new_second, direction = adam(reduced, first_moment[:, part], second_moment[:, part])
        firsts.append(new_first)
        seconds.append(new_second)
        line = [direction] + [shift_z(direction, k) for k in ks]
        line = line + [swap_y(x) for x in line]
        directions.append(line + [swap_core(x) for x in line])
    order = [(-k, dy, dc) for dc in (0, 1) for dy in (0, 1) for k in [0] + ks]
    update = back(list(zip(*directions)), projector, named(*order))
    return update, jnp.concatenate(firsts, axis=1), jnp.concatenate(seconds, axis=1)


def solution(mesh):
    devices = mesh.shape["dp"]

    def body(activations, out_grads, projector, first_moment, second_moment):
        aligned = projector.shape[0] % 128 == 0 and first_moment.shape[0] % 128 == 0
        if devices % 4 or devices < 8 or not aligned:
            return plain(activations, out_grads, projector, first_moment, second_moment)
        return levels(activations, out_grads, projector, first_moment, second_moment, nz=devices // 4)

    placed = P(("groups", "dp"), None)
    return jax.shard_map(
        body,
        mesh=mesh,
        in_specs=(placed,) * 5,
        out_specs=(P("groups", "dp"), placed, placed),
        check_vma=False,
    )
```

```python
import functools
import jax
import jax.numpy as jnp
from jax import lax
from jax.experimental import pallas as pl
from jax.experimental.pallas import tpu as pltpu
from jax.sharding import PartitionSpec as P

STEP = 100

decay_first = 0.9
decay_second = 0.999
epsilon = 1e-08

CHUNKS = 2
F32, BF16 = jnp.float32, jnp.bfloat16
VMEM_LIMIT = 40 * 1024 * 1024


def adam(reduced, first_moment, second_moment):
    new_first = decay_first * first_moment + (1.0 - decay_first) * reduced
    new_second = decay_second * second_moment + (1.0 - decay_second) * reduced * reduced
    first_fix = 1.0 - decay_first**STEP
    second_fix = 1.0 - decay_second**STEP
    direction = (new_first / first_fix / (jnp.sqrt(new_second / second_fix) + epsilon)).astype(BF16)
    return new_first, new_second, direction


def plain(activations, out_grads, projector, first_moment, second_moment):
    projected = jnp.dot(
        activations,
        lax.all_gather(projector, "dp", axis=0, tiled=True),
        preferred_element_type=F32,
    ).astype(BF16)
    reduced = lax.psum_scatter(
        lax.dot_general(out_grads, projected, (((0,), (0,)), ((), ())), preferred_element_type=F32),
        "dp",
        scatter_dimension=0,
        tiled=True,
    )
    new_first, new_second, direction = adam(reduced, first_moment, second_moment)
    update = lax.dot_general(
        lax.all_gather(direction, "dp", axis=0, tiled=True),
        projector,
        (((1,), (1,)), ((), ())),
        preferred_element_type=F32,
    ).astype(BF16)
    return update, new_first, new_second


def params():
    return pltpu.CompilerParams(vmem_limit_bytes=VMEM_LIMIT)


def cost(flops, moved):
    return pl.CostEstimate(flops=flops, bytes_accessed=moved, transcendentals=0)


def pick(array, at, width, transposed):
    rows, many = array.shape[0], at.shape[0]

    def kernel(at_ref, in_ref, out_ref):
        out_ref[...] = in_ref[...].T if transposed else in_ref[...]

    if transposed:
        out_spec = pl.BlockSpec((width, rows), lambda j, at_ref: (j, 0))
        out_shape = jax.ShapeDtypeStruct((many * width, rows), array.dtype)
    else:
        out_spec = pl.BlockSpec((rows, width), lambda j, at_ref: (0, j))
        out_shape = jax.ShapeDtypeStruct((rows, many * width), array.dtype)
    return pl.pallas_call(
        kernel,
        grid_spec=pltpu.PrefetchScalarGridSpec(
            num_scalar_prefetch=1,
            grid=(many,),
            in_specs=[pl.BlockSpec((rows, width), lambda j, at_ref: (0, at_ref[j]))],
            out_specs=out_spec,
        ),
        out_shape=out_shape,
        compiler_params=params(),
        cost_estimate=cost(0, 4 * rows * many * width),
        name="pick",
    )(at, array)


def call(kernel, scalars, arrays, outs, scratch, *, flops, moved, name, aliases=None):
    anywhere = pl.BlockSpec(memory_space=pl.ANY)
    return pl.pallas_call(
        kernel,
        grid_spec=pltpu.PrefetchScalarGridSpec(
            num_scalar_prefetch=1,
            grid=(),
            in_specs=[anywhere] * len(arrays),
            out_specs=[anywhere] * len(outs),
            scratch_shapes=scratch,
        ),
        out_shape=outs,
        input_output_aliases=aliases or {},
        compiler_params=params(),
        cost_estimate=cost(flops, moved),
        name=name,
    )(scalars, *arrays)


def project(activations, sibling, first, at, blocks, before):
    chunks, many = len(blocks), len(blocks[0])
    (depth, cols), rows = blocks[0][0].shape, activations.shape[0]
    copies = many * (2 + chunks)
    flat = [block for chunk in blocks for block in chunk]
    held = [] if before is None else [before]

    def kernel(at_ref, own_ref, sib_ref, *refs):
        block_refs, out_ref = refs[: chunks * many], refs[chunks * many + len(held)]
        a, b, total, sems = refs[chunks * many + len(held) + 1 :]
        started = []
        for j in range(many):
            start = pl.multiple_of(at_ref[j] * depth, depth)
            moves = [
                (own_ref.at[:, pl.ds(start, depth)], a.at[pl.ds(0, rows), pl.ds(j * depth, depth)]),
                (sib_ref.at[:, pl.ds((first + j) * depth, depth)], a.at[pl.ds(rows, rows), pl.ds(j * depth, depth)]),
            ]
            for i in range(chunks):
                moves.append((block_refs[i * many + j], b.at[pl.ds(j * depth, depth), pl.ds(i * cols, cols)]))
            for source, target in moves:
                started.append(pltpu.make_async_copy(source, target, sems.at[len(started)]))
                started[-1].start()
        if held:
            started.append(pltpu.make_async_copy(refs[chunks * many], total, sems.at[len(started)]))
            started[-1].start()
        for copy in started:
            copy.wait()
        for i in range(chunks):
            part = slice(i * cols, (i + 1) * cols)
            term = jnp.dot(a[...], b[:, part], preferred_element_type=F32)
            total[:, part] = total[:, part] + term if held else term
        back_copy = pltpu.make_async_copy(total, out_ref, sems.at[len(started)])
        back_copy.start()
        back_copy.wait()

    wide = chunks * cols
    return call(
        kernel,
        at,
        [activations, sibling, *flat, *held],
        [jax.ShapeDtypeStruct((2 * rows, wide), F32)],
        [
            pltpu.VMEM((2 * rows, many * depth), BF16),
            pltpu.VMEM((many * depth, wide), BF16),
            pltpu.VMEM((2 * rows, wide), F32),
            pltpu.SemaphoreType.DMA((copies + 2,)),
        ],
        flops=4 * rows * depth * many * wide,
        moved=4 * rows * depth * many + 2 * depth * many * wide + 8 * rows * wide,
        name="project",
    )[0]


def outer_first(own, sibling, mine, theirs, width):
    rows, cols = own.shape[1], mine.shape[1]

    def kernel(own_ref, sib_ref, mine_ref, theirs_ref, held_ref, out_ref):
        held_ref[:rows, :] = (mine_ref[:rows, :] + theirs_ref[rows:, :]).astype(BF16)
        held_ref[rows:, :] = (mine_ref[rows:, :] + theirs_ref[:rows, :]).astype(BF16)
        term = jnp.dot(own_ref[...], held_ref[:rows, :], preferred_element_type=F32)
        term += jnp.dot(sib_ref[...], held_ref[rows:, :], preferred_element_type=F32)
        out_ref[...] = term.astype(BF16)

    whole = lambda *shape: pl.BlockSpec(shape, lambda j: (0, 0))
    return pl.pallas_call(
        kernel,
        grid=(1,),
        in_specs=[whole(width, rows), whole(width, rows), whole(2 * rows, cols), whole(2 * rows, cols)],
        out_specs=[whole(2 * rows, cols), whole(width, cols)],
        out_shape=[jax.ShapeDtypeStruct((2 * rows, cols), BF16), jax.ShapeDtypeStruct((width, cols), BF16)],
        compiler_params=params(),
        cost_estimate=cost(4 * rows * width * cols, 4 * rows * width + 20 * rows * cols),
        name="outer_first",
    )(own, sibling, mine, theirs)


def outer(own, sibling, held, width, start, many, dtype):
    rows, cols = own.shape[1], held.shape[1]

    def kernel(own_ref, sib_ref, held_ref, *out_refs):
        for j, out_ref in enumerate(out_refs):

            @pl.when(pl.program_id(0) == j)
            def _(out_ref=out_ref):
                term = jnp.dot(own_ref[...], held_ref[:rows, :], preferred_element_type=F32)
                term += jnp.dot(sib_ref[...], held_ref[rows:, :], preferred_element_type=F32)
                out_ref[...] = term.astype(dtype)

    return pl.pallas_call(
        kernel,
        grid=(many,),
        in_specs=[
            pl.BlockSpec((width, rows), lambda j: (start + j, 0)),
            pl.BlockSpec((width, rows), lambda j: (start + j, 0)),
            pl.BlockSpec((2 * rows, cols), lambda j: (0, 0)),
        ],
        out_specs=[pl.BlockSpec((width, cols), lambda j: (0, 0))] * many,
        out_shape=[jax.ShapeDtypeStruct((width, cols), dtype)] * many,
        compiler_params=params(),
        cost_estimate=cost(4 * rows * width * many * cols, many * (4 * rows * width + 4 * width * cols)),
        name="outer",
    )(own, sibling, held)


def back(blocks, projector_t, at, rows_in_all, before):
    many, chunks = len(blocks), len(blocks[0])
    (rows, cols), (rank, width) = blocks[0][0].shape, projector_t.shape
    flat = [part for block in blocks for part in block]
    held = [] if before is None else [before]
    slots = min(4, many)

    def kernel(at_ref, projector_ref, *refs):
        block_refs, out_ref = refs[: many * chunks], refs[many * chunks + len(held)]
        p, d, o, in_sems, out_sems = refs[many * chunks + len(held) + 1 :]
        p_copy = pltpu.make_async_copy(projector_ref, p, in_sems.at[many * chunks])
        p_copy.start()
        loads, stores = [], []
        for j in range(many):
            for i in range(chunks):
                n = j * chunks + i
                loads.append(pltpu.make_async_copy(block_refs[n], d.at[j, :, pl.ds(i * cols, cols)], in_sems.at[n]))
                loads[-1].start()
        p_copy.wait()
        for j in range(many):
            for i in range(chunks):
                loads[j * chunks + i].wait()
            if j >= slots:
                stores[j - slots].wait()
            o[j % slots] = jnp.dot(d[j], p[...], preferred_element_type=F32).astype(BF16)
            target = out_ref.at[pl.ds(pl.multiple_of(at_ref[j] * rows, rows), rows), :]
            stores.append(pltpu.make_async_copy(o.at[j % slots], target, out_sems.at[j % slots]))
            stores[-1].start()
        for j in range(many - slots, many):
            stores[j].wait()

    return call(
        kernel,
        at,
        [projector_t, *flat, *held],
        [jax.ShapeDtypeStruct((rows_in_all, width), BF16)],
        [
            pltpu.VMEM((rank, width), BF16),
            pltpu.VMEM((many, rows, rank), BF16),
            pltpu.VMEM((slots, rows, width), BF16),
            pltpu.SemaphoreType.DMA((many * chunks + 1,)),
            pltpu.SemaphoreType.DMA((slots,)),
        ],
        flops=2 * many * rows * width * rank,
        moved=2 * many * rows * (width + rank),
        name="back",
        aliases={2 + len(flat): 0} if held else None,
    )[0]


def levels(activations, out_grads, projector, first_moment, second_moment, *, nz):
    me = lax.axis_index("dp")
    z, y, core = me // 4, me // 2 % 2, me % 2
    grid = [(a, b, c) for a in range(nz) for b in range(2) for c in range(2)]

    def pairs(to):
        return [((a * 2 + b) * 2 + c, (to(a, b, c)[0] * 2 + to(a, b, c)[1]) * 2 + to(a, b, c)[2]) for a, b, c in grid]

    def swap_core(x):
        return lax.ppermute(x, "dp", pairs(lambda a, b, c: (a, b, 1 - c)))

    def swap_y(x):
        return lax.ppermute(x, "dp", pairs(lambda a, b, c: (a, 1 - b, c)))

    def shift_z(x, k):
        return lax.ppermute(x, "dp", pairs(lambda a, b, c: ((a + k) % nz, b, c)))

    def index(k, dy, dc):
        return (lax.rem(z + nz + k, nz) * 2 + (1 - y if dy else y)) * 2 + (1 - core if dc else core)

    def named(order):
        return jnp.stack([index(*o) for o in order]).astype(jnp.int32)

    def gather(chunks):
        line = [[own] for own in chunks]
        across = [[] for _ in chunks]
        for step in range(nz):
            for i in range(len(chunks)):
                if step:
                    line[i][step], across[i][step - 1] = lax.optimization_barrier((line[i][step], across[i][step - 1]))
                if step < nz - 1:
                    line[i].append(shift_z(line[i][step], 1))
                if step < nz - 1 or i < len(chunks) - 1:
                    across[i].append(swap_y(line[i][step]))
                else:
                    across[i].append(shift_z(across[i][0], nz - 1))
        return [{(-k, dy): (line, across)[dy][i][k] for k in range(nz) for dy in (0, 1)} for i in range(len(chunks))]

    ks = sorted(range(1, nz), key=lambda k: -min(k, nz - k))
    depth, rank = projector.shape
    width = first_moment.shape[0]
    cols = rank // CHUNKS
    parts = [slice(i * cols, (i + 1) * cols) for i in range(CHUNKS)]

    late = [(2 - nz, 1), (1 - nz, 0), (1 - nz, 1)]
    early = [(-k, dy) for k in range(nz) for dy in (0, 1) if (-k, dy) not in late]
    order_out = [(k, dy) for dy in (1, 0) for k in ks + [0]]

    gathered = gather([projector[:, part] for part in parts])
    a_sibling = swap_core(pick(activations, named([(k, dy, 1) for k, dy in early + late]), depth, False))
    g_sibling = swap_core(pick(out_grads, named([(k, dy, 1) for k, dy in order_out]), width, True))
    g_own = pick(out_grads, named([(k, dy, 0) for k, dy in order_out]), width, True)
    projector_t = projector.T

    mine, first = None, 0
    for order in (early, late):
        at = named([(k, dy, 0) for k, dy in order])
        mine = project(activations, a_sibling, first, at, [[chunk[o] for o in order] for chunk in gathered], mine)
        first += len(order)

    held, send = outer_first(g_own, g_sibling, mine, swap_core(mine), width)
    sends = [send] + list(outer(g_own, g_sibling, held, width, 1, nz - 1, BF16))
    keeps = list(outer(g_own, g_sibling, held, width, nz, nz, F32))
    reduced = None
    for at, k in enumerate(ks + [0]):
        term = keeps[at] + swap_y(sends[at]).astype(F32)
        if k:
            term = shift_z(term.astype(BF16), k).astype(F32)
        reduced = term if reduced is None else reduced + term
    new_first, new_second, direction = adam(reduced, first_moment, second_moment)

    gathered = gather([direction[:, part] for part in parts])
    update = None
    for order in (early, late):
        blocks = [[chunk[o] for chunk in gathered] for o in order]
        blocks = blocks + [[swap_core(x) for x in block] for block in blocks]
        at = named([(k, dy, dc) for dc in (0, 1) for k, dy in order])
        update = back(blocks, projector_t, at, 4 * nz * width, update)
    return update, new_first, new_second


def solution(mesh):
    devices = mesh.shape["dp"]

    def body(activations, out_grads, projector, first_moment, second_moment):
        aligned = projector.shape[0] % 128 == 0 and first_moment.shape[0] % 128 == 0
        if devices % 4 or devices < 8 or not aligned:
            return plain(activations, out_grads, projector, first_moment, second_moment)
        return levels(activations, out_grads, projector, first_moment, second_moment, nz=devices // 4)

    placed = P(("groups", "dp"), None)
    return jax.shard_map(
        body,
        mesh=mesh,
        in_specs=(placed,) * 5,
        out_specs=(P("groups", "dp"), placed, placed),
        check_vma=False,
    )
```

```python
import functools
import jax
import jax.numpy as jnp
from jax import lax
from jax.experimental import pallas as pl
from jax.experimental.pallas import tpu as pltpu
from jax.sharding import PartitionSpec as P

STEP = 100

decay_first = 0.9
decay_second = 0.999
epsilon = 1e-08

CHUNKS = 2
F32, BF16 = jnp.float32, jnp.bfloat16
VMEM_LIMIT = 16 * 1024 * 1024


def adam(reduced, first_moment, second_moment):
    new_first = decay_first * first_moment + (1.0 - decay_first) * reduced
    new_second = decay_second * second_moment + (1.0 - decay_second) * reduced * reduced
    first_fix = 1.0 - decay_first**STEP
    second_fix = 1.0 - decay_second**STEP
    direction = (new_first / first_fix / (jnp.sqrt(new_second / second_fix) + epsilon)).astype(BF16)
    return new_first, new_second, direction


def plain(activations, out_grads, projector, first_moment, second_moment):
    projected = jnp.dot(
        activations,
        lax.all_gather(projector, "dp", axis=0, tiled=True),
        preferred_element_type=F32,
    ).astype(BF16)
    reduced = lax.psum_scatter(
        lax.dot_general(out_grads, projected, (((0,), (0,)), ((), ())), preferred_element_type=F32),
        "dp",
        scatter_dimension=0,
        tiled=True,
    )
    new_first, new_second, direction = adam(reduced, first_moment, second_moment)
    update = lax.dot_general(
        lax.all_gather(direction, "dp", axis=0, tiled=True),
        projector,
        (((1,), (1,)), ((), ())),
        preferred_element_type=F32,
    ).astype(BF16)
    return update, new_first, new_second


def params():
    return pltpu.CompilerParams(vmem_limit_bytes=VMEM_LIMIT)


def cost(flops, moved):
    return pl.CostEstimate(flops=flops, bytes_accessed=moved, transcendentals=0)


def take(array, at, width):
    rows, many = array.shape[0], at.shape[0]

    def kernel(at_ref, in_ref, out_ref, sems):
        copies = []
        for j in range(many):
            source = in_ref.at[:, pl.ds(pl.multiple_of(at_ref[j] * width, width), width)]
            copies.append(pltpu.make_async_copy(source, out_ref.at[:, pl.ds(j * width, width)], sems.at[j]))
            copies[-1].start()
        for copy in copies:
            copy.wait()

    return call(
        kernel,
        at,
        [array],
        [jax.ShapeDtypeStruct((rows, many * width), array.dtype)],
        [pltpu.SemaphoreType.DMA((many,))],
        flops=0,
        moved=4 * rows * many * width,
        name="take",
        in_hbm=1,
    )[0]


def turn(array, at, width):
    rows, many = array.shape[0], at.shape[0]
    half = many // 2

    def kernel(at_ref, in_ref, first_ref, second_ref, held, sem):
        copy = pltpu.make_async_copy(in_ref, held, sem)
        copy.start()
        copy.wait()
        for j in range(many):
            block = held[:, pl.ds(pl.multiple_of(at_ref[j] * width, width), width)]
            out_ref, i = (first_ref, j) if j < half else (second_ref, j - half)
            out_ref[i * width : (i + 1) * width, :] = block.T

    return pl.pallas_call(
        kernel,
        grid_spec=pltpu.PrefetchScalarGridSpec(
            num_scalar_prefetch=1,
            grid=(1,),
            in_specs=[pl.BlockSpec(memory_space=pltpu.HBM)],
            out_specs=[pl.BlockSpec((half * width, rows), lambda j, at_ref: (0, 0))] * 2,
            scratch_shapes=[pltpu.VMEM(array.shape, array.dtype), pltpu.SemaphoreType.DMA],
        ),
        out_shape=[jax.ShapeDtypeStruct((half * width, rows), array.dtype)] * 2,
        compiler_params=params(),
        cost_estimate=cost(0, 4 * rows * many * width),
        name="turn",
    )(at, array)


def call(kernel, scalars, arrays, outs, scratch, *, flops, moved, name, aliases=None, in_hbm=0):
    anywhere = pl.BlockSpec(memory_space=pl.ANY)
    return pl.pallas_call(
        kernel,
        grid_spec=pltpu.PrefetchScalarGridSpec(
            num_scalar_prefetch=1,
            grid=(),
            in_specs=[pl.BlockSpec(memory_space=pltpu.HBM)] * in_hbm + [anywhere] * (len(arrays) - in_hbm),
            out_specs=[anywhere] * len(outs),
            scratch_shapes=scratch,
        ),
        out_shape=outs,
        input_output_aliases=aliases or {},
        compiler_params=params(),
        cost_estimate=cost(flops, moved),
        name=name,
    )(scalars, *arrays)


def project(activations, sibling, slots, at, blocks, before):
    chunks, many = len(blocks), len(blocks[0])
    (depth, cols), rows = blocks[0][0].shape, activations.shape[0]
    copies = many * (2 + chunks)
    flat = [block for chunk in blocks for block in chunk]
    held = before or []

    def kernel(at_ref, own_ref, *refs):
        sib_refs, refs = refs[: len(sibling)], refs[len(sibling) :]
        block_refs, out_ref = refs[: chunks * many], refs[chunks * many + len(held)]
        a, b, total, sems = refs[chunks * many + len(held) + 1 :]
        started = []
        for j in range(many):
            start = pl.multiple_of(at_ref[j] * depth, depth)
            moves = [
                (own_ref.at[:, pl.ds(start, depth)], a.at[pl.ds(0, rows), pl.ds(j * depth, depth)]),
                (sib_refs[slots[j][0]].at[:, pl.ds(slots[j][1] * depth, depth)], a.at[pl.ds(rows, rows), pl.ds(j * depth, depth)]),
            ]
            for i in range(chunks):
                moves.append((block_refs[i * many + j], b.at[pl.ds(j * depth, depth), pl.ds(i * cols, cols)]))
            for source, target in moves:
                started.append(pltpu.make_async_copy(source, target, sems.at[len(started)]))
                started[-1].start()
        for i in range(len(held)):
            target = total.at[:, pl.ds(i * cols, cols)]
            started.append(pltpu.make_async_copy(refs[chunks * many + i], target, sems.at[len(started)]))
            started[-1].start()
        for copy in started:
            copy.wait()
        for i in range(chunks):
            part = slice(i * cols, (i + 1) * cols)
            term = jnp.dot(a[...], b[:, part], preferred_element_type=F32)
            total[:, part] = total[:, part] + term if held else term
        back_copy = pltpu.make_async_copy(total, out_ref, sems.at[len(started)])
        back_copy.start()
        back_copy.wait()

    wide = chunks * cols
    return call(
        kernel,
        at,
        [activations, *sibling, *flat, *held],
        [jax.ShapeDtypeStruct((2 * rows, wide), F32)],
        [
            pltpu.VMEM((2 * rows, many * depth), BF16),
            pltpu.VMEM((many * depth, wide), BF16),
            pltpu.VMEM((2 * rows, wide), F32),
            pltpu.SemaphoreType.DMA((copies + len(held) + 1,)),
        ],
        flops=4 * rows * depth * many * wide,
        moved=4 * rows * depth * many + 2 * depth * many * wide + 8 * rows * wide,
        name="project",
        in_hbm=1,
    )[0]


def outer_first(own, sibling, mine, theirs, width):
    rows, cols = own.shape[1], mine.shape[1]

    def kernel(own_ref, sib_ref, mine_ref, theirs_ref, held_ref, out_ref):
        held_ref[:rows, :] = (mine_ref[:rows, :] + theirs_ref[rows:, :]).astype(BF16)
        held_ref[rows:, :] = (mine_ref[rows:, :] + theirs_ref[:rows, :]).astype(BF16)
        term = jnp.dot(own_ref[...], held_ref[:rows, :], preferred_element_type=F32)
        term += jnp.dot(sib_ref[...], held_ref[rows:, :], preferred_element_type=F32)
        out_ref[...] = term.astype(BF16)

    whole = lambda *shape: pl.BlockSpec(shape, lambda j: (0, 0))
    return pl.pallas_call(
        kernel,
        grid=(1,),
        in_specs=[whole(width, rows), whole(width, rows), whole(2 * rows, cols), whole(2 * rows, cols)],
        out_specs=[whole(2 * rows, cols), whole(width, cols)],
        out_shape=[jax.ShapeDtypeStruct((2 * rows, cols), BF16), jax.ShapeDtypeStruct((width, cols), BF16)],
        compiler_params=params(),
        cost_estimate=cost(4 * rows * width * cols, 4 * rows * width + 20 * rows * cols),
        name="outer_first",
    )(own, sibling, mine, theirs)


def outer(own, sibling, held, width, start, many, dtype):
    rows, cols = own.shape[1], held.shape[1]

    def kernel(own_ref, sib_ref, held_ref, *out_refs):
        for j, out_ref in enumerate(out_refs):

            @pl.when(pl.program_id(0) == j)
            def _(out_ref=out_ref):
                term = jnp.dot(own_ref[...], held_ref[:rows, :], preferred_element_type=F32)
                term += jnp.dot(sib_ref[...], held_ref[rows:, :], preferred_element_type=F32)
                out_ref[...] = term.astype(dtype)

    return pl.pallas_call(
        kernel,
        grid=(many,),
        in_specs=[
            pl.BlockSpec((width, rows), lambda j: (start + j, 0)),
            pl.BlockSpec((width, rows), lambda j: (start + j, 0)),
            pl.BlockSpec((2 * rows, cols), lambda j: (0, 0)),
        ],
        out_specs=[pl.BlockSpec((width, cols), lambda j: (0, 0))] * many,
        out_shape=[jax.ShapeDtypeStruct((width, cols), dtype)] * many,
        compiler_params=params(),
        cost_estimate=cost(4 * rows * width * many * cols, many * (4 * rows * width + 4 * width * cols)),
        name="outer",
    )(own, sibling, held)


def back(arrays, blocks, projector_t, at, rows, cols, rows_in_all, before):
    many, chunks = len(blocks), len(blocks[0])
    rank, width = projector_t.shape
    held = [] if before is None else [before]
    slots = min(4, many)

    def kernel(at_ref, projector_ref, *refs):
        array_refs, out_ref = refs[: len(arrays)], refs[len(arrays) + len(held)]
        p, d, o, in_sems, out_sems = refs[len(arrays) + len(held) + 1 :]
        p_copy = pltpu.make_async_copy(projector_ref, p, in_sems.at[many * chunks])
        p_copy.start()
        loads, stores = [], []
        for j in range(many):
            for i in range(chunks):
                n = j * chunks + i
                which, start = blocks[j][i]
                source = array_refs[which].at[pl.ds(start, rows), :]
                loads.append(pltpu.make_async_copy(source, d.at[j, :, pl.ds(i * cols, cols)], in_sems.at[n]))
                loads[-1].start()
        p_copy.wait()
        for j in range(many):
            for i in range(chunks):
                loads[j * chunks + i].wait()
            if j >= slots:
                stores[j - slots].wait()
            o[j % slots] = jnp.dot(d[j], p[...], preferred_element_type=F32).astype(BF16)
            target = out_ref.at[pl.ds(pl.multiple_of(at_ref[j] * rows, rows), rows), :]
            stores.append(pltpu.make_async_copy(o.at[j % slots], target, out_sems.at[j % slots]))
            stores[-1].start()
        for j in range(many - slots, many):
            stores[j].wait()

    return call(
        kernel,
        at,
        [projector_t, *arrays, *held],
        [jax.ShapeDtypeStruct((rows_in_all, width), BF16)],
        [
            pltpu.VMEM((rank, width), BF16),
            pltpu.VMEM((many, rows, rank), BF16),
            pltpu.VMEM((slots, rows, width), BF16),
            pltpu.SemaphoreType.DMA((many * chunks + 1,)),
            pltpu.SemaphoreType.DMA((slots,)),
        ],
        flops=2 * many * rows * width * rank,
        moved=2 * many * rows * (width + rank),
        name="back",
        aliases={2 + len(arrays): 0} if held else None,
    )[0]


def levels(activations, out_grads, projector, first_moment, second_moment, *, nz):
    me = lax.axis_index("dp")
    z, y, core = me // 4, me // 2 % 2, me % 2
    grid = [(a, b, c) for a in range(nz) for b in range(2) for c in range(2)]

    def pairs(to):
        return [((a * 2 + b) * 2 + c, (to(a, b, c)[0] * 2 + to(a, b, c)[1]) * 2 + to(a, b, c)[2]) for a, b, c in grid]

    def swap_core(x):
        return lax.ppermute(x, "dp", pairs(lambda a, b, c: (a, b, 1 - c)))

    def swap_y(x):
        return lax.ppermute(x, "dp", pairs(lambda a, b, c: (a, 1 - b, c)))

    def shift_z(x, k):
        return lax.ppermute(x, "dp", pairs(lambda a, b, c: ((a + k) % nz, b, c)))

    def index(k, dy, dc):
        return (lax.rem(z + nz + k, nz) * 2 + (1 - y if dy else y)) * 2 + (1 - core if dc else core)

    def named(order):
        return jnp.stack([index(*o) for o in order]).astype(jnp.int32)

    def gather(chunks, beside):
        line = [[own] for own in chunks]
        across = [[] for _ in chunks]
        for step in range(nz):
            for i in range(len(chunks)):
                if step:
                    ready = beside(step, i, line, across)
                    line[i][step], across[i][step - 1], *_ = lax.optimization_barrier((line[i][step], across[i][step - 1], *ready))
                if step < nz - 1:
                    line[i].append(shift_z(line[i][step], 1))
                if step < nz - 1 or i < len(chunks) - 1:
                    across[i].append(swap_y(line[i][step]))
                else:
                    across[i].append(shift_z(across[i][0], nz - 1))
        return line, across

    after = lambda x, *those: lax.optimization_barrier((x, *those))[0]
    ks = sorted(range(1, nz), key=lambda k: -min(k, nz - k))
    depth, rank = projector.shape
    width = first_moment.shape[0]
    cols = rank // CHUNKS
    parts = [slice(i * cols, (i + 1) * cols) for i in range(CHUNKS)]

    order_in = [(-k, dy) for k in range(nz) for dy in (0, 1)]
    order_out = [(k, dy) for dy in (1, 0) for k in ks + [0]]
    last, half = len(order_in) - 1, len(order_in) // 2
    at_in = named([(k, dy, 0) for k, dy in order_in])
    at_sibling = named([(k, dy, 1) for k, dy in order_in])
    at_out = named([(k, dy, dc) for dc in (0, 1) for k, dy in order_out])
    slots = [(j // half, j % half) for j in range(len(order_in))]
    made = {}

    def beside_projector(step, i, line, across):
        if (step, i) == (1, 1):
            made["a0"] = take(activations, after(at_sibling[:half], line[0][1]), depth)
            return [made["a0"]]
        if (step, i) == (2, 0):
            made["a1"] = take(activations, after(at_sibling[half:], line[1][1]), depth)
            return [made["a1"]]
        if (step, i) == (2, 1):
            made["own"], other = turn(out_grads, after(at_out, line[0][2]), width)
            made["other"] = other
            return [made["own"], other]
        if (step, i) == (nz - 1, 0):
            made["pt"] = after(projector, line[1][2]).T
            made["a"] = [swap_core(made["a0"]), swap_core(made["a1"])]
            return [made["pt"]]
        if (step, i) == (nz - 1, 1):
            ready = [line[0][n // 2] if n % 2 == 0 else across[0][n // 2] for n in range(last)]
            made["p0"] = project(activations, made["a"], slots[:last], at_in[:last], [ready], None)
            return [made["p0"]]
        return []

    line, across = gather([projector[:, part] for part in parts], beside_projector)
    g_own, g_sibling = made["own"], swap_core(made["other"])
    ready = [line[1][n // 2] if n % 2 == 0 else across[1][n // 2] for n in range(last)]
    made["p1"] = project(activations, made["a"], slots[:last], at_in[:last], [ready], None)
    mine = project(
        activations, made["a"], slots[last:], at_in[last:], [[across[0][-1]], [across[1][-1]]], [made["p0"], made["p1"]]
    )

    held, send = outer_first(g_own, g_sibling, mine, swap_core(mine), width)
    sends = [send] + list(outer(g_own, g_sibling, held, width, 1, nz - 1, BF16))
    keeps = list(outer(g_own, g_sibling, held, width, nz, nz, F32))
    reduced = None
    for at, k in enumerate(ks + [0]):
        term = keeps[at] + swap_y(sends[at]).astype(F32)
        if k:
            term = shift_z(term.astype(BF16), k).astype(F32)
        reduced = term if reduced is None else reduced + term
    new_first, new_second, direction = adam(reduced, first_moment, second_moment)

    def beside_direction(step, i, line, across):
        if step == nz // 2 or step == nz - 1:
            low = 0 if step == nz // 2 else half
            high = half if step == nz // 2 else last
            group = [line[i][n // 2] if n % 2 == 0 else across[i][n // 2] for n in range(low, high)]
            made["group", low, i] = jnp.concatenate(group, axis=0)
            made["swapped", low, i] = swap_core(made["group", low, i])
        return []

    line, across = gather([direction[:, part] for part in parts], beside_direction)
    update = None
    for low, high in ((0, half), (half, last + 1)):
        arrays, blocks = [], []
        for name in ("group", "swapped"):
            base = len(arrays)
            arrays += [made[name, low, i] for i in range(CHUNKS)]
            blocks += [[(base + i, (n - low) * width) for i in range(CHUNKS)] for n in range(low, min(high, last))]
            if high > last:
                ends = [across[i][-1] for i in range(CHUNKS)]
                arrays += [swap_core(x) for x in ends] if name == "swapped" else ends
                blocks += [[(base + CHUNKS + i, 0) for i in range(CHUNKS)]]
        at = named([(k, dy, dc) for dc in (0, 1) for k, dy in order_in[low:high]])
        update = back(arrays, blocks, made["pt"], at, width, cols, 4 * nz * width, update)
    return update, new_first, new_second


def solution(mesh):
    devices = mesh.shape["dp"]

    def body(activations, out_grads, projector, first_moment, second_moment):
        aligned = projector.shape[0] % 128 == 0 and first_moment.shape[0] % 128 == 0
        if devices % 4 or devices < 16 or not aligned:
            return plain(activations, out_grads, projector, first_moment, second_moment)
        return levels(activations, out_grads, projector, first_moment, second_moment, nz=devices // 4)

    placed = P(("groups", "dp"), None)
    return jax.shard_map(
        body,
        mesh=mesh,
        in_specs=(placed,) * 5,
        out_specs=(P("groups", "dp"), placed, placed),
        check_vma=False,
    )
```

```python
import functools
import jax
import jax.numpy as jnp
from jax import lax
from jax.experimental import pallas as pl
from jax.experimental.pallas import tpu as pltpu
from jax.sharding import PartitionSpec as P

STEP = 100

decay_first = 0.9
decay_second = 0.999
epsilon = 1e-08

CHUNKS = 2
F32, BF16 = jnp.float32, jnp.bfloat16
VMEM_LIMIT = 16 * 1024 * 1024


def adam(reduced, first_moment, second_moment):
    new_first = decay_first * first_moment + (1.0 - decay_first) * reduced
    new_second = decay_second * second_moment + (1.0 - decay_second) * reduced * reduced
    first_fix = 1.0 - decay_first**STEP
    second_fix = 1.0 - decay_second**STEP
    direction = (new_first / first_fix / (jnp.sqrt(new_second / second_fix) + epsilon)).astype(BF16)
    return new_first, new_second, direction


def plain(activations, out_grads, projector, first_moment, second_moment):
    projected = jnp.dot(
        activations,
        lax.all_gather(projector, "dp", axis=0, tiled=True),
        preferred_element_type=F32,
    ).astype(BF16)
    reduced = lax.psum_scatter(
        lax.dot_general(out_grads, projected, (((0,), (0,)), ((), ())), preferred_element_type=F32),
        "dp",
        scatter_dimension=0,
        tiled=True,
    )
    new_first, new_second, direction = adam(reduced, first_moment, second_moment)
    update = lax.dot_general(
        lax.all_gather(direction, "dp", axis=0, tiled=True),
        projector,
        (((1,), (1,)), ((), ())),
        preferred_element_type=F32,
    ).astype(BF16)
    return update, new_first, new_second


def params():
    return pltpu.CompilerParams(vmem_limit_bytes=VMEM_LIMIT)


def cost(flops, moved):
    return pl.CostEstimate(flops=flops, bytes_accessed=moved, transcendentals=0)


def take(array, at, width):
    rows, many = array.shape[0], at.shape[0]

    def kernel(at_ref, in_ref, out_ref, sems):
        copies = []
        for j in range(many):
            source = in_ref.at[:, pl.ds(pl.multiple_of(at_ref[j] * width, width), width)]
            copies.append(pltpu.make_async_copy(source, out_ref.at[:, pl.ds(j * width, width)], sems.at[j]))
            copies[-1].start()
        for copy in copies:
            copy.wait()

    return call(
        kernel,
        at,
        [array],
        [jax.ShapeDtypeStruct((rows, many * width), array.dtype)],
        [pltpu.SemaphoreType.DMA((many,))],
        flops=0,
        moved=4 * rows * many * width,
        name="take",
        in_hbm=1,
    )[0]


def turn(array, at, width):
    rows, many = array.shape[0], at.shape[0]
    half = many // 2

    def kernel(at_ref, in_ref, first_ref, second_ref, held, sem):
        copy = pltpu.make_async_copy(in_ref, held, sem)
        copy.start()
        copy.wait()
        for j in range(many):
            block = held[:, pl.ds(pl.multiple_of(at_ref[j] * width, width), width)]
            out_ref, i = (first_ref, j) if j < half else (second_ref, j - half)
            out_ref[i * width : (i + 1) * width, :] = block.T

    return pl.pallas_call(
        kernel,
        grid_spec=pltpu.PrefetchScalarGridSpec(
            num_scalar_prefetch=1,
            grid=(1,),
            in_specs=[pl.BlockSpec(memory_space=pl.ANY)],
            out_specs=[pl.BlockSpec((half * width, rows), lambda j, at_ref: (0, 0))] * 2,
            scratch_shapes=[pltpu.VMEM(array.shape, array.dtype), pltpu.SemaphoreType.DMA],
        ),
        out_shape=[jax.ShapeDtypeStruct((half * width, rows), array.dtype)] * 2,
        compiler_params=params(),
        cost_estimate=cost(0, 4 * rows * many * width),
        name="turn",
    )(at, pinned(array))


def pinned(x):
    return pltpu.with_memory_space_constraint(x, pltpu.HBM)


def call(kernel, scalars, arrays, outs, scratch, *, flops, moved, name, aliases=None, in_hbm=0):
    anywhere = pl.BlockSpec(memory_space=pl.ANY)
    return pl.pallas_call(
        kernel,
        grid_spec=pltpu.PrefetchScalarGridSpec(
            num_scalar_prefetch=1,
            grid=(),
            in_specs=[anywhere] * len(arrays),
            out_specs=[anywhere] * len(outs),
            scratch_shapes=scratch,
        ),
        out_shape=outs,
        input_output_aliases=aliases or {},
        compiler_params=params(),
        cost_estimate=cost(flops, moved),
        name=name,
    )(scalars, *[pinned(x) for x in arrays[:in_hbm]], *arrays[in_hbm:])


def project(activations, sibling, slots, at, blocks, before):
    chunks, many = len(blocks), len(blocks[0])
    (depth, cols), rows = blocks[0][0].shape, activations.shape[0]
    copies = many * (2 + chunks)
    flat = [block for chunk in blocks for block in chunk]
    held = [] if before is None else [before]

    def kernel(at_ref, own_ref, *refs):
        sib_refs, refs = refs[: len(sibling)], refs[len(sibling) :]
        block_refs, out_ref = refs[: chunks * many], refs[chunks * many + len(held)]
        a, b, total, sems = refs[chunks * many + len(held) + 1 :]
        started = []
        for j in range(many):
            start = pl.multiple_of(at_ref[j] * depth, depth)
            moves = [
                (own_ref.at[:, pl.ds(start, depth)], a.at[pl.ds(0, rows), pl.ds(j * depth, depth)]),
                (sib_refs[slots[j][0]].at[:, pl.ds(slots[j][1] * depth, depth)], a.at[pl.ds(rows, rows), pl.ds(j * depth, depth)]),
            ]
            for i in range(chunks):
                moves.append((block_refs[i * many + j], b.at[pl.ds(j * depth, depth), pl.ds(i * cols, cols)]))
            for source, target in moves:
                started.append(pltpu.make_async_copy(source, target, sems.at[len(started)]))
                started[-1].start()
        if held:
            started.append(pltpu.make_async_copy(refs[chunks * many], total, sems.at[len(started)]))
            started[-1].start()
        for copy in started:
            copy.wait()
        for i in range(chunks):
            part = slice(i * cols, (i + 1) * cols)
            term = jnp.dot(a[...], b[:, part], preferred_element_type=F32)
            total[:, part] = total[:, part] + term if held else term
        back_copy = pltpu.make_async_copy(total, out_ref, sems.at[len(started)])
        back_copy.start()
        back_copy.wait()

    wide = chunks * cols
    return call(
        kernel,
        at,
        [activations, *sibling, *flat, *held],
        [jax.ShapeDtypeStruct((2 * rows, wide), F32)],
        [
            pltpu.VMEM((2 * rows, many * depth), BF16),
            pltpu.VMEM((many * depth, wide), BF16),
            pltpu.VMEM((2 * rows, wide), F32),
            pltpu.SemaphoreType.DMA((copies + len(held) + 1,)),
        ],
        flops=4 * rows * depth * many * wide,
        moved=4 * rows * depth * many + 2 * depth * many * wide + 8 * rows * wide,
        name="project",
        in_hbm=1,
    )[0]


def outer_first(own, sibling, mine, theirs, width):
    rows, cols = own.shape[1], mine.shape[1]

    def kernel(own_ref, sib_ref, mine_ref, theirs_ref, held_ref, out_ref):
        held_ref[:rows, :] = (mine_ref[:rows, :] + theirs_ref[rows:, :]).astype(BF16)
        held_ref[rows:, :] = (mine_ref[rows:, :] + theirs_ref[:rows, :]).astype(BF16)
        term = jnp.dot(own_ref[...], held_ref[:rows, :], preferred_element_type=F32)
        term += jnp.dot(sib_ref[...], held_ref[rows:, :], preferred_element_type=F32)
        out_ref[...] = term.astype(BF16)

    whole = lambda *shape: pl.BlockSpec(shape, lambda j: (0, 0))
    return pl.pallas_call(
        kernel,
        grid=(1,),
        in_specs=[whole(width, rows), whole(width, rows), whole(2 * rows, cols), whole(2 * rows, cols)],
        out_specs=[whole(2 * rows, cols), whole(width, cols)],
        out_shape=[jax.ShapeDtypeStruct((2 * rows, cols), BF16), jax.ShapeDtypeStruct((width, cols), BF16)],
        compiler_params=params(),
        cost_estimate=cost(4 * rows * width * cols, 4 * rows * width + 20 * rows * cols),
        name="outer_first",
    )(own, sibling, mine, theirs)


def outer(own, sibling, held, width, start, many, dtype):
    rows, cols = own.shape[1], held.shape[1]

    def kernel(own_ref, sib_ref, held_ref, *out_refs):
        for j, out_ref in enumerate(out_refs):

            @pl.when(pl.program_id(0) == j)
            def _(out_ref=out_ref):
                term = jnp.dot(own_ref[...], held_ref[:rows, :], preferred_element_type=F32)
                term += jnp.dot(sib_ref[...], held_ref[rows:, :], preferred_element_type=F32)
                out_ref[...] = term.astype(dtype)

    return pl.pallas_call(
        kernel,
        grid=(many,),
        in_specs=[
            pl.BlockSpec((width, rows), lambda j: (start + j, 0)),
            pl.BlockSpec((width, rows), lambda j: (start + j, 0)),
            pl.BlockSpec((2 * rows, cols), lambda j: (0, 0)),
        ],
        out_specs=[pl.BlockSpec((width, cols), lambda j: (0, 0))] * many,
        out_shape=[jax.ShapeDtypeStruct((width, cols), dtype)] * many,
        compiler_params=params(),
        cost_estimate=cost(4 * rows * width * many * cols, many * (4 * rows * width + 4 * width * cols)),
        name="outer",
    )(own, sibling, held)


def back(groups, projector_t, at, rows, rows_in_all, before):
    many, chunks, cols = at.shape[0], len(groups[0]), groups[0][0].shape[1]
    rank, width = projector_t.shape
    arrays = [x for group in groups for x in group]
    held = [] if before is None else [before]
    slots = min(4, many)

    def kernel(at_ref, projector_ref, *refs):
        array_refs, out_ref = refs[: len(arrays)], refs[len(arrays) + len(held)]
        p, d, o, in_sems, out_sems = refs[len(arrays) + len(held) + 1 :]
        loads, stores, waits = [pltpu.make_async_copy(projector_ref, p, in_sems.at[len(arrays)])], [], {}
        start = 0
        for g, group in enumerate(groups):
            size = group[0].shape[0]
            for i in range(chunks):
                target = d.at[pl.ds(start, size), pl.ds(i * cols, cols)]
                loads.append(pltpu.make_async_copy(array_refs[g * chunks + i], target, in_sems.at[g * chunks + i]))
            waits[start // rows] = loads[-chunks:]
            start += size
        for copy in loads:
            copy.start()
        loads[0].wait()
        for j in range(many):
            for copy in waits.get(j, []):
                copy.wait()
            if j >= slots:
                stores[j - slots].wait()
            block = d[j * rows : (j + 1) * rows, :]
            o[j % slots] = jnp.dot(block, p[...], preferred_element_type=F32).astype(BF16)
            target = out_ref.at[pl.ds(pl.multiple_of(at_ref[j] * rows, rows), rows), :]
            stores.append(pltpu.make_async_copy(o.at[j % slots], target, out_sems.at[j % slots]))
            stores[-1].start()
        for j in range(many - slots, many):
            stores[j].wait()

    return call(
        kernel,
        at,
        [projector_t, *arrays, *held],
        [jax.ShapeDtypeStruct((rows_in_all, width), BF16)],
        [
            pltpu.VMEM((rank, width), BF16),
            pltpu.VMEM((many * rows, rank), BF16),
            pltpu.VMEM((slots, rows, width), BF16),
            pltpu.SemaphoreType.DMA((len(arrays) + 1,)),
            pltpu.SemaphoreType.DMA((slots,)),
        ],
        flops=2 * many * rows * width * rank,
        moved=2 * many * rows * (width + rank),
        name="back",
        aliases={2 + len(arrays): 0} if held else None,
    )[0]


def levels(activations, out_grads, projector, first_moment, second_moment, *, nz):
    me = lax.axis_index("dp")
    z, y, core = me // 4, me // 2 % 2, me % 2
    grid = [(a, b, c) for a in range(nz) for b in range(2) for c in range(2)]

    def pairs(to):
        return [((a * 2 + b) * 2 + c, (to(a, b, c)[0] * 2 + to(a, b, c)[1]) * 2 + to(a, b, c)[2]) for a, b, c in grid]

    def swap_core(x):
        return lax.ppermute(x, "dp", pairs(lambda a, b, c: (a, b, 1 - c)))

    def swap_y(x):
        return lax.ppermute(x, "dp", pairs(lambda a, b, c: (a, 1 - b, c)))

    def shift_z(x, k):
        return lax.ppermute(x, "dp", pairs(lambda a, b, c: ((a + k) % nz, b, c)))

    def index(k, dy, dc):
        return (lax.rem(z + nz + k, nz) * 2 + (1 - y if dy else y)) * 2 + (1 - core if dc else core)

    def named(order):
        return jnp.stack([index(*o) for o in order]).astype(jnp.int32)

    def gather(chunks, beside):
        line = [[own] for own in chunks]
        across = [[] for _ in chunks]
        for step in range(nz):
            for i in range(len(chunks)):
                if step:
                    ready = beside(step, i, line, across)
                    line[i][step], across[i][step - 1], *_ = lax.optimization_barrier((line[i][step], across[i][step - 1], *ready))
                if step < nz - 1:
                    line[i].append(shift_z(line[i][step], 1))
                if step < nz - 1 or i < len(chunks) - 1:
                    across[i].append(swap_y(line[i][step]))
                else:
                    across[i].append(shift_z(across[i][0], nz - 1))
        return line, across

    after = lambda x, *those: lax.optimization_barrier((x, *those))[0]
    ks = list(range(nz - 2, 0, -1)) + [nz - 1]
    depth, rank = projector.shape
    width = first_moment.shape[0]
    cols = rank // CHUNKS
    parts = [slice(i * cols, (i + 1) * cols) for i in range(CHUNKS)]

    order_in = [(-k, dy) for k in range(nz) for dy in (0, 1)]
    order_out = [(k, dy) for dy in (1, 0) for k in ks + [0]]
    last, half = len(order_in) - 1, len(order_in) // 2
    at_in = named([(k, dy, 0) for k, dy in order_in])
    at_sibling = named([(k, dy, 1) for k, dy in order_in])
    at_out = named([(k, dy, dc) for dc in (0, 1) for k, dy in order_out])
    slots = [(j // half, j % half) for j in range(len(order_in))]
    made = {}

    def ready(line, across, i, low, high):
        return [(across if n % 2 else line)[i][n // 2] for n in range(low, high)]

    def beside_projector(step, i, line, across):
        if (step, i) == (1, 1):
            made["a0"] = take(activations, after(at_sibling[:half], line[1][1]), depth)
            return [made["a0"]]
        if (step, i) == (2, 0):
            made["a1"] = take(activations, after(at_sibling[half:], line[0][2]), depth)
            made["a"] = [swap_core(made["a0"]), swap_core(made["a1"])]
            return [made["a1"]]
        if (step, i) == (2, 1):
            made["own"], made["other"] = turn(out_grads, after(at_out, line[1][2]), width)
            return [made["own"], made["other"]]
        if (step, i) == (nz - 1, 0):
            blocks = [ready(line, across, n, 0, soon) for n in range(CHUNKS)]
            made["early"] = project(activations, made["a"], slots[:soon], after(at_in[:soon], line[0][nz - 1]), blocks, None)
            return [made["early"]]
        return []

    soon = last - 2
    line, across = gather([projector[:, part] for part in parts], beside_projector)
    g_own, g_sibling = made["own"], swap_core(made["other"])
    middle = [ready(line, across, i, soon, last) for i in range(CHUNKS)]
    middle = project(activations, made["a"], slots[soon:last], at_in[soon:last], middle, made["early"])
    ends = [ready(line, across, i, last, last + 1) for i in range(CHUNKS)]
    mine = project(activations, made["a"], slots[last:], at_in[last:], ends, middle)

    held, send = outer_first(g_own, g_sibling, mine, swap_core(mine), width)
    sends = [send] + list(outer(g_own, g_sibling, held, width, 1, nz - 1, BF16))
    keeps = list(outer(g_own, g_sibling, held, width, nz, nz, F32))
    terms = [keep + swap_y(send).astype(F32) for keep, send in zip(keeps, sends)]
    passed = terms[0]
    for term in terms[1 : nz - 2]:
        passed = term + shift_z(passed.astype(BF16), 1).astype(F32)
    reduced = terms[nz - 1] + shift_z(terms[nz - 2].astype(BF16), nz - 1).astype(F32) + shift_z(passed.astype(BF16), 1).astype(F32)
    new_first, new_second, direction = adam(reduced, first_moment, second_moment)
    projector_t = after(projector, terms[0]).T

    def beside_direction(step, i, line, across):
        if step == nz // 2 or step == nz - 1:
            low, high = (0, half) if step == nz // 2 else (half, last)
            made[low, i] = jnp.concatenate(ready(line, across, i, low, high), axis=0)
            made["swapped", low, i] = swap_core(made[low, i])
        return []

    line, across = gather([direction[:, part] for part in parts], beside_direction)
    chunks = range(CHUNKS)
    at_back = [named([(k, dy, dc) for dc in (0, 1) for k, dy in order]) for order in (order_in[:half], order_in[half:])]
    groups = [[made[0, i] for i in chunks], [made["swapped", 0, i] for i in chunks]]
    update = back(groups, projector_t, at_back[0], width, 4 * nz * width, None)
    ends = [across[i][-1] for i in chunks]
    groups = [[made[half, i] for i in chunks], ends, [made["swapped", half, i] for i in chunks], [swap_core(x) for x in ends]]
    update = back(groups, projector_t, at_back[1], width, 4 * nz * width, update)
    return update, new_first, new_second


def solution(mesh):
    devices = mesh.shape["dp"]

    def body(activations, out_grads, projector, first_moment, second_moment):
        aligned = projector.shape[0] % 128 == 0 and first_moment.shape[0] % 128 == 0
        if devices % 4 or devices < 16 or not aligned:
            return plain(activations, out_grads, projector, first_moment, second_moment)
        return levels(activations, out_grads, projector, first_moment, second_moment, nz=devices // 4)

    placed = P(("groups", "dp"), None)
    return jax.shard_map(
        body,
        mesh=mesh,
        in_specs=(placed,) * 5,
        out_specs=(P("groups", "dp"), placed, placed),
        check_vma=False,
    )
```

```python
import functools
import jax
import jax.numpy as jnp
from jax import lax
from jax.experimental import pallas as pl
from jax.experimental.pallas import tpu as pltpu
from jax.sharding import PartitionSpec as P

STEP = 100

decay_first = 0.9
decay_second = 0.999
epsilon = 1e-08

CHUNKS = 2
F32, BF16 = jnp.float32, jnp.bfloat16
VMEM_LIMIT = 16 * 1024 * 1024


def adam(reduced, first_moment, second_moment):
    new_first = decay_first * first_moment + (1.0 - decay_first) * reduced
    new_second = decay_second * second_moment + (1.0 - decay_second) * reduced * reduced
    first_fix = 1.0 - decay_first**STEP
    second_fix = 1.0 - decay_second**STEP
    direction = (new_first / first_fix / (jnp.sqrt(new_second / second_fix) + epsilon)).astype(BF16)
    return new_first, new_second, direction


def plain(activations, out_grads, projector, first_moment, second_moment):
    projected = jnp.dot(
        activations,
        lax.all_gather(projector, "dp", axis=0, tiled=True),
        preferred_element_type=F32,
    ).astype(BF16)
    reduced = lax.psum_scatter(
        lax.dot_general(out_grads, projected, (((0,), (0,)), ((), ())), preferred_element_type=F32),
        "dp",
        scatter_dimension=0,
        tiled=True,
    )
    new_first, new_second, direction = adam(reduced, first_moment, second_moment)
    update = lax.dot_general(
        lax.all_gather(direction, "dp", axis=0, tiled=True),
        projector,
        (((1,), (1,)), ((), ())),
        preferred_element_type=F32,
    ).astype(BF16)
    return update, new_first, new_second


def params():
    return pltpu.CompilerParams(vmem_limit_bytes=VMEM_LIMIT)


def cost(flops, moved):
    return pl.CostEstimate(flops=flops, bytes_accessed=moved, transcendentals=0)


def take(array, at, width):
    rows, many = array.shape[0], at.shape[0]

    def kernel(at_ref, in_ref, out_ref, sems):
        copies = []
        for j in range(many):
            source = in_ref.at[:, pl.ds(pl.multiple_of(at_ref[j] * width, width), width)]
            copies.append(pltpu.make_async_copy(source, out_ref.at[:, pl.ds(j * width, width)], sems.at[j]))
            copies[-1].start()
        for copy in copies:
            copy.wait()

    return pl.pallas_call(
        kernel,
        grid_spec=pltpu.PrefetchScalarGridSpec(
            num_scalar_prefetch=1,
            grid=(1,),
            in_specs=[pl.BlockSpec(memory_space=pl.ANY)],
            out_specs=pl.BlockSpec((rows, many * width), lambda j, at_ref: (0, 0)),
            scratch_shapes=[pltpu.SemaphoreType.DMA((many,))],
        ),
        out_shape=jax.ShapeDtypeStruct((rows, many * width), array.dtype),
        compiler_params=params(),
        cost_estimate=cost(0, 4 * rows * many * width),
        name="take",
    )(at, pinned(array))


def turn(array, at, width):
    rows, many = array.shape[0], at.shape[0]
    half = many // 2

    def kernel(at_ref, in_ref, first_ref, second_ref, held, sem):
        copy = pltpu.make_async_copy(in_ref, held, sem)
        copy.start()
        copy.wait()
        for j in range(many):
            block = held[:, pl.ds(pl.multiple_of(at_ref[j] * width, width), width)]
            out_ref, i = (first_ref, j) if j < half else (second_ref, j - half)
            out_ref[i * width : (i + 1) * width, :] = block.T

    return pl.pallas_call(
        kernel,
        grid_spec=pltpu.PrefetchScalarGridSpec(
            num_scalar_prefetch=1,
            grid=(1,),
            in_specs=[pl.BlockSpec(memory_space=pl.ANY)],
            out_specs=[pl.BlockSpec((half * width, rows), lambda j, at_ref: (0, 0))] * 2,
            scratch_shapes=[pltpu.VMEM(array.shape, array.dtype), pltpu.SemaphoreType.DMA],
        ),
        out_shape=[jax.ShapeDtypeStruct((half * width, rows), array.dtype)] * 2,
        compiler_params=params(),
        cost_estimate=cost(0, 4 * rows * many * width),
        name="turn",
    )(at, pinned(array))


def pinned(x):
    return pltpu.with_memory_space_constraint(x, pltpu.HBM)


def call(kernel, scalars, arrays, outs, scratch, *, flops, moved, name, aliases=None, in_hbm=0):
    anywhere = pl.BlockSpec(memory_space=pl.ANY)
    return pl.pallas_call(
        kernel,
        grid_spec=pltpu.PrefetchScalarGridSpec(
            num_scalar_prefetch=1,
            grid=(),
            in_specs=[anywhere] * len(arrays),
            out_specs=[anywhere] * len(outs),
            scratch_shapes=scratch,
        ),
        out_shape=outs,
        input_output_aliases=aliases or {},
        compiler_params=params(),
        cost_estimate=cost(flops, moved),
        name=name,
    )(scalars, *[pinned(x) for x in arrays[:in_hbm]], *arrays[in_hbm:])


def project(activations, sibling, slots, at, blocks, before):
    chunks, many = len(blocks), len(blocks[0])
    (depth, cols), rows = blocks[0][0].shape, activations.shape[0]
    copies = many * (2 + chunks)
    flat = [block for chunk in blocks for block in chunk]
    held = [] if before is None else [before]

    def kernel(at_ref, own_ref, *refs):
        sib_refs, refs = refs[: len(sibling)], refs[len(sibling) :]
        block_refs, out_ref = refs[: chunks * many], refs[chunks * many + len(held)]
        a, b, total, sems = refs[chunks * many + len(held) + 1 :]
        started = []
        for j in range(many):
            start = pl.multiple_of(at_ref[j] * depth, depth)
            moves = [
                (own_ref.at[:, pl.ds(start, depth)], a.at[pl.ds(0, rows), pl.ds(j * depth, depth)]),
                (sib_refs[slots[j][0]].at[:, pl.ds(slots[j][1] * depth, depth)], a.at[pl.ds(rows, rows), pl.ds(j * depth, depth)]),
            ]
            for i in range(chunks):
                moves.append((block_refs[i * many + j], b.at[pl.ds(j * depth, depth), pl.ds(i * cols, cols)]))
            for source, target in moves:
                started.append(pltpu.make_async_copy(source, target, sems.at[len(started)]))
                started[-1].start()
        if held:
            started.append(pltpu.make_async_copy(refs[chunks * many], total, sems.at[len(started)]))
            started[-1].start()
        for copy in started:
            copy.wait()
        for i in range(chunks):
            part = slice(i * cols, (i + 1) * cols)
            term = jnp.dot(a[...], b[:, part], preferred_element_type=F32)
            total[:, part] = total[:, part] + term if held else term
        back_copy = pltpu.make_async_copy(total, out_ref, sems.at[len(started)])
        back_copy.start()
        back_copy.wait()

    wide = chunks * cols
    return call(
        kernel,
        at,
        [activations, *sibling, *flat, *held],
        [jax.ShapeDtypeStruct((2 * rows, wide), F32)],
        [
            pltpu.VMEM((2 * rows, many * depth), BF16),
            pltpu.VMEM((many * depth, wide), BF16),
            pltpu.VMEM((2 * rows, wide), F32),
            pltpu.SemaphoreType.DMA((copies + len(held) + 1,)),
        ],
        flops=4 * rows * depth * many * wide,
        moved=4 * rows * depth * many + 2 * depth * many * wide + 8 * rows * wide,
        name="project",
        in_hbm=1,
    )[0]


def outer_first(own, sibling, mine, theirs, width):
    rows, cols = own.shape[1], mine.shape[1]

    def kernel(own_ref, sib_ref, mine_ref, theirs_ref, held_ref, out_ref):
        held_ref[:rows, :] = (mine_ref[:rows, :] + theirs_ref[rows:, :]).astype(BF16)
        held_ref[rows:, :] = (mine_ref[rows:, :] + theirs_ref[:rows, :]).astype(BF16)
        term = jnp.dot(own_ref[...], held_ref[:rows, :], preferred_element_type=F32)
        term += jnp.dot(sib_ref[...], held_ref[rows:, :], preferred_element_type=F32)
        out_ref[...] = term.astype(BF16)

    whole = lambda *shape: pl.BlockSpec(shape, lambda j: (0, 0))
    return pl.pallas_call(
        kernel,
        grid=(1,),
        in_specs=[whole(width, rows), whole(width, rows), whole(2 * rows, cols), whole(2 * rows, cols)],
        out_specs=[whole(2 * rows, cols), whole(width, cols)],
        out_shape=[jax.ShapeDtypeStruct((2 * rows, cols), BF16), jax.ShapeDtypeStruct((width, cols), BF16)],
        compiler_params=params(),
        cost_estimate=cost(4 * rows * width * cols, 4 * rows * width + 20 * rows * cols),
        name="outer_first",
    )(own, sibling, mine, theirs)


def outer(own, sibling, held, width, start, many, dtype):
    rows, cols = own.shape[1], held.shape[1]

    def kernel(own_ref, sib_ref, held_ref, *out_refs):
        for j, out_ref in enumerate(out_refs):

            @pl.when(pl.program_id(0) == j)
            def _(out_ref=out_ref):
                term = jnp.dot(own_ref[...], held_ref[:rows, :], preferred_element_type=F32)
                term += jnp.dot(sib_ref[...], held_ref[rows:, :], preferred_element_type=F32)
                out_ref[...] = term.astype(dtype)

    return pl.pallas_call(
        kernel,
        grid=(many,),
        in_specs=[
            pl.BlockSpec((width, rows), lambda j: (start + j, 0)),
            pl.BlockSpec((width, rows), lambda j: (start + j, 0)),
            pl.BlockSpec((2 * rows, cols), lambda j: (0, 0)),
        ],
        out_specs=[pl.BlockSpec((width, cols), lambda j: (0, 0))] * many,
        out_shape=[jax.ShapeDtypeStruct((width, cols), dtype)] * many,
        compiler_params=params(),
        cost_estimate=cost(4 * rows * width * many * cols, many * (4 * rows * width + 4 * width * cols)),
        name="outer",
    )(own, sibling, held)


def back(groups, projector_t, at, rows, rows_in_all, before):
    many, chunks, cols = at.shape[0], len(groups[0]), groups[0][0].shape[1]
    rank, width = projector_t.shape
    arrays = [x for group in groups for x in group]
    held = [] if before is None else [before]
    slots = min(4, many)

    def kernel(at_ref, projector_ref, *refs):
        array_refs, out_ref = refs[: len(arrays)], refs[len(arrays) + len(held)]
        p, d, o, in_sems, out_sems = refs[len(arrays) + len(held) + 1 :]
        loads, stores, waits = [pltpu.make_async_copy(projector_ref, p, in_sems.at[len(arrays)])], [], {}
        start = 0
        for g, group in enumerate(groups):
            size = group[0].shape[0]
            for i in range(chunks):
                target = d.at[pl.ds(start, size), pl.ds(i * cols, cols)]
                loads.append(pltpu.make_async_copy(array_refs[g * chunks + i], target, in_sems.at[g * chunks + i]))
            waits[start // rows] = loads[-chunks:]
            start += size
        for copy in loads:
            copy.start()
        loads[0].wait()
        for j in range(many):
            for copy in waits.get(j, []):
                copy.wait()
            if j >= slots:
                stores[j - slots].wait()
            block = d[j * rows : (j + 1) * rows, :]
            o[j % slots] = jnp.dot(block, p[...], preferred_element_type=F32).astype(BF16)
            target = out_ref.at[pl.ds(pl.multiple_of(at_ref[j] * rows, rows), rows), :]
            stores.append(pltpu.make_async_copy(o.at[j % slots], target, out_sems.at[j % slots]))
            stores[-1].start()
        for j in range(many - slots, many):
            stores[j].wait()

    return call(
        kernel,
        at,
        [projector_t, *arrays, *held],
        [jax.ShapeDtypeStruct((rows_in_all, width), BF16)],
        [
            pltpu.VMEM((rank, width), BF16),
            pltpu.VMEM((many * rows, rank), BF16),
            pltpu.VMEM((slots, rows, width), BF16),
            pltpu.SemaphoreType.DMA((len(arrays) + 1,)),
            pltpu.SemaphoreType.DMA((slots,)),
        ],
        flops=2 * many * rows * width * rank,
        moved=2 * many * rows * (width + rank),
        name="back",
        aliases={2 + len(arrays): 0} if held else None,
    )[0]


def levels(activations, out_grads, projector, first_moment, second_moment, *, nz):
    me = lax.axis_index("dp")
    z, y, core = me // 4, me // 2 % 2, me % 2
    grid = [(a, b, c) for a in range(nz) for b in range(2) for c in range(2)]

    def pairs(to):
        return [((a * 2 + b) * 2 + c, (to(a, b, c)[0] * 2 + to(a, b, c)[1]) * 2 + to(a, b, c)[2]) for a, b, c in grid]

    def swap_core(x):
        return lax.ppermute(x, "dp", pairs(lambda a, b, c: (a, b, 1 - c)))

    def swap_y(x):
        return lax.ppermute(x, "dp", pairs(lambda a, b, c: (a, 1 - b, c)))

    def shift_z(x, k):
        return lax.ppermute(x, "dp", pairs(lambda a, b, c: ((a + k) % nz, b, c)))

    def index(k, dy, dc):
        return (lax.rem(z + nz + k, nz) * 2 + (1 - y if dy else y)) * 2 + (1 - core if dc else core)

    def named(order):
        return jnp.stack([index(*o) for o in order]).astype(jnp.int32)

    def gather(chunks, beside):
        line = [[own] for own in chunks]
        across = [[] for _ in chunks]
        for step in range(nz):
            for i in range(len(chunks)):
                if step:
                    ready = beside(step, i, line, across)
                    line[i][step], across[i][step - 1], *_ = lax.optimization_barrier((line[i][step], across[i][step - 1], *ready))
                if step < nz - 1:
                    line[i].append(shift_z(line[i][step], 1))
                if step < nz - 1 or i < len(chunks) - 1:
                    across[i].append(swap_y(line[i][step]))
                else:
                    across[i].append(shift_z(across[i][0], nz - 1))
        return line, across

    after = lambda x, *those: lax.optimization_barrier((x, *those))[0]
    ks = list(range(nz - 2, 0, -1)) + [nz - 1]
    depth, rank = projector.shape
    width = first_moment.shape[0]
    cols = rank // CHUNKS
    parts = [slice(i * cols, (i + 1) * cols) for i in range(CHUNKS)]

    order_in = [(-k, dy) for k in range(nz) for dy in (0, 1)]
    order_out = [(k, dy) for dy in (1, 0) for k in ks + [0]]
    last, half = len(order_in) - 1, len(order_in) // 2
    at_in = named([(k, dy, 0) for k, dy in order_in])
    at_sibling = named([(k, dy, 1) for k, dy in order_in])
    at_out = named([(k, dy, dc) for dc in (0, 1) for k, dy in order_out])
    slots = [(j // half, j % half) for j in range(len(order_in))]
    made = {}

    def ready(line, across, i, low, high):
        return [(across if n % 2 else line)[i][n // 2] for n in range(low, high)]

    def beside_projector(step, i, line, across):
        if (step, i) == (1, 1):
            made["a0"] = take(activations, after(at_sibling[:half], line[1][1]), depth)
            return [made["a0"]]
        if (step, i) == (2, 0):
            made["a1"] = take(activations, after(at_sibling[half:], line[0][2]), depth)
            made["a"] = [swap_core(made["a0"]), swap_core(made["a1"])]
            return [made["a1"]]
        if (step, i) == (2, 1):
            made["own"], made["other"] = turn(out_grads, after(at_out, line[1][2]), width)
            return [made["own"], made["other"]]
        if (step, i) == (nz - 1, 0):
            blocks = [ready(line, across, n, 0, soon) for n in range(CHUNKS)]
            made["early"] = project(activations, made["a"], slots[:soon], after(at_in[:soon], line[0][nz - 1]), blocks, None)
            return [made["early"]]
        return []

    soon = last - 2
    line, across = gather([projector[:, part] for part in parts], beside_projector)
    g_own, g_sibling = made["own"], swap_core(made["other"])
    middle = [ready(line, across, i, soon, last) for i in range(CHUNKS)]
    middle = project(activations, made["a"], slots[soon:last], at_in[soon:last], middle, made["early"])
    ends = [ready(line, across, i, last, last + 1) for i in range(CHUNKS)]
    mine = project(activations, made["a"], slots[last:], at_in[last:], ends, middle)

    held, send = outer_first(g_own, g_sibling, mine, swap_core(mine), width)
    sends = [send] + list(outer(g_own, g_sibling, held, width, 1, nz - 1, BF16))
    keeps = list(outer(g_own, g_sibling, held, width, nz, nz, F32))
    terms = [keep + swap_y(send).astype(F32) for keep, send in zip(keeps, sends)]
    passed = terms[0]
    for term in terms[1 : nz - 2]:
        passed = term + shift_z(passed.astype(BF16), 1).astype(F32)
    reduced = terms[nz - 1] + shift_z(terms[nz - 2].astype(BF16), nz - 1).astype(F32) + shift_z(passed.astype(BF16), 1).astype(F32)
    new_first, new_second, direction = adam(reduced, first_moment, second_moment)
    projector_t = after(projector, terms[0]).T

    def beside_direction(step, i, line, across):
        if step == nz // 2 or step == nz - 1:
            low, high = (0, half) if step == nz // 2 else (half, last)
            made[low, i] = jnp.concatenate(ready(line, across, i, low, high), axis=0)
            made["swapped", low, i] = swap_core(made[low, i])
        return [projector_t] if (step, i) == (1, 1) else []

    line, across = gather([direction[:, part] for part in parts], beside_direction)
    chunks = range(CHUNKS)
    at_back = [named([(k, dy, dc) for dc in (0, 1) for k, dy in order]) for order in (order_in[:half], order_in[half:])]
    groups = [[made[0, i] for i in chunks], [made["swapped", 0, i] for i in chunks]]
    update = back(groups, projector_t, at_back[0], width, 4 * nz * width, None)
    ends = [across[i][-1] for i in chunks]
    groups = [[made[half, i] for i in chunks], ends, [made["swapped", half, i] for i in chunks], [swap_core(after(x, update)) for x in ends]]
    update = back(groups, projector_t, at_back[1], width, 4 * nz * width, update)
    return update, new_first, new_second


def solution(mesh):
    devices = mesh.shape["dp"]

    def body(activations, out_grads, projector, first_moment, second_moment):
        aligned = projector.shape[0] % 128 == 0 and first_moment.shape[0] % 128 == 0
        if devices % 4 or devices < 16 or not aligned:
            return plain(activations, out_grads, projector, first_moment, second_moment)
        return levels(activations, out_grads, projector, first_moment, second_moment, nz=devices // 4)

    placed = P(("groups", "dp"), None)
    return jax.shard_map(
        body,
        mesh=mesh,
        in_specs=(placed,) * 5,
        out_specs=(P("groups", "dp"), placed, placed),
        check_vma=False,
    )
```

```python
import functools
import jax
import jax.numpy as jnp
from jax import lax
from jax.experimental import pallas as pl
from jax.experimental.pallas import tpu as pltpu
from jax.sharding import PartitionSpec as P

STEP = 100

decay_first = 0.9
decay_second = 0.999
epsilon = 1e-08

CHUNKS = 2
COSTX = 30
F32, BF16 = jnp.float32, jnp.bfloat16
VMEM_LIMIT = 16 * 1024 * 1024


def adam(reduced, first_moment, second_moment):
    new_first = decay_first * first_moment + (1.0 - decay_first) * reduced
    new_second = decay_second * second_moment + (1.0 - decay_second) * reduced * reduced
    first_fix = 1.0 - decay_first**STEP
    second_fix = 1.0 - decay_second**STEP
    direction = (new_first / first_fix / (jnp.sqrt(new_second / second_fix) + epsilon)).astype(BF16)
    return new_first, new_second, direction


def plain(activations, out_grads, projector, first_moment, second_moment):
    projected = jnp.dot(
        activations,
        lax.all_gather(projector, "dp", axis=0, tiled=True),
        preferred_element_type=F32,
    ).astype(BF16)
    reduced = lax.psum_scatter(
        lax.dot_general(out_grads, projected, (((0,), (0,)), ((), ())), preferred_element_type=F32),
        "dp",
        scatter_dimension=0,
        tiled=True,
    )
    new_first, new_second, direction = adam(reduced, first_moment, second_moment)
    update = lax.dot_general(
        lax.all_gather(direction, "dp", axis=0, tiled=True),
        projector,
        (((1,), (1,)), ((), ())),
        preferred_element_type=F32,
    ).astype(BF16)
    return update, new_first, new_second


def params():
    return pltpu.CompilerParams(vmem_limit_bytes=VMEM_LIMIT)


def cost(flops, moved):
    return pl.CostEstimate(flops=COSTX * flops, bytes_accessed=COSTX * moved, transcendentals=0)


def pinned(x):
    return pltpu.with_memory_space_constraint(x, pltpu.HBM)


def call(kernel, scalars, arrays, outs, scratch, *, flops, moved, name, aliases=None, in_hbm=0):
    anywhere = pl.BlockSpec(memory_space=pl.ANY)
    return pl.pallas_call(
        kernel,
        grid_spec=pltpu.PrefetchScalarGridSpec(
            num_scalar_prefetch=1,
            grid=(),
            in_specs=[anywhere] * len(arrays),
            out_specs=[anywhere] * len(outs),
            scratch_shapes=scratch,
        ),
        out_shape=outs,
        input_output_aliases=aliases or {},
        compiler_params=params(),
        cost_estimate=cost(flops, moved),
        name=name,
    )(scalars, *[pinned(x) for x in arrays[:in_hbm]], *arrays[in_hbm:])


def project(activations, sibling, at, blocks, before):
    chunks, many = len(blocks), len(blocks[0])
    (depth, cols), rows = blocks[0][0].shape, activations.shape[0]
    copies = many * (2 + chunks)
    flat = [block for chunk in blocks for block in chunk]
    held = [] if before is None else [before]

    def kernel(at_ref, own_ref, sib_ref, *refs):
        block_refs, out_ref = refs[: chunks * many], refs[chunks * many + len(held)]
        a, b, total, sems = refs[chunks * many + len(held) + 1 :]
        started = []
        for j in range(many):
            columns = pl.ds(pl.multiple_of(at_ref[j] * depth, depth), depth)
            moves = [
                (own_ref.at[:, columns], a.at[pl.ds(0, rows), pl.ds(j * depth, depth)]),
                (sib_ref.at[:, columns], a.at[pl.ds(rows, rows), pl.ds(j * depth, depth)]),
            ]
            for i in range(chunks):
                moves.append((block_refs[i * many + j], b.at[pl.ds(j * depth, depth), pl.ds(i * cols, cols)]))
            for source, target in moves:
                started.append(pltpu.make_async_copy(source, target, sems.at[len(started)]))
                started[-1].start()
        if held:
            started.append(pltpu.make_async_copy(refs[chunks * many], total, sems.at[len(started)]))
            started[-1].start()
        groups = [(0, (many + 1) // 2), ((many + 1) // 2, many)] if many > 1 else [(0, 1)]
        for at, (low, high) in enumerate(groups):
            for copy in started[low * (2 + chunks) : high * (2 + chunks)] + (started[copies:] if at == 0 else []):
                copy.wait()
            deep = slice(low * depth, high * depth)
            term = jnp.dot(a[:, deep], b[deep, :], preferred_element_type=F32)
            total[...] = total[...] + term if held or at else term
        back_copy = pltpu.make_async_copy(total, out_ref, sems.at[len(started)])
        back_copy.start()
        back_copy.wait()

    wide = chunks * cols
    return call(
        kernel,
        at,
        [activations, sibling, *flat, *held],
        [jax.ShapeDtypeStruct((2 * rows, wide), F32)],
        [
            pltpu.VMEM((2 * rows, many * depth), BF16),
            pltpu.VMEM((many * depth, wide), BF16),
            pltpu.VMEM((2 * rows, wide), F32),
            pltpu.SemaphoreType.DMA((copies + 2,)),
        ],
        flops=4 * rows * depth * many * wide,
        moved=4 * rows * depth * many + 2 * depth * many * wide + 8 * rows * wide,
        name="project",
        in_hbm=2,
    )[0]


def outer(out_grads, sibling, at, width, dtype, projected):
    rows, many, cols = out_grads.shape[0], at.shape[0], projected.shape[1]

    def kernel(at_ref, own_ref, sib_ref, projected_ref, *refs):
        outs, (g, sems) = refs[:-2], refs[-2:]
        copies = []
        for j in range(many):
            columns = pl.ds(pl.multiple_of(at_ref[j] * width, width), width)
            for i, ref in enumerate((own_ref, sib_ref)):
                target = g.at[pl.ds(i * rows, rows), pl.ds(j * width, width)]
                copies.append(pltpu.make_async_copy(ref.at[:, columns], target, sems.at[len(copies)]))
                copies[-1].start()
        for j in range(many):
            copies[2 * j].wait()
            copies[2 * j + 1].wait()
            block = g[:, j * width : (j + 1) * width].T
            outs[j][...] = jnp.dot(block, projected_ref[...], preferred_element_type=F32).astype(dtype)

    whole = lambda *shape: pl.BlockSpec(shape, lambda j, at_ref: (0, 0))
    return pl.pallas_call(
        kernel,
        grid_spec=pltpu.PrefetchScalarGridSpec(
            num_scalar_prefetch=1,
            grid=(1,),
            in_specs=[pl.BlockSpec(memory_space=pl.ANY)] * 2 + [whole(2 * rows, cols)],
            out_specs=[whole(width, cols)] * many,
            scratch_shapes=[pltpu.VMEM((2 * rows, many * width), BF16), pltpu.SemaphoreType.DMA((2 * many,))],
        ),
        out_shape=[jax.ShapeDtypeStruct((width, cols), dtype)] * many,
        compiler_params=params(),
        cost_estimate=cost(4 * rows * width * many * cols, many * (4 * rows * width + 4 * width * cols)),
        name="outer",
    )(at, pinned(out_grads), pinned(sibling), projected)


def back(blocks, projectors_t, at, rows_in_all, before):
    many, chunks = len(blocks), len(blocks[0])
    (rows, cols), (rank, both) = blocks[0][0].shape, projectors_t.shape
    width = both // 2
    arrays = [x for block in blocks for x in block]
    held = [] if before is None else [before]

    def kernel(at_ref, projector_ref, *refs):
        array_refs, (out_ref, other_ref) = refs[: len(arrays)], refs[len(arrays) + len(held) :][:2]
        p, d, o, in_sems, out_sems = refs[len(arrays) + len(held) + 2 :]
        p_copy = pltpu.make_async_copy(projector_ref, p, in_sems.at[len(arrays)])
        p_copy.start()
        loads, stores = [], []
        for n, ref in enumerate(array_refs):
            j, i = n // chunks, n % chunks
            loads.append(pltpu.make_async_copy(ref, d.at[pl.ds(j * rows, rows), pl.ds(i * cols, cols)], in_sems.at[n]))
            loads[-1].start()
        p_copy.wait()
        for j in range(many):
            for copy in loads[j * chunks : (j + 1) * chunks]:
                copy.wait()
            here = pl.ds(j * rows, rows)
            o[here, :] = jnp.dot(d[here, :], p[...], preferred_element_type=F32).astype(BF16)
            for n, (columns, target) in enumerate(
                (
                    (pl.ds(0, width), out_ref.at[pl.ds(pl.multiple_of(at_ref[j] * rows, rows), rows), :]),
                    (pl.ds(width, width), other_ref.at[here, :]),
                )
            ):
                stores.append(pltpu.make_async_copy(o.at[here, columns], target, out_sems.at[2 * j + n]))
                stores[-1].start()
        for copy in stores:
            copy.wait()

    return call(
        kernel,
        at,
        [projectors_t, *arrays, *held],
        [jax.ShapeDtypeStruct((rows_in_all, width), BF16), jax.ShapeDtypeStruct((many * rows, width), BF16)],
        [
            pltpu.VMEM((rank, both), BF16),
            pltpu.VMEM((many * rows, rank), BF16),
            pltpu.VMEM((many * rows, both), BF16),
            pltpu.SemaphoreType.DMA((len(arrays) + 1,)),
            pltpu.SemaphoreType.DMA((2 * many,)),
        ],
        flops=2 * many * rows * both * rank,
        moved=2 * many * rows * (both + rank),
        name="back",
        aliases={2 + len(arrays): 0} if held else None,
    )


def place(whole, pieces, at, rows):
    many, width, sizes = at.shape[0], whole.shape[1], [piece.shape[0] for piece in pieces]

    def kernel(at_ref, *refs):
        piece_refs, (out_ref, held, sems) = refs[: len(pieces)], refs[len(pieces) + 1 :]
        copies, start = [], 0
        for n, ref in enumerate(piece_refs):
            copies.append(pltpu.make_async_copy(ref, held.at[pl.ds(start, sizes[n]), :], sems.at[n]))
            copies[-1].start()
            start += sizes[n]
        for copy in copies:
            copy.wait()
        copies = []
        for j in range(many):
            target = out_ref.at[pl.ds(pl.multiple_of(at_ref[j] * rows, rows), rows), :]
            copies.append(pltpu.make_async_copy(held.at[pl.ds(j * rows, rows), :], target, sems.at[len(pieces) + j]))
            copies[-1].start()
        for copy in copies:
            copy.wait()

    return call(
        kernel,
        at,
        [*pieces, whole],
        [jax.ShapeDtypeStruct(whole.shape, whole.dtype)],
        [pltpu.VMEM((many * rows, width), whole.dtype), pltpu.SemaphoreType.DMA((len(pieces) + many,))],
        flops=0,
        moved=4 * many * rows * width,
        name="place",
        aliases={1 + len(pieces): 0},
    )[0]


def levels(activations, out_grads, projector, first_moment, second_moment, *, nz):
    me = lax.axis_index("dp")
    z, y, core = me // 4, me // 2 % 2, me % 2
    grid = [(a, b, c) for a in range(nz) for b in range(2) for c in range(2)]

    def pairs(to):
        return [((a * 2 + b) * 2 + c, (to(a, b, c)[0] * 2 + to(a, b, c)[1]) * 2 + to(a, b, c)[2]) for a, b, c in grid]

    def swap_core(x):
        return lax.ppermute(x, "dp", pairs(lambda a, b, c: (a, b, 1 - c)))

    def swap_y(x):
        return lax.ppermute(x, "dp", pairs(lambda a, b, c: (a, 1 - b, c)))

    def shift_z(x, k):
        return lax.ppermute(x, "dp", pairs(lambda a, b, c: ((a + k) % nz, b, c)))

    def index(k, dy, dc):
        return (lax.rem(z + nz + k, nz) * 2 + (1 - y if dy else y)) * 2 + (1 - core if dc else core)

    def named(order):
        return jnp.stack([index(*o) for o in order]).astype(jnp.int32)

    def gather(chunks):
        line = [[own] for own in chunks]
        across = [[] for _ in chunks]
        for step in range(nz):
            for i in range(len(chunks)):
                if step:
                    line[i][step], across[i][step - 1] = lax.optimization_barrier((line[i][step], across[i][step - 1]))
                if step < nz - 1:
                    line[i].append(shift_z(line[i][step], 1))
                if step < nz - 1 or i < len(chunks) - 1:
                    across[i].append(swap_y(line[i][step]))
                else:
                    across[i].append(shift_z(across[i][0], nz - 1))
        return line, across

    after = lambda x, *those: lax.optimization_barrier((x, *those))[0]
    ks = list(range(nz - 2, 0, -1)) + [nz - 1]
    depth, rank = projector.shape
    width = first_moment.shape[0]
    cols = rank // CHUNKS
    parts = [slice(i * cols, (i + 1) * cols) for i in range(CHUNKS)]

    order_in = [(-k, dy) for k in range(nz) for dy in (0, 1)]
    order_out = [(k, dy) for dy in (1, 0) for k in ks + [0]]
    last = len(order_in) - 1
    at_in = named([(k, dy, 0) for k, dy in order_in])
    at_out = named([(k, dy, 0) for k, dy in order_out])
    at_sibling = named([(k, dy, 1) for k, dy in order_in])

    def ready(line, across, low, high):
        return [[(across if n % 2 else line)[i][n // 2] for n in range(low, high)] for i in range(CHUNKS)]

    a_sibling = swap_core(activations)
    made = {"end": 0, "mine": None}

    def project_to(end, line, across):
        low = made["end"]
        made["mine"] = project(activations, a_sibling, at_in[low:end], ready(line, across, low, end), made["mine"])
        made["end"] = end
        return made["mine"]

    line, across = gather([projector[:, part] for part in parts])
    p_sibling = swap_core(after(projector, a_sibling, line[0][2]))
    g_sibling = swap_core(after(out_grads, p_sibling))
    project_to(last, line, across)
    mine = project_to(last + 1, line, across)

    projectors_t = jnp.concatenate([after(projector, mine).T, after(p_sibling, mine).T], axis=1)
    theirs = after(swap_core(mine), projectors_t)
    rows = activations.shape[0]
    projected = (mine + jnp.concatenate([theirs[rows:], theirs[:rows]], axis=0)).astype(BF16)
    sends, keeps = [], []
    for low, high in ((0, 1), (1, nz)):
        sends += list(outer(out_grads, g_sibling, at_out[low:high], width, BF16, projected))
    keeps = list(outer(out_grads, g_sibling, at_out[nz:], width, F32, projected))
    terms = [keep + swap_y(send).astype(F32) for keep, send in zip(keeps, sends)]
    passed = terms[0]
    for term in terms[1 : nz - 2]:
        passed = term + shift_z(passed.astype(BF16), 1).astype(F32)
    reduced = terms[nz - 1] + shift_z(terms[nz - 2].astype(BF16), nz - 1).astype(F32) + shift_z(passed.astype(BF16), 1).astype(F32)
    new_first, new_second, direction = adam(reduced, first_moment, second_moment)

    line, across = gather([direction[:, part] for part in parts])
    rows_in_all = 4 * nz * width
    update, early = back(list(zip(*ready(line, across, 0, last))), projectors_t, at_in[:last], rows_in_all, None)
    early = swap_core(early)
    ends = [x[0] for x in ready(line, across, last, last + 1)]
    update, late = back([ends], projectors_t, at_in[last:], rows_in_all, update)
    update = place(update, [early, swap_core(late)], at_sibling, width)
    return update, new_first, new_second


def solution(mesh):
    devices = mesh.shape["dp"]

    def body(activations, out_grads, projector, first_moment, second_moment):
        aligned = projector.shape[0] % 128 == 0 and first_moment.shape[0] % 128 == 0
        if devices % 4 or devices < 16 or not aligned:
            return plain(activations, out_grads, projector, first_moment, second_moment)
        return levels(activations, out_grads, projector, first_moment, second_moment, nz=devices // 4)

    placed = P(("groups", "dp"), None)
    return jax.shard_map(
        body,
        mesh=mesh,
        in_specs=(placed,) * 5,
        out_specs=(P("groups", "dp"), placed, placed),
        check_vma=False,
    )
```

```python
import functools
import jax
import jax.numpy as jnp
from jax import lax
from jax.experimental import pallas as pl
from jax.experimental.pallas import tpu as pltpu
from jax.sharding import PartitionSpec as P

STEP = 100

decay_first = 0.9
decay_second = 0.999
epsilon = 1e-08

CHUNKS = 2
W_EARLY, W_LATE, W_OUTER, W_BACK, W_LAST = 30, 30, 30, 30, 30000
F32, BF16 = jnp.float32, jnp.bfloat16
VMEM_LIMIT = 16 * 1024 * 1024


def adam(reduced, first_moment, second_moment):
    new_first = decay_first * first_moment + (1.0 - decay_first) * reduced
    new_second = decay_second * second_moment + (1.0 - decay_second) * reduced * reduced
    first_fix = 1.0 - decay_first**STEP
    second_fix = 1.0 - decay_second**STEP
    direction = (new_first / first_fix / (jnp.sqrt(new_second / second_fix) + epsilon)).astype(BF16)
    return new_first, new_second, direction


def plain(activations, out_grads, projector, first_moment, second_moment):
    projected = jnp.dot(
        activations,
        lax.all_gather(projector, "dp", axis=0, tiled=True),
        preferred_element_type=F32,
    ).astype(BF16)
    reduced = lax.psum_scatter(
        lax.dot_general(out_grads, projected, (((0,), (0,)), ((), ())), preferred_element_type=F32),
        "dp",
        scatter_dimension=0,
        tiled=True,
    )
    new_first, new_second, direction = adam(reduced, first_moment, second_moment)
    update = lax.dot_general(
        lax.all_gather(direction, "dp", axis=0, tiled=True),
        projector,
        (((1,), (1,)), ((), ())),
        preferred_element_type=F32,
    ).astype(BF16)
    return update, new_first, new_second


def params():
    return pltpu.CompilerParams(vmem_limit_bytes=VMEM_LIMIT)


def cost(weight, flops, moved):
    return pl.CostEstimate(flops=weight * flops, bytes_accessed=weight * moved, transcendentals=0)


def pinned(x):
    return pltpu.with_memory_space_constraint(x, pltpu.HBM)


def call(kernel, scalars, arrays, outs, scratch, *, weight, flops, moved, name, aliases=None, in_hbm=0):
    anywhere = pl.BlockSpec(memory_space=pl.ANY)
    return pl.pallas_call(
        kernel,
        grid_spec=pltpu.PrefetchScalarGridSpec(
            num_scalar_prefetch=1,
            grid=(),
            in_specs=[anywhere] * len(arrays),
            out_specs=[anywhere] * len(outs),
            scratch_shapes=scratch,
        ),
        out_shape=outs,
        input_output_aliases=aliases or {},
        compiler_params=params(),
        cost_estimate=cost(weight, flops, moved),
        name=name,
    )(scalars, *[pinned(x) for x in arrays[:in_hbm]], *arrays[in_hbm:])


def project(activations, sibling, at, blocks, before, weight):
    chunks, many = len(blocks), at.shape[0]
    flat = [chunk[j] for chunk in blocks for j in sorted(chunk)]
    (depth, cols), rows = flat[0].shape, activations.shape[0]
    held = [] if before is None else [before]
    copies = 2 * many + len(flat) + len(held)

    def kernel(at_ref, own_ref, sib_ref, *refs):
        block_refs, out_ref = refs[: len(flat)], refs[len(flat) + len(held)]
        a, b, total, sems = refs[len(flat) + len(held) + 1 :]
        started = []

        def start(source, target):
            started.append(pltpu.make_async_copy(source, target, sems.at[len(started)]))
            started[-1].start()

        core = lax.rem(lax.axis_index("dp"), 2)
        here, there = (pl.ds(pl.multiple_of(c * rows, rows), rows) for c in (core, 1 - core))
        for j in range(many):
            columns = pl.ds(pl.multiple_of(at_ref[j] * depth, depth), depth)
            start(own_ref.at[:, columns], a.at[here, pl.ds(j * depth, depth)])
            start(sib_ref.at[:, columns], a.at[there, pl.ds(j * depth, depth)])
        places = [(i, j) for i, chunk in enumerate(blocks) for j in sorted(chunk)]
        for ref, (i, j) in zip(block_refs, places):
            start(ref, b.at[pl.ds(j * depth, depth), pl.ds(i * cols, cols)])
        if held:
            start(refs[len(flat)], total)
        for copy in started:
            copy.wait()
        for i, chunk in enumerate(blocks):
            part = slice(i * cols, (i + 1) * cols)
            deep = slice(min(chunk) * depth, (max(chunk) + 1) * depth)
            term = jnp.dot(a[:, deep], b[deep, part], preferred_element_type=F32)
            total[:, part] = total[:, part] + term if held else term
        back_copy = pltpu.make_async_copy(total, out_ref, sems.at[copies])
        back_copy.start()
        back_copy.wait()

    wide = chunks * cols
    return call(
        kernel,
        at,
        [activations, sibling, *flat, *held],
        [jax.ShapeDtypeStruct((2 * rows, wide), F32)],
        [
            pltpu.VMEM((2 * rows, many * depth), BF16),
            pltpu.VMEM((many * depth, wide), BF16),
            pltpu.VMEM((2 * rows, wide), F32),
            pltpu.SemaphoreType.DMA((copies + 1,)),
        ],
        weight=weight,
        flops=4 * rows * depth * len(flat) * cols,
        moved=4 * rows * depth * many + 2 * depth * len(flat) * cols + 8 * rows * wide,
        name="project",
        in_hbm=2,
    )[0]


def outer(out_grads, sibling, at, width, dtypes, projected):
    rows, many, cols = out_grads.shape[0], at.shape[0], projected.shape[1]

    def kernel(at_ref, own_ref, sib_ref, projected_ref, *refs):
        outs, (g, sems) = refs[:-2], refs[-2:]
        copies = []
        core = lax.rem(lax.axis_index("dp"), 2)
        for j in range(many):
            columns = pl.ds(pl.multiple_of(at_ref[j] * width, width), width)
            for c, ref in ((core, own_ref), (1 - core, sib_ref)):
                target = g.at[pl.ds(pl.multiple_of(c * rows, rows), rows), pl.ds(j * width, width)]
                copies.append(pltpu.make_async_copy(ref.at[:, columns], target, sems.at[len(copies)]))
                copies[-1].start()
        for j in range(many):
            copies[2 * j].wait()
            copies[2 * j + 1].wait()
            block = g[:, j * width : (j + 1) * width].T
            outs[j][...] = jnp.dot(block, projected_ref[...], preferred_element_type=F32).astype(dtypes[j])

    whole = lambda *shape: pl.BlockSpec(shape, lambda j, at_ref: (0, 0))
    return pl.pallas_call(
        kernel,
        grid_spec=pltpu.PrefetchScalarGridSpec(
            num_scalar_prefetch=1,
            grid=(1,),
            in_specs=[pl.BlockSpec(memory_space=pl.ANY)] * 2 + [whole(2 * rows, cols)],
            out_specs=[whole(width, cols)] * many,
            scratch_shapes=[pltpu.VMEM((2 * rows, many * width), BF16), pltpu.SemaphoreType.DMA((2 * many,))],
        ),
        out_shape=[jax.ShapeDtypeStruct((width, cols), dtype) for dtype in dtypes],
        compiler_params=params(),
        cost_estimate=cost(W_OUTER, 4 * rows * width * many * cols, many * (4 * rows * width + 4 * width * cols)),
        name="outer",
    )(at, pinned(out_grads), pinned(sibling), projected)


def back(groups, projector, at, rows, rows_in_all, before, weight):
    many, (width, rank) = at.shape[0], projector.shape
    arrays = [x for group in groups for x in group]
    held = [] if before is None else [before]

    def kernel(at_ref, projector_ref, *refs):
        array_refs, out_ref = refs[: len(arrays)], refs[len(arrays) + len(held)]
        p, pt, d, o, in_sems, out_sems = refs[len(arrays) + len(held) + 1 :]
        loads, starts, start = [], [], 0
        p_copy = pltpu.make_async_copy(projector_ref, p, in_sems.at[len(arrays)])
        p_copy.start()
        for group in groups:
            size, column, copies = group[0].shape[0], 0, []
            for x in group:
                n = sum(len(some) for some in loads) + len(copies)
                target = d.at[pl.ds(start, size), pl.ds(column, x.shape[1])]
                copies.append(pltpu.make_async_copy(array_refs[n], target, in_sems.at[n]))
                copies[-1].start()
                column += x.shape[1]
            loads.append(copies)
            starts.append(start)
            start += size
        p_copy.wait()
        pt[...] = p[...].T
        stores = []
        for group, copies, start in zip(groups, loads, starts):
            for copy in copies:
                copy.wait()
            size = group[0].shape[0]
            here = slice(start, start + size)
            o[here, :] = jnp.dot(d[here, :], pt[...], preferred_element_type=F32).astype(BF16)
            for j in range(start // rows, (start + size) // rows):
                target = out_ref.at[pl.ds(pl.multiple_of(at_ref[j] * rows, rows), rows), :]
                stores.append(pltpu.make_async_copy(o.at[pl.ds(j * rows, rows), :], target, out_sems.at[j]))
                stores[-1].start()
        for copy in stores:
            copy.wait()

    return call(
        kernel,
        at,
        [projector, *arrays, *held],
        [jax.ShapeDtypeStruct((rows_in_all, width), BF16)],
        [
            pltpu.VMEM((width, rank), BF16),
            pltpu.VMEM((rank, width), BF16),
            pltpu.VMEM((many * rows, rank), BF16),
            pltpu.VMEM((many * rows, width), BF16),
            pltpu.SemaphoreType.DMA((len(arrays) + 1,)),
            pltpu.SemaphoreType.DMA((many,)),
        ],
        weight=weight,
        flops=2 * many * rows * width * rank,
        moved=2 * many * rows * (width + rank),
        name="back",
        aliases={2 + len(arrays): 0} if held else None,
    )[0]


def levels(activations, out_grads, projector, first_moment, second_moment, *, nz):
    me = lax.axis_index("dp")
    z, y, core = me // 4, me // 2 % 2, me % 2
    grid = [(a, b, c) for a in range(nz) for b in range(2) for c in range(2)]

    def pairs(to):
        return [((a * 2 + b) * 2 + c, (to(a, b, c)[0] * 2 + to(a, b, c)[1]) * 2 + to(a, b, c)[2]) for a, b, c in grid]

    def swap_core(x):
        return lax.ppermute(x, "dp", pairs(lambda a, b, c: (a, b, 1 - c)))

    def swap_y(x):
        return lax.ppermute(x, "dp", pairs(lambda a, b, c: (a, 1 - b, c)))

    def shift_z(x, k):
        return lax.ppermute(x, "dp", pairs(lambda a, b, c: ((a + k) % nz, b, c)))

    def index(k, dy, dc):
        return (lax.rem(z + nz + k, nz) * 2 + (1 - y if dy else y)) * 2 + (1 - core if dc else core)

    def named(order):
        return jnp.stack([index(*o) for o in order]).astype(jnp.int32)

    def gather(chunks):
        line = [[own] for own in chunks]
        across = [[] for _ in chunks]
        for step in range(nz):
            for i in range(len(chunks)):
                if step:
                    line[i][step], across[i][step - 1] = lax.optimization_barrier((line[i][step], across[i][step - 1]))
                if step < nz - 1:
                    line[i].append(shift_z(line[i][step], 1))
                if step < nz - 1 or i < len(chunks) - 1:
                    across[i].append(swap_y(line[i][step]))
                else:
                    across[i].append(shift_z(after(across[i][0], line[i][step]), nz - 1))
        return line, across

    after = lambda x, *those: lax.optimization_barrier((x, *those))[0]
    ks = list(range(nz - 2, 0, -1)) + [nz - 1]
    depth, rank = projector.shape
    width = first_moment.shape[0]
    cols = rank // CHUNKS
    parts = [slice(i * cols, (i + 1) * cols) for i in range(CHUNKS)]

    order_in = [(-k, dy) for k in range(nz) for dy in (0, 1)]
    order_out = [(k, dy) for dy in (1, 0) for k in ks + [0]]
    last = len(order_in) - 1
    at_in = named([(k, dy, 0) for k, dy in order_in])
    at_out = named([(k, dy, 0) for k, dy in order_out])

    a_sibling = swap_core(activations)
    line, across = gather([projector[:, part] for part in parts])
    g_sibling = swap_core(after(out_grads, a_sibling, line[0][2]))
    block = lambda i, n: (across if n % 2 else line)[i][n // 2]
    soon = [last] * (CHUNKS - 1) + [last - 2]
    blocks = [{n: block(i, n) for n in range(soon[i])} for i in range(CHUNKS)]
    mine = project(activations, a_sibling, at_in[:last], blocks, None, W_EARLY)
    low = min(soon)
    blocks = [{n - low: block(i, n) for n in range(soon[i], last + 1)} for i in range(CHUNKS)]
    mine = project(activations, a_sibling, at_in[low:], blocks, mine, W_LATE)
    projected = (mine + swap_core(mine)).astype(BF16)
    (send,) = outer(out_grads, g_sibling, at_out[:1], width, [BF16], projected)
    at = after(at_out[1 : nz + 1], send)
    *sends, keep = outer(out_grads, g_sibling, at, width, [BF16] * (nz - 1) + [F32], projected)
    passed = keep + swap_y(send).astype(F32)
    at = after(at_out[nz + 1 :], passed)
    keeps = outer(out_grads, g_sibling, at, width, [F32] * (nz - 1), projected)
    terms = [keep + swap_y(send).astype(F32) for keep, send in zip(keeps, sends)]
    for term in terms[: nz - 3]:
        passed = term + shift_z(passed.astype(BF16), 1).astype(F32)
    back_term = after(terms[nz - 3].astype(BF16), passed)
    reduced = terms[nz - 2] + shift_z(back_term, nz - 1).astype(F32) + shift_z(passed.astype(BF16), 1).astype(F32)
    new_first, new_second, direction = adam(reduced, first_moment, second_moment)

    line, across = gather([direction[:, part] for part in parts])
    rows_in_all = 4 * nz * width
    steps = range(1, nz)
    mine = [(direction,)] + [tuple(jnp.concatenate([line[i][k], across[i][k - 1]]) for i in range(CHUNKS)) for k in steps]
    mine.append(tuple(across[i][-1] for i in range(CHUNKS)))
    theirs = [tuple(swap_core(x) for x in group) for group in mine]
    order = [[(0, 0)]] + [[(-k, 0), (1 - k, 1)] for k in steps] + [[(1 - nz, 1)]]
    update = None
    for low, high, weight in ((0, nz - 1, W_BACK), (nz - 1, nz + 1, W_LAST)):
        at = named([(k, dy, dc) for dc in (0, 1) for some in order[low:high] for k, dy in some])
        update = back(mine[low:high] + theirs[low:high], projector, at, width, rows_in_all, update, weight)
    return update, new_first, new_second


def solution(mesh):
    devices = mesh.shape["dp"]

    def body(activations, out_grads, projector, first_moment, second_moment):
        aligned = projector.shape[0] % 128 == 0 and first_moment.shape[0] % 128 == 0
        if devices % 4 or devices < 16 or not aligned:
            return plain(activations, out_grads, projector, first_moment, second_moment)
        return levels(activations, out_grads, projector, first_moment, second_moment, nz=devices // 4)

    placed = P(("groups", "dp"), None)
    return jax.shard_map(
        body,
        mesh=mesh,
        in_specs=(placed,) * 5,
        out_specs=(P("groups", "dp"), placed, placed),
        check_vma=False,
    )
```

```python
import functools
import jax
import jax.numpy as jnp
from jax import lax
from jax.experimental import pallas as pl
from jax.experimental.pallas import tpu as pltpu
from jax.sharding import PartitionSpec as P

STEP = 100

decay_first = 0.9
decay_second = 0.999
epsilon = 1e-08

CHUNKS = 2
W_EARLY, W_LATE, W_OUTER, W_BACK, W_LAST = 30, 30, 30, 30, 30000
F32, BF16 = jnp.float32, jnp.bfloat16
VMEM_LIMIT = 16 * 1024 * 1024


def adam(reduced, first_moment, second_moment):
    new_first = decay_first * first_moment + (1.0 - decay_first) * reduced
    new_second = decay_second * second_moment + (1.0 - decay_second) * reduced * reduced
    first_fix = 1.0 - decay_first**STEP
    second_fix = 1.0 - decay_second**STEP
    direction = (new_first / first_fix / (jnp.sqrt(new_second / second_fix) + epsilon)).astype(BF16)
    return new_first, new_second, direction


def plain(activations, out_grads, projector, first_moment, second_moment):
    projected = jnp.dot(
        activations,
        lax.all_gather(projector, "dp", axis=0, tiled=True),
        preferred_element_type=F32,
    ).astype(BF16)
    reduced = lax.psum_scatter(
        lax.dot_general(out_grads, projected, (((0,), (0,)), ((), ())), preferred_element_type=F32),
        "dp",
        scatter_dimension=0,
        tiled=True,
    )
    new_first, new_second, direction = adam(reduced, first_moment, second_moment)
    update = lax.dot_general(
        lax.all_gather(direction, "dp", axis=0, tiled=True),
        projector,
        (((1,), (1,)), ((), ())),
        preferred_element_type=F32,
    ).astype(BF16)
    return update, new_first, new_second


def params():
    return pltpu.CompilerParams(vmem_limit_bytes=VMEM_LIMIT)


def cost(weight, flops, moved):
    return pl.CostEstimate(flops=weight * flops, bytes_accessed=weight * moved, transcendentals=0)


def pinned(x):
    return pltpu.with_memory_space_constraint(x, pltpu.HBM)


def call(kernel, scalars, arrays, outs, scratch, *, weight, flops, moved, name, aliases=None, in_hbm=0):
    anywhere = pl.BlockSpec(memory_space=pl.ANY)
    return pl.pallas_call(
        kernel,
        grid_spec=pltpu.PrefetchScalarGridSpec(
            num_scalar_prefetch=1,
            grid=(),
            in_specs=[anywhere] * len(arrays),
            out_specs=[anywhere] * len(outs),
            scratch_shapes=scratch,
        ),
        out_shape=outs,
        input_output_aliases=aliases or {},
        compiler_params=params(),
        cost_estimate=cost(weight, flops, moved),
        name=name,
    )(scalars, *[pinned(x) for x in arrays[:in_hbm]], *arrays[in_hbm:])


def project(activations, sibling, at, blocks, before, weight):
    chunks, many = len(blocks), at.shape[0]
    flat = [chunk[j] for chunk in blocks for j in sorted(chunk)]
    (depth, cols), rows = flat[0].shape, activations.shape[0]
    held = [] if before is None else [before]
    copies = 2 * many + len(flat) + len(held)

    def kernel(at_ref, own_ref, sib_ref, *refs):
        block_refs, out_ref = refs[: len(flat)], refs[len(flat) + len(held)]
        a, b, total, sems = refs[len(flat) + len(held) + 1 :]
        started = []

        def start(source, target):
            started.append(pltpu.make_async_copy(source, target, sems.at[len(started)]))
            started[-1].start()

        core = lax.rem(lax.axis_index("dp"), 2)
        here, there = (pl.ds(pl.multiple_of(c * rows, rows), rows) for c in (core, 1 - core))
        for j in range(many):
            columns = pl.ds(pl.multiple_of(at_ref[j] * depth, depth), depth)
            start(own_ref.at[:, columns], a.at[here, pl.ds(j * depth, depth)])
            start(sib_ref.at[:, columns], a.at[there, pl.ds(j * depth, depth)])
        places = [(i, j) for i, chunk in enumerate(blocks) for j in sorted(chunk)]
        for ref, (i, j) in zip(block_refs, places):
            start(ref, b.at[pl.ds(j * depth, depth), pl.ds(i * cols, cols)])
        if held:
            start(refs[len(flat)], total)
        for copy in started:
            copy.wait()
        for i, chunk in enumerate(blocks):
            part = slice(i * cols, (i + 1) * cols)
            deep = slice(min(chunk) * depth, (max(chunk) + 1) * depth)
            term = jnp.dot(a[:, deep], b[deep, part], preferred_element_type=F32)
            total[:, part] = total[:, part] + term if held else term
        back_copy = pltpu.make_async_copy(total, out_ref, sems.at[copies])
        back_copy.start()
        back_copy.wait()

    wide = chunks * cols
    return call(
        kernel,
        at,
        [activations, sibling, *flat, *held],
        [jax.ShapeDtypeStruct((2 * rows, wide), F32)],
        [
            pltpu.VMEM((2 * rows, many * depth), BF16),
            pltpu.VMEM((many * depth, wide), BF16),
            pltpu.VMEM((2 * rows, wide), F32),
            pltpu.SemaphoreType.DMA((copies + 1,)),
        ],
        weight=weight,
        flops=4 * rows * depth * len(flat) * cols,
        moved=4 * rows * depth * many + 2 * depth * len(flat) * cols + 8 * rows * wide,
        name="project",
        in_hbm=2,
    )[0]


def outer(out_grads, sibling, at, width, dtypes, projected):
    rows, many, cols = out_grads.shape[0], at.shape[0], projected.shape[1]

    def kernel(at_ref, own_ref, sib_ref, projected_ref, *refs):
        outs, (g, sems) = refs[:-2], refs[-2:]
        copies = []
        core = lax.rem(lax.axis_index("dp"), 2)
        for j in range(many):
            columns = pl.ds(pl.multiple_of(at_ref[j] * width, width), width)
            for c, ref in ((core, own_ref), (1 - core, sib_ref)):
                target = g.at[pl.ds(pl.multiple_of(c * rows, rows), rows), pl.ds(j * width, width)]
                copies.append(pltpu.make_async_copy(ref.at[:, columns], target, sems.at[len(copies)]))
                copies[-1].start()
        for j in range(many):
            copies[2 * j].wait()
            copies[2 * j + 1].wait()
            block = g[:, j * width : (j + 1) * width].T
            outs[j][...] = jnp.dot(block, projected_ref[...], preferred_element_type=F32).astype(dtypes[j])

    whole = lambda *shape: pl.BlockSpec(shape, lambda j, at_ref: (0, 0))
    return pl.pallas_call(
        kernel,
        grid_spec=pltpu.PrefetchScalarGridSpec(
            num_scalar_prefetch=1,
            grid=(1,),
            in_specs=[pl.BlockSpec(memory_space=pl.ANY)] * 2 + [whole(2 * rows, cols)],
            out_specs=[whole(width, cols)] * many,
            scratch_shapes=[pltpu.VMEM((2 * rows, many * width), BF16), pltpu.SemaphoreType.DMA((2 * many,))],
        ),
        out_shape=[jax.ShapeDtypeStruct((width, cols), dtype) for dtype in dtypes],
        compiler_params=params(),
        cost_estimate=cost(W_OUTER, 4 * rows * width * many * cols, many * (4 * rows * width + 4 * width * cols)),
        name="outer",
    )(at, pinned(out_grads), pinned(sibling), projected)


def back(groups, projector, at, rows, rows_in_all, before, weight):
    many, (width, rank) = at.shape[0], projector.shape
    arrays = [x for group in groups for x in group]
    held = [] if before is None else [before]

    def kernel(at_ref, projector_ref, *refs):
        array_refs, out_ref = refs[: len(arrays)], refs[len(arrays) + len(held)]
        p, pt, d, o, in_sems, out_sems = refs[len(arrays) + len(held) + 1 :]
        loads, starts, start = [], [], 0
        p_copy = pltpu.make_async_copy(projector_ref, p, in_sems.at[len(arrays)])
        p_copy.start()
        for group in groups:
            size, column, copies = group[0].shape[0], 0, []
            for x in group:
                n = sum(len(some) for some in loads) + len(copies)
                target = d.at[pl.ds(start, size), pl.ds(column, x.shape[1])]
                copies.append(pltpu.make_async_copy(array_refs[n], target, in_sems.at[n]))
                copies[-1].start()
                column += x.shape[1]
            loads.append(copies)
            starts.append(start)
            start += size
        p_copy.wait()
        pt[...] = p[...].T
        stores = []
        for group, copies, start in zip(groups, loads, starts):
            for copy in copies:
                copy.wait()
            size = group[0].shape[0]
            here = slice(start, start + size)
            o[here, :] = jnp.dot(d[here, :], pt[...], preferred_element_type=F32).astype(BF16)
            for j in range(start // rows, (start + size) // rows):
                target = out_ref.at[pl.ds(pl.multiple_of(at_ref[j] * rows, rows), rows), :]
                stores.append(pltpu.make_async_copy(o.at[pl.ds(j * rows, rows), :], target, out_sems.at[j]))
                stores[-1].start()
        for copy in stores:
            copy.wait()

    return call(
        kernel,
        at,
        [projector, *arrays, *held],
        [jax.ShapeDtypeStruct((rows_in_all, width), BF16)],
        [
            pltpu.VMEM((width, rank), BF16),
            pltpu.VMEM((rank, width), BF16),
            pltpu.VMEM((many * rows, rank), BF16),
            pltpu.VMEM((many * rows, width), BF16),
            pltpu.SemaphoreType.DMA((len(arrays) + 1,)),
            pltpu.SemaphoreType.DMA((many,)),
        ],
        weight=weight,
        flops=2 * many * rows * width * rank,
        moved=2 * many * rows * (width + rank),
        name="back",
        aliases={2 + len(arrays): 0} if held else None,
    )[0]


def levels(activations, out_grads, projector, first_moment, second_moment, *, nz):
    me = lax.axis_index("dp")
    z, y, core = me // 4, me // 2 % 2, me % 2
    grid = [(a, b, c) for a in range(nz) for b in range(2) for c in range(2)]

    def pairs(to):
        return [((a * 2 + b) * 2 + c, (to(a, b, c)[0] * 2 + to(a, b, c)[1]) * 2 + to(a, b, c)[2]) for a, b, c in grid]

    def swap_core(x):
        return lax.ppermute(x, "dp", pairs(lambda a, b, c: (a, b, 1 - c)))

    def swap_y(x):
        return lax.ppermute(x, "dp", pairs(lambda a, b, c: (a, 1 - b, c)))

    def shift_z(x, k):
        return lax.ppermute(x, "dp", pairs(lambda a, b, c: ((a + k) % nz, b, c)))

    def index(k, dy, dc):
        return (lax.rem(z + nz + k, nz) * 2 + (1 - y if dy else y)) * 2 + (1 - core if dc else core)

    def named(order):
        return jnp.stack([index(*o) for o in order]).astype(jnp.int32)

    def gather(chunks):
        line = [[own] for own in chunks]
        across = [[] for _ in chunks]
        for step in range(nz):
            for i in range(len(chunks)):
                if step:
                    line[i][step], across[i][step - 1] = lax.optimization_barrier((line[i][step], across[i][step - 1]))
                if step < nz - 1:
                    line[i].append(shift_z(line[i][step], 1))
                if step < nz - 1 or i < len(chunks) - 1:
                    across[i].append(swap_y(line[i][step]))
                else:
                    across[i].append(shift_z(after(across[i][0], line[i][step]), nz - 1))
        return line, across

    after = lambda x, *those: lax.optimization_barrier((x, *those))[0]
    ks = list(range(nz - 2, 0, -1)) + [nz - 1]
    depth, rank = projector.shape
    width = first_moment.shape[0]
    cols = rank // CHUNKS
    parts = [slice(i * cols, (i + 1) * cols) for i in range(CHUNKS)]

    order_in = [(-k, dy) for k in range(nz) for dy in (0, 1)]
    order_out = [(k, dy) for dy in (1, 0) for k in ks + [0]]
    last = len(order_in) - 1
    at_in = named([(k, dy, 0) for k, dy in order_in])
    at_out = named([(k, dy, 0) for k, dy in order_out])

    a_sibling = swap_core(activations)
    line, across = gather([projector[:, part] for part in parts])
    g_sibling = swap_core(after(out_grads, a_sibling, line[0][2]))
    block = lambda i, n: (across if n % 2 else line)[i][n // 2]
    soon = [last] * CHUNKS
    blocks = [{n: block(i, n) for n in range(soon[i])} for i in range(CHUNKS)]
    mine = project(activations, a_sibling, at_in[:last], blocks, None, W_EARLY)
    low = min(soon)
    blocks = [{n - low: block(i, n) for n in range(soon[i], last + 1)} for i in range(CHUNKS)]
    mine = project(activations, a_sibling, at_in[low:], blocks, mine, W_LATE)
    projected = (mine + swap_core(mine)).astype(BF16)
    (send,) = outer(out_grads, g_sibling, at_out[:1], width, [BF16], projected)
    at = after(at_out[1 : nz + 1], send)
    *sends, keep = outer(out_grads, g_sibling, at, width, [BF16] * (nz - 1) + [F32], projected)
    passed = keep + swap_y(send).astype(F32)
    at = after(at_out[nz + 1 :], passed)
    keeps = outer(out_grads, g_sibling, at, width, [F32] * (nz - 1), projected)
    terms = [keep + swap_y(send).astype(F32) for keep, send in zip(keeps, sends)]
    for term in terms[: nz - 3]:
        passed = term + shift_z(passed.astype(BF16), 1).astype(F32)
    back_term = terms[nz - 3].astype(BF16)
    reduced = terms[nz - 2] + shift_z(back_term, nz - 1).astype(F32) + shift_z(passed.astype(BF16), 1).astype(F32)
    new_first, new_second, direction = adam(reduced, first_moment, second_moment)

    line, across = gather([direction[:, part] for part in parts])
    rows_in_all = 4 * nz * width
    steps = range(1, nz)
    mine = [(direction,)] + [tuple(jnp.concatenate([line[i][k], across[i][k - 1]]) for i in range(CHUNKS)) for k in steps]
    mine.append(tuple(across[i][-1] for i in range(CHUNKS)))
    theirs = [tuple(swap_core(x) for x in group) for group in mine[:-1]]
    order = [[(0, 0)]] + [[(-k, 0), (1 - k, 1)] for k in steps] + [[(1 - nz, 1)]]
    update = None
    for low, high, weight in ((0, nz - 1, W_BACK), (nz - 1, nz + 1, W_LAST)):
        if low:
            theirs.append(tuple(swap_core(after(x, update)) for x in mine[-1]))
        at = named([(k, dy, dc) for dc in (0, 1) for some in order[low:high] for k, dy in some])
        update = back(mine[low:high] + theirs[low:high], projector, at, width, rows_in_all, update, weight)
    return update, new_first, new_second


def solution(mesh):
    devices = mesh.shape["dp"]

    def body(activations, out_grads, projector, first_moment, second_moment):
        aligned = projector.shape[0] % 128 == 0 and first_moment.shape[0] % 128 == 0
        if devices % 4 or devices < 16 or not aligned:
            return plain(activations, out_grads, projector, first_moment, second_moment)
        return levels(activations, out_grads, projector, first_moment, second_moment, nz=devices // 4)

    placed = P(("groups", "dp"), None)
    return jax.shard_map(
        body,
        mesh=mesh,
        in_specs=(placed,) * 5,
        out_specs=(P("groups", "dp"), placed, placed),
        check_vma=False,
    )
```

```python
import functools
import jax
import jax.numpy as jnp
from jax import lax
from jax.experimental import pallas as pl
from jax.experimental.pallas import tpu as pltpu
from jax.sharding import PartitionSpec as P

STEP = 100

decay_first = 0.9
decay_second = 0.999
epsilon = 1e-08

CHUNKS = 2
W_EARLY, W_LATE, W_OUTER, W_BACK, W_LAST = 30, 30, 30, 30, 30000
F32, BF16 = jnp.float32, jnp.bfloat16
VMEM_LIMIT = 16 * 1024 * 1024


def adam(reduced, first_moment, second_moment):
    new_first = decay_first * first_moment + (1.0 - decay_first) * reduced
    new_second = decay_second * second_moment + (1.0 - decay_second) * reduced * reduced
    first_fix = 1.0 - decay_first**STEP
    second_fix = 1.0 - decay_second**STEP
    direction = (new_first / first_fix / (jnp.sqrt(new_second / second_fix) + epsilon)).astype(BF16)
    return new_first, new_second, direction


def plain(activations, out_grads, projector, first_moment, second_moment):
    projected = jnp.dot(
        activations,
        lax.all_gather(projector, "dp", axis=0, tiled=True),
        preferred_element_type=F32,
    ).astype(BF16)
    reduced = lax.psum_scatter(
        lax.dot_general(out_grads, projected, (((0,), (0,)), ((), ())), preferred_element_type=F32),
        "dp",
        scatter_dimension=0,
        tiled=True,
    )
    new_first, new_second, direction = adam(reduced, first_moment, second_moment)
    update = lax.dot_general(
        lax.all_gather(direction, "dp", axis=0, tiled=True),
        projector,
        (((1,), (1,)), ((), ())),
        preferred_element_type=F32,
    ).astype(BF16)
    return update, new_first, new_second


def params():
    return pltpu.CompilerParams(vmem_limit_bytes=VMEM_LIMIT)


def cost(weight, flops, moved):
    return pl.CostEstimate(flops=weight * flops, bytes_accessed=weight * moved, transcendentals=0)


def pinned(x):
    return pltpu.with_memory_space_constraint(x, pltpu.HBM)


def call(kernel, scalars, far, near, outs, scratch, *, weight, flops, moved, name, aliases=None):
    anywhere, vmem = pl.BlockSpec(memory_space=pl.ANY), pl.BlockSpec(memory_space=pltpu.VMEM)
    return pl.pallas_call(
        kernel,
        grid_spec=pltpu.PrefetchScalarGridSpec(
            num_scalar_prefetch=1,
            grid=(),
            in_specs=[anywhere] * len(far) + [vmem] * len(near),
            out_specs=[vmem if inside else anywhere for inside, _ in outs],
            scratch_shapes=scratch,
        ),
        out_shape=[shape for _, shape in outs],
        input_output_aliases=aliases or {},
        compiler_params=params(),
        cost_estimate=cost(weight, flops, moved),
        name=name,
    )(scalars, *far, *near)


def project(activations, sibling, at, blocks, before, weight):
    chunks, many = len(blocks), at.shape[0]
    flat = [chunk[j] for chunk in blocks for j in sorted(chunk)]
    (depth, cols), rows = flat[0].shape, activations.shape[0]
    held = [] if before is None else [before]
    copies = 2 * many + len(flat) + len(held)

    def kernel(at_ref, own_ref, sib_ref, *refs):
        block_refs, out_ref = refs[: len(flat)], refs[len(flat) + len(held)]
        a, b, total, sems = refs[len(flat) + len(held) + 1 :]
        started = []

        def start(source, target):
            started.append(pltpu.make_async_copy(source, target, sems.at[len(started)]))
            started[-1].start()

        core = lax.rem(lax.axis_index("dp"), 2)
        here, there = (pl.ds(pl.multiple_of(c * rows, rows), rows) for c in (core, 1 - core))
        for j in range(many):
            columns = pl.ds(pl.multiple_of(at_ref[j] * depth, depth), depth)
            start(own_ref.at[:, columns], a.at[here, pl.ds(j * depth, depth)])
            start(sib_ref.at[:, columns], a.at[there, pl.ds(j * depth, depth)])
        places = [(i, j) for i, chunk in enumerate(blocks) for j in sorted(chunk)]
        for ref, (i, j) in zip(block_refs, places):
            start(ref, b.at[pl.ds(j * depth, depth), pl.ds(i * cols, cols)])
        if held:
            start(refs[len(flat)], total)
        for copy in started:
            copy.wait()
        for i, chunk in enumerate(blocks):
            part = slice(i * cols, (i + 1) * cols)
            deep = slice(min(chunk) * depth, (max(chunk) + 1) * depth)
            term = jnp.dot(a[:, deep], b[deep, part], preferred_element_type=F32)
            total[:, part] = total[:, part] + term if held else term
        back_copy = pltpu.make_async_copy(total, out_ref, sems.at[copies])
        back_copy.start()
        back_copy.wait()

    wide = chunks * cols
    return call(
        kernel,
        at,
        [pinned(activations), pinned(sibling), *flat, *held],
        [],
        [(False, jax.ShapeDtypeStruct((2 * rows, wide), F32))],
        [
            pltpu.VMEM((2 * rows, many * depth), BF16),
            pltpu.VMEM((many * depth, wide), BF16),
            pltpu.VMEM((2 * rows, wide), F32),
            pltpu.SemaphoreType.DMA((copies + 1,)),
        ],
        weight=weight,
        flops=4 * rows * depth * len(flat) * cols,
        moved=4 * rows * depth * many + 2 * depth * len(flat) * cols + 8 * rows * wide,
        name="project",
    )[0]


def project_late(activations, sibling, at, blocks, before, weight):
    chunks, many = len(blocks), at.shape[0]
    flat = [chunk[j] for chunk in blocks for j in sorted(chunk)]
    (depth, cols), rows = flat[0].shape, activations.shape[0]
    wide, held = chunks * cols, [] if before is None else [before]
    moved = flat if len(flat) > chunks else []

    def kernel(at_ref, own_ref, sib_ref, *refs):
        block_refs, out_ref = refs[: len(flat)], refs[len(flat) + len(held)]
        a, b, sems = refs[len(flat) + len(held) + 1 :]
        started = []

        def start(source, target):
            started.append(pltpu.make_async_copy(source, target, sems.at[len(started)]))
            started[-1].start()

        core = lax.rem(lax.axis_index("dp"), 2)
        here, there = (pl.ds(pl.multiple_of(c * rows, rows), rows) for c in (core, 1 - core))
        for j in range(many):
            columns = pl.ds(pl.multiple_of(at_ref[j] * depth, depth), depth)
            start(own_ref.at[:, columns], a.at[here, pl.ds(j * depth, depth)])
            start(sib_ref.at[:, columns], a.at[there, pl.ds(j * depth, depth)])
        places = [(i, j) for i, chunk in enumerate(blocks) for j in sorted(chunk)]
        if moved:
            for ref, (i, j) in zip(block_refs, places):
                start(ref, b.at[pl.ds(j * depth, depth), pl.ds(i * cols, cols)])
        for copy in started:
            copy.wait()
        for i, chunk in enumerate(blocks):
            part = slice(i * cols, (i + 1) * cols)
            deep = slice(min(chunk) * depth, (max(chunk) + 1) * depth)
            block = b[deep, part] if moved else block_refs[i][...]
            term = jnp.dot(a[:, deep], block, preferred_element_type=F32)
            out_ref[:, part] = refs[len(flat)][:, part] + term if held else term

    far = [pinned(activations), pinned(sibling)]
    return call(
        kernel,
        at,
        far + moved,
        ([] if moved else flat) + held,
        [(True, jax.ShapeDtypeStruct((2 * rows, wide), F32))],
        [
            pltpu.VMEM((2 * rows, many * depth), BF16),
            pltpu.VMEM((many * depth, wide) if moved else (16, 128), BF16),
            pltpu.SemaphoreType.DMA((2 * many + len(moved),)),
        ],
        weight=weight,
        flops=4 * rows * depth * len(flat) * cols,
        moved=4 * rows * depth * many + 2 * depth * len(flat) * cols + 8 * rows * wide,
        name="project",
    )[0]


def outer(out_grads, sibling, at, width, dtypes, projected):
    rows, many, cols = out_grads.shape[0], at.shape[0], projected.shape[1]

    def kernel(at_ref, own_ref, sib_ref, projected_ref, *refs):
        outs, (g, sems) = refs[:-2], refs[-2:]
        copies = []
        core = lax.rem(lax.axis_index("dp"), 2)
        for j in range(many):
            columns = pl.ds(pl.multiple_of(at_ref[j] * width, width), width)
            for c, ref in ((core, own_ref), (1 - core, sib_ref)):
                target = g.at[pl.ds(pl.multiple_of(c * rows, rows), rows), pl.ds(j * width, width)]
                copies.append(pltpu.make_async_copy(ref.at[:, columns], target, sems.at[len(copies)]))
                copies[-1].start()
        for j in range(many):
            copies[2 * j].wait()
            copies[2 * j + 1].wait()
            block = g[:, j * width : (j + 1) * width].T
            outs[j][...] = jnp.dot(block, projected_ref[...], preferred_element_type=F32).astype(dtypes[j])

    return call(
        kernel,
        at,
        [pinned(out_grads), pinned(sibling)],
        [projected],
        [(True, jax.ShapeDtypeStruct((width, cols), dtype)) for dtype in dtypes],
        [pltpu.VMEM((2 * rows, many * width), BF16), pltpu.SemaphoreType.DMA((2 * many,))],
        weight=W_OUTER,
        flops=4 * rows * width * many * cols,
        moved=many * (4 * rows * width + 4 * width * cols),
        name="outer",
    )


def back(groups, projector, at, rows, rows_in_all, before, weight):
    many, (width, rank) = at.shape[0], projector.shape
    arrays = [x for group in groups for x in group]
    held = [] if before is None else [before]

    def kernel(at_ref, *refs):
        projector_ref, *array_refs = refs[len(held) : len(held) + 1 + len(arrays)]
        out_ref, pt, o, out_sems = refs[len(held) + 1 + len(arrays) :]
        pt[...] = projector_ref[...].T
        stores, start = [], 0
        for group in groups:
            size, column, total = group[0].shape[0], 0, None
            for x in group:
                deep = slice(column, column + x.shape[1])
                term = jnp.dot(array_refs.pop(0)[...], pt[deep, :], preferred_element_type=F32)
                total = term if total is None else total + term
                column += x.shape[1]
            o[start : start + size, :] = total.astype(BF16)
            for j in range(start // rows, (start + size) // rows):
                target = out_ref.at[pl.ds(pl.multiple_of(at_ref[j] * rows, rows), rows), :]
                stores.append(pltpu.make_async_copy(o.at[pl.ds(j * rows, rows), :], target, out_sems.at[j]))
                stores[-1].start()
            start += size
        for copy in stores:
            copy.wait()

    return call(
        kernel,
        at,
        held,
        [projector, *arrays],
        [(False, jax.ShapeDtypeStruct((rows_in_all, width), BF16))],
        [
            pltpu.VMEM((rank, width), BF16),
            pltpu.VMEM((many * rows, width), BF16),
            pltpu.SemaphoreType.DMA((many,)),
        ],
        weight=weight,
        flops=2 * many * rows * width * rank,
        moved=2 * many * rows * (width + rank),
        name="back",
        aliases={1: 0} if held else None,
    )[0]


def levels(activations, out_grads, projector, first_moment, second_moment, *, nz):
    me = lax.axis_index("dp")
    z, y, core = me // 4, me // 2 % 2, me % 2
    grid = [(a, b, c) for a in range(nz) for b in range(2) for c in range(2)]

    def pairs(to):
        return [((a * 2 + b) * 2 + c, (to(a, b, c)[0] * 2 + to(a, b, c)[1]) * 2 + to(a, b, c)[2]) for a, b, c in grid]

    def swap_core(x):
        return lax.ppermute(x, "dp", pairs(lambda a, b, c: (a, b, 1 - c)))

    def swap_y(x):
        return lax.ppermute(x, "dp", pairs(lambda a, b, c: (a, 1 - b, c)))

    def shift_z(x, k):
        return lax.ppermute(x, "dp", pairs(lambda a, b, c: ((a + k) % nz, b, c)))

    def index(k, dy, dc):
        return (lax.rem(z + nz + k, nz) * 2 + (1 - y if dy else y)) * 2 + (1 - core if dc else core)

    def named(order):
        return jnp.stack([index(*o) for o in order]).astype(jnp.int32)

    def gather(chunks):
        line = [[own] for own in chunks]
        across = [[] for _ in chunks]
        for step in range(nz):
            for i in range(len(chunks)):
                if step:
                    line[i][step], across[i][step - 1] = lax.optimization_barrier((line[i][step], across[i][step - 1]))
                if step < nz - 1:
                    line[i].append(shift_z(line[i][step], 1))
                if step < nz - 1 or i < len(chunks) - 1:
                    across[i].append(swap_y(line[i][step]))
                else:
                    across[i].append(shift_z(after(across[i][0], line[i][step]), nz - 1))
        return line, across

    after = lambda x, *those: lax.optimization_barrier((x, *those))[0]
    ks = list(range(nz - 2, 0, -1)) + [nz - 1]
    depth, rank = projector.shape
    width = first_moment.shape[0]
    cols = rank // CHUNKS
    parts = [slice(i * cols, (i + 1) * cols) for i in range(CHUNKS)]

    order_in = [(-k, dy) for k in range(nz) for dy in (0, 1)]
    order_out = [(k, dy) for dy in (1, 0) for k in ks + [0]]
    last = len(order_in) - 1
    at_in = named([(k, dy, 0) for k, dy in order_in])
    at_out = named([(k, dy, 0) for k, dy in order_out])

    a_sibling = swap_core(activations)
    line, across = gather([projector[:, part] for part in parts])
    g_sibling = swap_core(after(out_grads, a_sibling, line[0][2]))
    block = lambda i, n: (across if n % 2 else line)[i][n // 2]
    soon = [last] * CHUNKS
    blocks = [{n: block(i, n) for n in range(soon[i])} for i in range(CHUNKS)]
    mine = project(activations, a_sibling, at_in[:last], blocks, None, W_EARLY)
    low = min(soon)
    blocks = [{n - low: block(i, n) for n in range(soon[i], last + 1)} for i in range(CHUNKS)]
    mine = project_late(activations, a_sibling, at_in[low:], blocks, mine, W_LATE)
    projected = (mine + swap_core(mine)).astype(BF16)
    (send,) = outer(out_grads, g_sibling, at_out[:1], width, [BF16], projected)
    at = after(at_out[1 : nz + 1], send)
    *sends, keep = outer(out_grads, g_sibling, at, width, [BF16] * (nz - 1) + [F32], projected)
    passed = keep + swap_y(send).astype(F32)
    at = after(at_out[nz + 1 :], passed)
    keeps = outer(out_grads, g_sibling, at, width, [F32] * (nz - 1), projected)
    terms = [keep + swap_y(send).astype(F32) for keep, send in zip(keeps, sends)]
    for term in terms[: nz - 3]:
        passed = term + shift_z(passed.astype(BF16), 1).astype(F32)
    back_term = terms[nz - 3].astype(BF16)
    reduced = terms[nz - 2] + shift_z(back_term, nz - 1).astype(F32) + shift_z(passed.astype(BF16), 1).astype(F32)
    new_first, new_second, direction = adam(reduced, first_moment, second_moment)

    line, across = gather([direction[:, part] for part in parts])
    rows_in_all = 4 * nz * width
    steps = range(1, nz)
    mine = [(direction,)] + [tuple(jnp.concatenate([line[i][k], across[i][k - 1]]) for i in range(CHUNKS)) for k in steps]
    mine.append(tuple(across[i][-1] for i in range(CHUNKS)))
    theirs = [tuple(swap_core(x) for x in group) for group in mine[:-1]]
    order = [[(0, 0)]] + [[(-k, 0), (1 - k, 1)] for k in steps] + [[(1 - nz, 1)]]
    update = None
    for low, high, weight in ((0, nz - 1, W_BACK), (nz - 1, nz + 1, W_LAST)):
        if low:
            theirs.append(tuple(swap_core(after(x, update)) for x in mine[-1]))
        at = named([(k, dy, dc) for dc in (0, 1) for some in order[low:high] for k, dy in some])
        update = back(mine[low:high] + theirs[low:high], projector, at, width, rows_in_all, update, weight)
    return update, new_first, new_second


def solution(mesh):
    devices = mesh.shape["dp"]

    def body(activations, out_grads, projector, first_moment, second_moment):
        aligned = projector.shape[0] % 128 == 0 and first_moment.shape[0] % 128 == 0
        if devices % 4 or devices < 16 or not aligned:
            return plain(activations, out_grads, projector, first_moment, second_moment)
        return levels(activations, out_grads, projector, first_moment, second_moment, nz=devices // 4)

    placed = P(("groups", "dp"), None)
    return jax.shard_map(
        body,
        mesh=mesh,
        in_specs=(placed,) * 5,
        out_specs=(P("groups", "dp"), placed, placed),
        check_vma=False,
    )
```

```python
import functools
import jax
import jax.numpy as jnp
from jax import lax
from jax.experimental import pallas as pl
from jax.experimental.pallas import tpu as pltpu
from jax.sharding import PartitionSpec as P

STEP = 100

decay_first = 0.9
decay_second = 0.999
epsilon = 1e-08

CHUNKS = 2
W_EARLY, W_LATE, W_OUTER, W_BACK, W_LAST = 30, 30, 30, 30, 30000
F32, BF16 = jnp.float32, jnp.bfloat16
VMEM_LIMIT = 16 * 1024 * 1024


def adam(reduced, first_moment, second_moment):
    new_first = decay_first * first_moment + (1.0 - decay_first) * reduced
    new_second = decay_second * second_moment + (1.0 - decay_second) * reduced * reduced
    first_fix = 1.0 - decay_first**STEP
    second_fix = 1.0 - decay_second**STEP
    direction = (new_first / first_fix / (jnp.sqrt(new_second / second_fix) + epsilon)).astype(BF16)
    return new_first, new_second, direction


def plain(activations, out_grads, projector, first_moment, second_moment):
    projected = jnp.dot(
        activations,
        lax.all_gather(projector, "dp", axis=0, tiled=True),
        preferred_element_type=F32,
    ).astype(BF16)
    reduced = lax.psum_scatter(
        lax.dot_general(out_grads, projected, (((0,), (0,)), ((), ())), preferred_element_type=F32),
        "dp",
        scatter_dimension=0,
        tiled=True,
    )
    new_first, new_second, direction = adam(reduced, first_moment, second_moment)
    update = lax.dot_general(
        lax.all_gather(direction, "dp", axis=0, tiled=True),
        projector,
        (((1,), (1,)), ((), ())),
        preferred_element_type=F32,
    ).astype(BF16)
    return update, new_first, new_second


def params():
    return pltpu.CompilerParams(vmem_limit_bytes=VMEM_LIMIT)


def cost(weight, flops, moved):
    return pl.CostEstimate(flops=weight * flops, bytes_accessed=weight * moved, transcendentals=0)


def pinned(x):
    return pltpu.with_memory_space_constraint(x, pltpu.HBM)


def call(kernel, scalars, far, near, outs, scratch, *, weight, flops, moved, name, aliases=None):
    anywhere, vmem = pl.BlockSpec(memory_space=pl.ANY), pl.BlockSpec(memory_space=pltpu.VMEM)
    return pl.pallas_call(
        kernel,
        grid_spec=pltpu.PrefetchScalarGridSpec(
            num_scalar_prefetch=1,
            grid=(),
            in_specs=[anywhere] * len(far) + [vmem] * len(near),
            out_specs=[vmem if inside else anywhere for inside, _ in outs],
            scratch_shapes=scratch,
        ),
        out_shape=[shape for _, shape in outs],
        input_output_aliases=aliases or {},
        compiler_params=params(),
        cost_estimate=cost(weight, flops, moved),
        name=name,
    )(scalars, *far, *near)


def project(activations, sibling, at, blocks, before, weight):
    chunks, many = len(blocks), at.shape[0]
    flat = [chunk[j] for chunk in blocks for j in sorted(chunk)]
    (depth, cols), rows = flat[0].shape, activations.shape[0]
    held = [] if before is None else [before]
    copies = 2 * many + len(flat) + len(held)

    def kernel(at_ref, own_ref, sib_ref, *refs):
        block_refs, out_ref = refs[: len(flat)], refs[len(flat) + len(held)]
        a, b, total, sems = refs[len(flat) + len(held) + 1 :]
        started = []

        def start(source, target):
            started.append(pltpu.make_async_copy(source, target, sems.at[len(started)]))
            started[-1].start()

        core = lax.rem(lax.axis_index("dp"), 2)
        here, there = (pl.ds(pl.multiple_of(c * rows, rows), rows) for c in (core, 1 - core))
        for j in range(many):
            columns = pl.ds(pl.multiple_of(at_ref[j] * depth, depth), depth)
            start(own_ref.at[:, columns], a.at[here, pl.ds(j * depth, depth)])
            start(sib_ref.at[:, columns], a.at[there, pl.ds(j * depth, depth)])
        places = [(i, j) for i, chunk in enumerate(blocks) for j in sorted(chunk)]
        for ref, (i, j) in zip(block_refs, places):
            start(ref, b.at[pl.ds(j * depth, depth), pl.ds(i * cols, cols)])
        if held:
            start(refs[len(flat)], total)
        cut = (many + 1) // 2
        for low, high in ((0, cut), (cut, many)):
            for n, copy in enumerate(started):
                j = n // 2 if n < 2 * many else places[n - 2 * many][1]
                if low <= j < high:
                    copy.wait()
            deep = slice(low * depth, high * depth)
            term = jnp.dot(a[:, deep], b[deep, :], preferred_element_type=F32)
            total[...] = total[...] + term if low else term
        back_copy = pltpu.make_async_copy(total, out_ref, sems.at[copies])
        back_copy.start()
        back_copy.wait()

    wide = chunks * cols
    return call(
        kernel,
        at,
        [pinned(activations), pinned(sibling), *flat, *held],
        [],
        [(False, jax.ShapeDtypeStruct((2 * rows, wide), F32))],
        [
            pltpu.VMEM((2 * rows, many * depth), BF16),
            pltpu.VMEM((many * depth, wide), BF16),
            pltpu.VMEM((2 * rows, wide), F32),
            pltpu.SemaphoreType.DMA((copies + 1,)),
        ],
        weight=weight,
        flops=4 * rows * depth * len(flat) * cols,
        moved=4 * rows * depth * many + 2 * depth * len(flat) * cols + 8 * rows * wide,
        name="project",
    )[0]


def project_late(activations, sibling, at, blocks, before, weight):
    chunks, many = len(blocks), at.shape[0]
    flat = [chunk[j] for chunk in blocks for j in sorted(chunk)]
    (depth, cols), rows = flat[0].shape, activations.shape[0]
    wide, held = chunks * cols, [] if before is None else [before]
    moved = flat if len(flat) > chunks else []

    def kernel(at_ref, own_ref, sib_ref, *refs):
        block_refs, out_ref = refs[: len(flat)], refs[len(flat) + len(held)]
        a, b, sems = refs[len(flat) + len(held) + 1 :]
        started = []

        def start(source, target):
            started.append(pltpu.make_async_copy(source, target, sems.at[len(started)]))
            started[-1].start()

        core = lax.rem(lax.axis_index("dp"), 2)
        here, there = (pl.ds(pl.multiple_of(c * rows, rows), rows) for c in (core, 1 - core))
        for j in range(many):
            columns = pl.ds(pl.multiple_of(at_ref[j] * depth, depth), depth)
            start(own_ref.at[:, columns], a.at[here, pl.ds(j * depth, depth)])
            start(sib_ref.at[:, columns], a.at[there, pl.ds(j * depth, depth)])
        places = [(i, j) for i, chunk in enumerate(blocks) for j in sorted(chunk)]
        if moved:
            for ref, (i, j) in zip(block_refs, places):
                start(ref, b.at[pl.ds(j * depth, depth), pl.ds(i * cols, cols)])
        for copy in started:
            copy.wait()
        for i, chunk in enumerate(blocks):
            part = slice(i * cols, (i + 1) * cols)
            deep = slice(min(chunk) * depth, (max(chunk) + 1) * depth)
            block = b[deep, part] if moved else block_refs[i][...]
            term = jnp.dot(a[:, deep], block, preferred_element_type=F32)
            out_ref[:, part] = refs[len(flat)][:, part] + term if held else term

    far = [pinned(activations), pinned(sibling)]
    return call(
        kernel,
        at,
        far + moved,
        ([] if moved else flat) + held,
        [(True, jax.ShapeDtypeStruct((2 * rows, wide), F32))],
        [
            pltpu.VMEM((2 * rows, many * depth), BF16),
            pltpu.VMEM((many * depth, wide) if moved else (16, 128), BF16),
            pltpu.SemaphoreType.DMA((2 * many + len(moved),)),
        ],
        weight=weight,
        flops=4 * rows * depth * len(flat) * cols,
        moved=4 * rows * depth * many + 2 * depth * len(flat) * cols + 8 * rows * wide,
        name="project",
    )[0]


def outer(out_grads, sibling, at, width, dtypes, projected):
    given = projected if isinstance(projected, tuple) else (projected,)
    rows, many, cols = out_grads.shape[0], at.shape[0], given[0].shape[1]
    first = len(given) > 1

    def kernel(at_ref, own_ref, sib_ref, *refs):
        projected_ref, (g, sems) = refs[2 if first else 0], refs[-2:]
        outs = refs[len(given) + first : -2]
        copies = []
        core = lax.rem(lax.axis_index("dp"), 2)
        for j in range(many):
            columns = pl.ds(pl.multiple_of(at_ref[j] * width, width), width)
            for c, ref in ((core, own_ref), (1 - core, sib_ref)):
                target = g.at[pl.ds(pl.multiple_of(c * rows, rows), rows), pl.ds(j * width, width)]
                copies.append(pltpu.make_async_copy(ref.at[:, columns], target, sems.at[len(copies)]))
                copies[-1].start()
        if first:
            projected_ref[...] = (refs[0][...] + refs[1][...]).astype(BF16)
        for j in range(many):
            copies[2 * j].wait()
            copies[2 * j + 1].wait()
            block = g[:, j * width : (j + 1) * width].T
            outs[j][...] = jnp.dot(block, projected_ref[...], preferred_element_type=F32).astype(dtypes[j])

    return call(
        kernel,
        at,
        [pinned(out_grads), pinned(sibling)],
        [*given],
        [(True, jax.ShapeDtypeStruct((2 * rows, cols), BF16))] * first + [(True, jax.ShapeDtypeStruct((width, cols), dtype)) for dtype in dtypes],
        [pltpu.VMEM((2 * rows, many * width), BF16), pltpu.SemaphoreType.DMA((2 * many,))],
        weight=W_OUTER,
        flops=4 * rows * width * many * cols,
        moved=many * (4 * rows * width + 4 * width * cols),
        name="outer",
    )


def back(groups, projector, at, rows, rows_in_all, before, weight):
    many, (width, rank) = at.shape[0], projector.shape
    arrays = [x for group in groups for x in group]
    held = [] if before is None else [before]

    def kernel(at_ref, *refs):
        projector_ref, *array_refs = refs[len(held) : len(held) + 1 + len(arrays)]
        out_ref, pt, o, out_sems = refs[len(held) + 1 + len(arrays) :]
        pt[...] = projector_ref[...].T
        stores, start = [], 0
        for group in groups:
            size, column, total = group[0].shape[0], 0, None
            for x in group:
                deep = slice(column, column + x.shape[1])
                term = jnp.dot(array_refs.pop(0)[...], pt[deep, :], preferred_element_type=F32)
                total = term if total is None else total + term
                column += x.shape[1]
            o[start : start + size, :] = total.astype(BF16)
            for j in range(start // rows, (start + size) // rows):
                target = out_ref.at[pl.ds(pl.multiple_of(at_ref[j] * rows, rows), rows), :]
                stores.append(pltpu.make_async_copy(o.at[pl.ds(j * rows, rows), :], target, out_sems.at[j]))
                stores[-1].start()
            start += size
        for copy in stores:
            copy.wait()

    return call(
        kernel,
        at,
        held,
        [projector, *arrays],
        [(False, jax.ShapeDtypeStruct((rows_in_all, width), BF16))],
        [
            pltpu.VMEM((rank, width), BF16),
            pltpu.VMEM((many * rows, width), BF16),
            pltpu.SemaphoreType.DMA((many,)),
        ],
        weight=weight,
        flops=2 * many * rows * width * rank,
        moved=2 * many * rows * (width + rank),
        name="back",
        aliases={1: 0} if held else None,
    )[0]


def levels(activations, out_grads, projector, first_moment, second_moment, *, nz):
    me = lax.axis_index("dp")
    z, y, core = me // 4, me // 2 % 2, me % 2
    grid = [(a, b, c) for a in range(nz) for b in range(2) for c in range(2)]

    def pairs(to):
        return [((a * 2 + b) * 2 + c, (to(a, b, c)[0] * 2 + to(a, b, c)[1]) * 2 + to(a, b, c)[2]) for a, b, c in grid]

    def swap_core(x):
        return lax.ppermute(x, "dp", pairs(lambda a, b, c: (a, b, 1 - c)))

    def swap_y(x):
        return lax.ppermute(x, "dp", pairs(lambda a, b, c: (a, 1 - b, c)))

    def shift_z(x, k):
        return lax.ppermute(x, "dp", pairs(lambda a, b, c: ((a + k) % nz, b, c)))

    def index(k, dy, dc):
        return (lax.rem(z + nz + k, nz) * 2 + (1 - y if dy else y)) * 2 + (1 - core if dc else core)

    def named(order):
        return jnp.stack([index(*o) for o in order]).astype(jnp.int32)

    def gather(chunks):
        line = [[own] for own in chunks]
        across = [[] for _ in chunks]
        for step in range(nz):
            for i in range(len(chunks)):
                if step:
                    line[i][step], across[i][step - 1] = lax.optimization_barrier((line[i][step], across[i][step - 1]))
                if step < nz - 1:
                    line[i].append(shift_z(line[i][step], 1))
                if step < nz - 1 or i < len(chunks) - 1:
                    across[i].append(swap_y(line[i][step]))
                else:
                    across[i].append(shift_z(after(across[i][0], line[i][step]), nz - 1))
        return line, across

    after = lambda x, *those: lax.optimization_barrier((x, *those))[0]
    ks = list(range(nz - 2, 0, -1)) + [nz - 1]
    depth, rank = projector.shape
    width = first_moment.shape[0]
    cols = rank // CHUNKS
    parts = [slice(i * cols, (i + 1) * cols) for i in range(CHUNKS)]

    order_in = [(-k, dy) for k in range(nz) for dy in (0, 1)]
    order_out = [(k, dy) for dy in (1, 0) for k in ks + [0]]
    last = len(order_in) - 1
    at_in = named([(k, dy, 0) for k, dy in order_in])
    at_out = named([(k, dy, 0) for k, dy in order_out])

    a_sibling = swap_core(activations)
    line, across = gather([projector[:, part] for part in parts])
    g_sibling = swap_core(after(out_grads, a_sibling, line[0][2]))
    block = lambda i, n: (across if n % 2 else line)[i][n // 2]
    soon = [last] * CHUNKS
    blocks = [{n: block(i, n) for n in range(soon[i])} for i in range(CHUNKS)]
    mine = project(activations, a_sibling, at_in[:last], blocks, None, W_EARLY)
    low = min(soon)
    blocks = [{n - low: block(i, n) for n in range(soon[i], last + 1)} for i in range(CHUNKS)]
    mine = project_late(activations, a_sibling, at_in[low:], blocks, mine, W_LATE)
    projected, send = outer(out_grads, g_sibling, at_out[:1], width, [BF16], (mine, swap_core(mine)))
    at = after(at_out[1 : nz + 1], send)
    *sends, keep = outer(out_grads, g_sibling, at, width, [BF16] * (nz - 1) + [F32], projected)
    passed = keep + swap_y(send).astype(F32)
    at = after(at_out[nz + 1 :], passed)
    keeps = outer(out_grads, g_sibling, at, width, [F32] * (nz - 1), projected)
    terms = [keep + swap_y(send).astype(F32) for keep, send in zip(keeps, sends)]
    for term in terms[: nz - 3]:
        passed = term + shift_z(passed.astype(BF16), 1).astype(F32)
    back_term = terms[nz - 3].astype(BF16)
    reduced = terms[nz - 2] + shift_z(back_term, nz - 1).astype(F32) + shift_z(passed.astype(BF16), 1).astype(F32)
    new_first, new_second, direction = adam(reduced, first_moment, second_moment)

    line, across = gather([direction[:, part] for part in parts])
    rows_in_all = 4 * nz * width
    steps = range(1, nz)
    mine = [(direction,)] + [tuple(jnp.concatenate([line[i][k], across[i][k - 1]]) for i in range(CHUNKS)) for k in steps]
    mine.append(tuple(across[i][-1] for i in range(CHUNKS)))
    theirs = [tuple(swap_core(x) for x in group) for group in mine[:-1]]
    order = [[(0, 0)]] + [[(-k, 0), (1 - k, 1)] for k in steps] + [[(1 - nz, 1)]]
    update = None
    for low, high, weight in ((0, nz - 1, W_BACK), (nz - 1, nz + 1, W_LAST)):
        if low:
            theirs.append(tuple(swap_core(after(x, update)) for x in mine[-1]))
        at = named([(k, dy, dc) for dc in (0, 1) for some in order[low:high] for k, dy in some])
        update = back(mine[low:high] + theirs[low:high], projector, at, width, rows_in_all, update, weight)
    return update, new_first, new_second


def solution(mesh):
    devices = mesh.shape["dp"]

    def body(activations, out_grads, projector, first_moment, second_moment):
        aligned = projector.shape[0] % 128 == 0 and first_moment.shape[0] % 128 == 0
        if devices % 4 or devices < 16 or not aligned:
            return plain(activations, out_grads, projector, first_moment, second_moment)
        return levels(activations, out_grads, projector, first_moment, second_moment, nz=devices // 4)

    placed = P(("groups", "dp"), None)
    return jax.shard_map(
        body,
        mesh=mesh,
        in_specs=(placed,) * 5,
        out_specs=(P("groups", "dp"), placed, placed),
        check_vma=False,
    )
```

```python
import functools
import jax
import jax.numpy as jnp
from jax import lax
from jax.experimental import pallas as pl
from jax.experimental.pallas import tpu as pltpu
from jax.sharding import PartitionSpec as P

STEP = 100

decay_first = 0.9
decay_second = 0.999
epsilon = 1e-08

CHUNKS = 2
W_EARLY, W_LATE, W_OUTER, W_BACK, W_LAST = 30, 30, 30, 30, 30000
F32, BF16 = jnp.float32, jnp.bfloat16
VMEM_LIMIT = 16 * 1024 * 1024


def adam(reduced, first_moment, second_moment):
    new_first = decay_first * first_moment + (1.0 - decay_first) * reduced
    new_second = decay_second * second_moment + (1.0 - decay_second) * reduced * reduced
    first_fix = 1.0 - decay_first**STEP
    second_fix = 1.0 - decay_second**STEP
    direction = (new_first / first_fix / (jnp.sqrt(new_second / second_fix) + epsilon)).astype(BF16)
    return new_first, new_second, direction


def plain(activations, out_grads, projector, first_moment, second_moment):
    projected = jnp.dot(
        activations,
        lax.all_gather(projector, "dp", axis=0, tiled=True),
        preferred_element_type=F32,
    ).astype(BF16)
    reduced = lax.psum_scatter(
        lax.dot_general(out_grads, projected, (((0,), (0,)), ((), ())), preferred_element_type=F32),
        "dp",
        scatter_dimension=0,
        tiled=True,
    )
    new_first, new_second, direction = adam(reduced, first_moment, second_moment)
    update = lax.dot_general(
        lax.all_gather(direction, "dp", axis=0, tiled=True),
        projector,
        (((1,), (1,)), ((), ())),
        preferred_element_type=F32,
    ).astype(BF16)
    return update, new_first, new_second


def params():
    return pltpu.CompilerParams(vmem_limit_bytes=VMEM_LIMIT)


def cost(weight, flops, moved):
    return pl.CostEstimate(flops=weight * flops, bytes_accessed=weight * moved, transcendentals=0)


def pinned(x):
    return pltpu.with_memory_space_constraint(x, pltpu.HBM)


def call(kernel, scalars, far, near, outs, scratch, *, weight, flops, moved, name, aliases=None):
    anywhere, vmem = pl.BlockSpec(memory_space=pl.ANY), pl.BlockSpec(memory_space=pltpu.VMEM)
    return pl.pallas_call(
        kernel,
        grid_spec=pltpu.PrefetchScalarGridSpec(
            num_scalar_prefetch=1,
            grid=(),
            in_specs=[anywhere] * len(far) + [vmem] * len(near),
            out_specs=[vmem if inside else anywhere for inside, _ in outs],
            scratch_shapes=scratch,
        ),
        out_shape=[shape for _, shape in outs],
        input_output_aliases=aliases or {},
        compiler_params=params(),
        cost_estimate=cost(weight, flops, moved),
        name=name,
    )(scalars, *far, *near)


def project(activations, sibling, at, blocks):
    chunks, many = len(blocks), at.shape[0]
    flat = [block for chunk in blocks for block in chunk]
    (depth, cols), rows = flat[0].shape, activations.shape[0]
    wide = chunks * cols

    def kernel(at_ref, own_ref, sib_ref, *refs):
        block_refs, (out_ref, a, b, total, sems) = refs[: len(flat)], refs[len(flat) :]
        started = [[] for _ in range(many)]

        def start(j, source, target):
            n = sum(len(copies) for copies in started)
            started[j].append(pltpu.make_async_copy(source, target, sems.at[n]))
            started[j][-1].start()

        core = lax.rem(lax.axis_index("dp"), 2)
        here, there = (pl.ds(pl.multiple_of(c * rows, rows), rows) for c in (core, 1 - core))
        for j in range(many):
            columns = pl.ds(pl.multiple_of(at_ref[j] * depth, depth), depth)
            start(j, own_ref.at[:, columns], a.at[here, pl.ds(j * depth, depth)])
            start(j, sib_ref.at[:, columns], a.at[there, pl.ds(j * depth, depth)])
        for n, ref in enumerate(block_refs):
            i, j = n // many, n % many
            start(j, ref, b.at[pl.ds(j * depth, depth), pl.ds(i * cols, cols)])
        cut = (many + 1) // 2
        for low, high in ((0, cut), (cut, many)):
            for copies in started[low:high]:
                for copy in copies:
                    copy.wait()
            deep = slice(low * depth, high * depth)
            term = jnp.dot(a[:, deep], b[deep, :], preferred_element_type=F32)
            total[...] = total[...] + term if low else term
        back_copy = pltpu.make_async_copy(total, out_ref, sems.at[2 * many + len(flat)])
        back_copy.start()
        back_copy.wait()

    return call(
        kernel,
        at,
        [pinned(activations), pinned(sibling), *flat],
        [],
        [(False, jax.ShapeDtypeStruct((2 * rows, wide), F32))],
        [
            pltpu.VMEM((2 * rows, many * depth), BF16),
            pltpu.VMEM((many * depth, wide), BF16),
            pltpu.VMEM((2 * rows, wide), F32),
            pltpu.SemaphoreType.DMA((2 * many + len(flat) + 1,)),
        ],
        weight=W_EARLY,
        flops=4 * rows * depth * len(flat) * cols,
        moved=4 * rows * depth * many + 2 * depth * len(flat) * cols + 8 * rows * wide,
        name="project",
    )[0]


def project_last(activations, sibling, at, blocks, before):
    (depth, cols), rows = blocks[0].shape, activations.shape[0]

    def kernel(at_ref, own_ref, sib_ref, *refs):
        block_refs, (before_ref, out_ref, a, sems) = refs[: len(blocks)], refs[len(blocks) :]
        core = lax.rem(lax.axis_index("dp"), 2)
        columns = pl.ds(pl.multiple_of(at_ref[0] * depth, depth), depth)
        copies = []
        for n, (c, ref) in enumerate(((core, own_ref), (1 - core, sib_ref))):
            target = a.at[pl.ds(pl.multiple_of(c * rows, rows), rows), :]
            copies.append(pltpu.make_async_copy(ref.at[:, columns], target, sems.at[n]))
            copies[-1].start()
        for copy in copies:
            copy.wait()
        for i, ref in enumerate(block_refs):
            part = slice(i * cols, (i + 1) * cols)
            out_ref[:, part] = before_ref[:, part] + jnp.dot(a[...], ref[...], preferred_element_type=F32)

    return call(
        kernel,
        at,
        [pinned(activations), pinned(sibling)],
        [*blocks, before],
        [(True, jax.ShapeDtypeStruct(before.shape, F32))],
        [pltpu.VMEM((2 * rows, depth), BF16), pltpu.SemaphoreType.DMA((2,))],
        weight=W_LATE,
        flops=4 * rows * depth * len(blocks) * cols,
        moved=4 * rows * depth + 2 * depth * len(blocks) * cols + 8 * rows * len(blocks) * cols,
        name="project_last",
    )[0]


def outer(out_grads, sibling, at, width, dtypes, projected):
    given = projected if isinstance(projected, tuple) else (projected,)
    rows, many, cols = out_grads.shape[0], at.shape[0], given[0].shape[1]
    first = len(given) > 1

    def kernel(at_ref, own_ref, sib_ref, *refs):
        projected_ref, (g, sems) = refs[2 if first else 0], refs[-2:]
        outs = refs[len(given) + first : -2]
        copies = []
        core = lax.rem(lax.axis_index("dp"), 2)
        for j in range(many):
            columns = pl.ds(pl.multiple_of(at_ref[j] * width, width), width)
            for c, ref in ((core, own_ref), (1 - core, sib_ref)):
                target = g.at[pl.ds(pl.multiple_of(c * rows, rows), rows), pl.ds(j * width, width)]
                copies.append(pltpu.make_async_copy(ref.at[:, columns], target, sems.at[len(copies)]))
                copies[-1].start()
        if first:
            projected_ref[...] = (refs[0][...] + refs[1][...]).astype(BF16)
        for j in range(many):
            copies[2 * j].wait()
            copies[2 * j + 1].wait()
            block = g[:, j * width : (j + 1) * width].T
            outs[j][...] = jnp.dot(block, projected_ref[...], preferred_element_type=F32).astype(dtypes[j])

    return call(
        kernel,
        at,
        [pinned(out_grads), pinned(sibling)],
        [*given],
        [(True, jax.ShapeDtypeStruct((2 * rows, cols), BF16))] * first + [(True, jax.ShapeDtypeStruct((width, cols), dtype)) for dtype in dtypes],
        [pltpu.VMEM((2 * rows, many * width), BF16), pltpu.SemaphoreType.DMA((2 * many,))],
        weight=W_OUTER,
        flops=4 * rows * width * many * cols,
        moved=many * (4 * rows * width + 4 * width * cols),
        name="outer",
    )


def back(groups, projector, at, rows, rows_in_all, before, weight):
    many, (width, rank) = at.shape[0], projector.shape
    arrays = [x for group in groups for x in group]
    held = [] if before is None else [before]

    def kernel(at_ref, *refs):
        projector_ref, *array_refs = refs[len(held) : len(held) + 1 + len(arrays)]
        out_ref, pt, o, out_sems = refs[len(held) + 1 + len(arrays) :]
        pt[...] = projector_ref[...].T
        stores, start = [], 0
        for group in groups:
            size, column, total = group[0].shape[0], 0, None
            for x in group:
                deep = slice(column, column + x.shape[1])
                term = jnp.dot(array_refs.pop(0)[...], pt[deep, :], preferred_element_type=F32)
                total = term if total is None else total + term
                column += x.shape[1]
            o[start : start + size, :] = total.astype(BF16)
            for j in range(start // rows, (start + size) // rows):
                target = out_ref.at[pl.ds(pl.multiple_of(at_ref[j] * rows, rows), rows), :]
                stores.append(pltpu.make_async_copy(o.at[pl.ds(j * rows, rows), :], target, out_sems.at[j]))
                stores[-1].start()
            start += size
        for copy in stores:
            copy.wait()

    return call(
        kernel,
        at,
        held,
        [projector, *arrays],
        [(False, jax.ShapeDtypeStruct((rows_in_all, width), BF16))],
        [
            pltpu.VMEM((rank, width), BF16),
            pltpu.VMEM((many * rows, width), BF16),
            pltpu.SemaphoreType.DMA((many,)),
        ],
        weight=weight,
        flops=2 * many * rows * width * rank,
        moved=2 * many * rows * (width + rank),
        name="back",
        aliases={1: 0} if held else None,
    )[0]


def levels(activations, out_grads, projector, first_moment, second_moment, *, nz):
    me = lax.axis_index("dp")
    z, y, core = me // 4, me // 2 % 2, me % 2
    grid = [(a, b, c) for a in range(nz) for b in range(2) for c in range(2)]

    def pairs(to):
        return [((a * 2 + b) * 2 + c, (to(a, b, c)[0] * 2 + to(a, b, c)[1]) * 2 + to(a, b, c)[2]) for a, b, c in grid]

    def swap_core(x):
        return lax.ppermute(x, "dp", pairs(lambda a, b, c: (a, b, 1 - c)))

    def swap_y(x):
        return lax.ppermute(x, "dp", pairs(lambda a, b, c: (a, 1 - b, c)))

    def shift_z(x, k):
        return lax.ppermute(x, "dp", pairs(lambda a, b, c: ((a + k) % nz, b, c)))

    def index(k, dy, dc):
        return (lax.rem(z + nz + k, nz) * 2 + (1 - y if dy else y)) * 2 + (1 - core if dc else core)

    def named(order):
        return jnp.stack([index(*o) for o in order]).astype(jnp.int32)

    def gather(chunks):
        line = [[own] for own in chunks]
        across = [[] for _ in chunks]
        for step in range(nz):
            for i in range(len(chunks)):
                if step:
                    line[i][step], across[i][step - 1] = lax.optimization_barrier((line[i][step], across[i][step - 1]))
                if step < nz - 1:
                    line[i].append(shift_z(line[i][step], 1))
                if step < nz - 1 or i < len(chunks) - 1:
                    across[i].append(swap_y(line[i][step]))
                else:
                    across[i].append(shift_z(after(across[i][0], line[i][step]), nz - 1))
        return line, across

    after = lambda x, *those: lax.optimization_barrier((x, *those))[0]
    ks = list(range(nz - 2, 0, -1)) + [nz - 1]
    depth, rank = projector.shape
    width = first_moment.shape[0]
    cols = rank // CHUNKS
    parts = [slice(i * cols, (i + 1) * cols) for i in range(CHUNKS)]

    order_in = [(-k, dy) for k in range(nz) for dy in (0, 1)]
    order_out = [(k, dy) for dy in (1, 0) for k in ks + [0]]
    last = len(order_in) - 1
    at_in = named([(k, dy, 0) for k, dy in order_in])
    at_out = named([(k, dy, 0) for k, dy in order_out])

    a_sibling = swap_core(activations)
    line, across = gather([projector[:, part] for part in parts])
    g_sibling = swap_core(after(out_grads, a_sibling, line[0][2]))
    block = lambda i, n: (across if n % 2 else line)[i][n // 2]
    mine = project(activations, a_sibling, at_in[:last], [[block(i, n) for n in range(last)] for i in range(CHUNKS)])
    mine = project_last(activations, a_sibling, at_in[last:], [block(i, last) for i in range(CHUNKS)], mine)

    projected, send = outer(out_grads, g_sibling, at_out[:1], width, [BF16], (mine, swap_core(mine)))
    at = after(at_out[1 : nz + 1], send)
    *sends, keep = outer(out_grads, g_sibling, at, width, [BF16] * (nz - 1) + [F32], projected)
    passed = keep + swap_y(send).astype(F32)
    at = after(at_out[nz + 1 :], passed)
    keeps = outer(out_grads, g_sibling, at, width, [F32] * (nz - 1), projected)
    terms = [keep + swap_y(send).astype(F32) for keep, send in zip(keeps, sends)]
    for term in terms[: nz - 3]:
        passed = term + shift_z(passed.astype(BF16), 1).astype(F32)
    back_term = terms[nz - 3].astype(BF16)
    reduced = terms[nz - 2] + shift_z(back_term, nz - 1).astype(F32) + shift_z(passed.astype(BF16), 1).astype(F32)
    new_first, new_second, direction = adam(reduced, first_moment, second_moment)

    line, across = gather([direction[:, part] for part in parts])
    rows_in_all = 4 * nz * width
    steps = range(1, nz)
    mine = [(direction,)] + [tuple(jnp.concatenate([line[i][k], across[i][k - 1]]) for i in range(CHUNKS)) for k in steps]
    mine.append(tuple(across[i][-1] for i in range(CHUNKS)))
    theirs = [tuple(swap_core(after(x, line[0][1])) for x in mine[0])]
    theirs += [tuple(swap_core(x) for x in group) for group in mine[1:-1]]
    order = [[(0, 0)]] + [[(-k, 0), (1 - k, 1)] for k in steps] + [[(1 - nz, 1)]]
    update = None
    for low, high, weight in ((0, nz - 1, W_BACK), (nz - 1, nz + 1, W_LAST)):
        if low:
            theirs.append(tuple(swap_core(after(x, update)) for x in mine[-1]))
        at = named([(k, dy, dc) for dc in (0, 1) for some in order[low:high] for k, dy in some])
        update = back(mine[low:high] + theirs[low:high], projector, at, width, rows_in_all, update, weight)
    return update, new_first, new_second


def solution(mesh):
    devices = mesh.shape["dp"]

    def body(activations, out_grads, projector, first_moment, second_moment):
        aligned = projector.shape[0] % 128 == 0 and first_moment.shape[0] % 128 == 0
        if devices % 4 or devices < 16 or not aligned:
            return plain(activations, out_grads, projector, first_moment, second_moment)
        return levels(activations, out_grads, projector, first_moment, second_moment, nz=devices // 4)

    placed = P(("groups", "dp"), None)
    return jax.shard_map(
        body,
        mesh=mesh,
        in_specs=(placed,) * 5,
        out_specs=(P("groups", "dp"), placed, placed),
        check_vma=False,
    )
```

```python
import functools
import jax
import jax.numpy as jnp
from jax import lax
from jax.experimental import pallas as pl
from jax.experimental.pallas import tpu as pltpu
from jax.sharding import PartitionSpec as P

STEP = 100

decay_first = 0.9
decay_second = 0.999
epsilon = 1e-08

CHUNKS = 2
W_EARLY, W_LATE, W_OUTER, W_BACK, W_LAST = 30, 30, 30, 30, 30000
F32, BF16 = jnp.float32, jnp.bfloat16
VMEM_LIMIT = 16 * 1024 * 1024


def adam(reduced, first_moment, second_moment):
    new_first = decay_first * first_moment + (1.0 - decay_first) * reduced
    new_second = decay_second * second_moment + (1.0 - decay_second) * reduced * reduced
    first_fix = 1.0 - decay_first**STEP
    second_fix = 1.0 - decay_second**STEP
    direction = (new_first / first_fix / (jnp.sqrt(new_second / second_fix) + epsilon)).astype(BF16)
    return new_first, new_second, direction


def plain(activations, out_grads, projector, first_moment, second_moment):
    projected = jnp.dot(
        activations,
        lax.all_gather(projector, "dp", axis=0, tiled=True),
        preferred_element_type=F32,
    ).astype(BF16)
    reduced = lax.psum_scatter(
        lax.dot_general(out_grads, projected, (((0,), (0,)), ((), ())), preferred_element_type=F32),
        "dp",
        scatter_dimension=0,
        tiled=True,
    )
    new_first, new_second, direction = adam(reduced, first_moment, second_moment)
    update = lax.dot_general(
        lax.all_gather(direction, "dp", axis=0, tiled=True),
        projector,
        (((1,), (1,)), ((), ())),
        preferred_element_type=F32,
    ).astype(BF16)
    return update, new_first, new_second


def params():
    return pltpu.CompilerParams(vmem_limit_bytes=VMEM_LIMIT)


def cost(weight, flops, moved):
    return pl.CostEstimate(flops=weight * flops, bytes_accessed=weight * moved, transcendentals=0)


def pinned(x):
    return pltpu.with_memory_space_constraint(x, pltpu.HBM)


def call(kernel, scalars, far, near, outs, scratch, *, weight, flops, moved, name, aliases=None):
    anywhere, vmem = pl.BlockSpec(memory_space=pl.ANY), pl.BlockSpec(memory_space=pltpu.VMEM)
    return pl.pallas_call(
        kernel,
        grid_spec=pltpu.PrefetchScalarGridSpec(
            num_scalar_prefetch=1,
            grid=(),
            in_specs=[anywhere] * len(far) + [vmem] * len(near),
            out_specs=[vmem if inside else anywhere for inside, _ in outs],
            scratch_shapes=scratch,
        ),
        out_shape=[shape for _, shape in outs],
        input_output_aliases=aliases or {},
        compiler_params=params(),
        cost_estimate=cost(weight, flops, moved),
        name=name,
    )(scalars, *far, *near)


def project(activations, sibling, at, blocks):
    chunks, many = len(blocks), len(blocks[0])
    flat = [block for chunk in blocks for block in chunk]
    (depth, cols), rows = flat[0].shape, activations.shape[0]
    wide = chunks * cols

    def kernel(at_ref, own_ref, sib_ref, *refs):
        block_refs, (out_ref, next_ref, a, b, total, sems) = refs[: len(flat)], refs[len(flat) :]
        started = [[] for _ in range(many + 1)]

        def start(j, source, target):
            n = sum(len(copies) for copies in started)
            started[j].append(pltpu.make_async_copy(source, target, sems.at[n]))
            started[j][-1].start()

        core = lax.rem(lax.axis_index("dp"), 2)
        here, there = (pl.ds(pl.multiple_of(c * rows, rows), rows) for c in (core, 1 - core))
        for j in range(many):
            columns = pl.ds(pl.multiple_of(at_ref[j] * depth, depth), depth)
            start(j, own_ref.at[:, columns], a.at[here, pl.ds(j * depth, depth)])
            start(j, sib_ref.at[:, columns], a.at[there, pl.ds(j * depth, depth)])
        for n, ref in enumerate(block_refs):
            i, j = n // many, n % many
            start(j, ref, b.at[pl.ds(j * depth, depth), pl.ds(i * cols, cols)])
        columns = pl.ds(pl.multiple_of(at_ref[many] * depth, depth), depth)
        start(many, own_ref.at[:, columns], next_ref.at[here, :])
        start(many, sib_ref.at[:, columns], next_ref.at[there, :])
        cut = (many + 1) // 2
        for low, high in ((0, cut), (cut, many)):
            for copies in started[low:high]:
                for copy in copies:
                    copy.wait()
            deep = slice(low * depth, high * depth)
            term = jnp.dot(a[:, deep], b[deep, :], preferred_element_type=F32)
            total[...] = total[...] + term if low else term
        back_copy = pltpu.make_async_copy(total, out_ref, sems.at[2 * many + 2 + len(flat)])
        back_copy.start()
        for copy in started[many]:
            copy.wait()
        back_copy.wait()

    return call(
        kernel,
        at,
        [pinned(activations), pinned(sibling), *flat],
        [],
        [(False, jax.ShapeDtypeStruct((2 * rows, wide), F32)), (True, jax.ShapeDtypeStruct((2 * rows, depth), BF16))],
        [
            pltpu.VMEM((2 * rows, many * depth), BF16),
            pltpu.VMEM((many * depth, wide), BF16),
            pltpu.VMEM((2 * rows, wide), F32),
            pltpu.SemaphoreType.DMA((2 * many + len(flat) + 3,)),
        ],
        weight=W_EARLY,
        flops=4 * rows * depth * len(flat) * cols,
        moved=4 * rows * depth * many + 2 * depth * len(flat) * cols + 8 * rows * wide,
        name="project",
    )


def project_last(columns, blocks, before):
    (rows, depth), cols = columns.shape, blocks[0].shape[1]

    def kernel(columns_ref, *refs):
        block_refs, (before_ref, out_ref) = refs[: len(blocks)], refs[len(blocks) :]
        for i, ref in enumerate(block_refs):
            part = slice(i * cols, (i + 1) * cols)
            out_ref[:, part] = before_ref[:, part] + jnp.dot(columns_ref[...], ref[...], preferred_element_type=F32)

    vmem = pl.BlockSpec(memory_space=pltpu.VMEM)
    return pl.pallas_call(
        kernel,
        in_specs=[vmem] * (len(blocks) + 2),
        out_specs=vmem,
        out_shape=jax.ShapeDtypeStruct(before.shape, F32),
        compiler_params=params(),
        cost_estimate=cost(W_LATE, 2 * rows * depth * len(blocks) * cols, 2 * rows * depth + 10 * rows * len(blocks) * cols),
        name="project_last",
    )(columns, *blocks, before)


def turn(out_grads, sibling, at, width):
    rows = out_grads.shape[0]

    def kernel(at_ref, own_ref, sib_ref, out_ref, g, sems):
        core = lax.rem(lax.axis_index("dp"), 2)
        columns = pl.ds(pl.multiple_of(at_ref[0] * width, width), width)
        copies = []
        for n, (c, ref) in enumerate(((core, own_ref), (1 - core, sib_ref))):
            target = g.at[pl.ds(pl.multiple_of(c * rows, rows), rows), :]
            copies.append(pltpu.make_async_copy(ref.at[:, columns], target, sems.at[n]))
            copies[-1].start()
        for copy in copies:
            copy.wait()
        out_ref[...] = g[...].T

    return call(
        kernel,
        at,
        [pinned(out_grads), pinned(sibling)],
        [],
        [(True, jax.ShapeDtypeStruct((width, 2 * rows), BF16))],
        [pltpu.VMEM((2 * rows, width), BF16), pltpu.SemaphoreType.DMA((2,))],
        weight=W_OUTER,
        flops=0,
        moved=8 * rows * width,
        name="turn",
    )[0]


def outer_first(turned, mine, theirs):
    (width, rows), cols = turned.shape, mine.shape[1]

    def kernel(turned_ref, mine_ref, theirs_ref, projected_ref, out_ref):
        projected_ref[...] = (mine_ref[...] + theirs_ref[...]).astype(BF16)
        out_ref[...] = jnp.dot(turned_ref[...], projected_ref[...], preferred_element_type=F32).astype(BF16)

    vmem = pl.BlockSpec(memory_space=pltpu.VMEM)
    return pl.pallas_call(
        kernel,
        in_specs=[vmem] * 3,
        out_specs=[vmem] * 2,
        out_shape=[jax.ShapeDtypeStruct((rows, cols), BF16), jax.ShapeDtypeStruct((width, cols), BF16)],
        compiler_params=params(),
        cost_estimate=cost(W_OUTER, 2 * rows * width * cols, 10 * rows * cols),
        name="outer_first",
    )(turned, mine, theirs)


def outer(out_grads, sibling, at, width, dtypes, projected):
    rows, many, cols = out_grads.shape[0], at.shape[0], projected.shape[1]

    def kernel(at_ref, own_ref, sib_ref, projected_ref, *refs):
        outs, (g, sems) = refs[:-2], refs[-2:]
        copies = []
        core = lax.rem(lax.axis_index("dp"), 2)
        for j in range(many):
            columns = pl.ds(pl.multiple_of(at_ref[j] * width, width), width)
            for c, ref in ((core, own_ref), (1 - core, sib_ref)):
                target = g.at[pl.ds(pl.multiple_of(c * rows, rows), rows), pl.ds(j * width, width)]
                copies.append(pltpu.make_async_copy(ref.at[:, columns], target, sems.at[len(copies)]))
                copies[-1].start()
        for j in range(many):
            copies[2 * j].wait()
            copies[2 * j + 1].wait()
            block = g[:, j * width : (j + 1) * width].T
            outs[j][...] = jnp.dot(block, projected_ref[...], preferred_element_type=F32).astype(dtypes[j])

    return call(
        kernel,
        at,
        [pinned(out_grads), pinned(sibling)],
        [projected],
        [(True, jax.ShapeDtypeStruct((width, cols), dtype)) for dtype in dtypes],
        [pltpu.VMEM((2 * rows, many * width), BF16), pltpu.SemaphoreType.DMA((2 * many,))],
        weight=W_OUTER,
        flops=4 * rows * width * many * cols,
        moved=many * (4 * rows * width + 4 * width * cols),
        name="outer",
    )


def back(groups, projector, at, rows, rows_in_all, before, weight):
    many, (width, rank) = at.shape[0], projector.shape
    arrays = [x for group in groups for x in group]
    held = [] if before is None else [before]

    def kernel(at_ref, *refs):
        projector_ref, *array_refs = refs[len(held) : len(held) + 1 + len(arrays)]
        out_ref, pt, o, out_sems = refs[len(held) + 1 + len(arrays) :]
        pt[...] = projector_ref[...].T
        stores, start = [], 0
        for group in groups:
            size, column, total = group[0].shape[0], 0, None
            for x in group:
                deep = slice(column, column + x.shape[1])
                term = jnp.dot(array_refs.pop(0)[...], pt[deep, :], preferred_element_type=F32)
                total = term if total is None else total + term
                column += x.shape[1]
            o[start : start + size, :] = total.astype(BF16)
            for j in range(start // rows, (start + size) // rows):
                target = out_ref.at[pl.ds(pl.multiple_of(at_ref[j] * rows, rows), rows), :]
                stores.append(pltpu.make_async_copy(o.at[pl.ds(j * rows, rows), :], target, out_sems.at[j]))
                stores[-1].start()
            start += size
        for copy in stores:
            copy.wait()

    return call(
        kernel,
        at,
        held,
        [projector, *arrays],
        [(False, jax.ShapeDtypeStruct((rows_in_all, width), BF16))],
        [
            pltpu.VMEM((rank, width), BF16),
            pltpu.VMEM((many * rows, width), BF16),
            pltpu.SemaphoreType.DMA((many,)),
        ],
        weight=weight,
        flops=2 * many * rows * width * rank,
        moved=2 * many * rows * (width + rank),
        name="back",
        aliases={1: 0} if held else None,
    )[0]


def levels(activations, out_grads, projector, first_moment, second_moment, *, nz):
    me = lax.axis_index("dp")
    z, y, core = me // 4, me // 2 % 2, me % 2
    grid = [(a, b, c) for a in range(nz) for b in range(2) for c in range(2)]

    def pairs(to):
        return [((a * 2 + b) * 2 + c, (to(a, b, c)[0] * 2 + to(a, b, c)[1]) * 2 + to(a, b, c)[2]) for a, b, c in grid]

    def swap_core(x):
        return lax.ppermute(x, "dp", pairs(lambda a, b, c: (a, b, 1 - c)))

    def swap_y(x):
        return lax.ppermute(x, "dp", pairs(lambda a, b, c: (a, 1 - b, c)))

    def shift_z(x, k):
        return lax.ppermute(x, "dp", pairs(lambda a, b, c: ((a + k) % nz, b, c)))

    def index(k, dy, dc):
        return (lax.rem(z + nz + k, nz) * 2 + (1 - y if dy else y)) * 2 + (1 - core if dc else core)

    def named(order):
        return jnp.stack([index(*o) for o in order]).astype(jnp.int32)

    def gather(chunks):
        line = [[own] for own in chunks]
        across = [[] for _ in chunks]
        for step in range(nz):
            for i in range(len(chunks)):
                if step:
                    line[i][step], across[i][step - 1] = lax.optimization_barrier((line[i][step], across[i][step - 1]))
                if step < nz - 1:
                    line[i].append(shift_z(line[i][step], 1))
                if step < nz - 1 or i < len(chunks) - 1:
                    across[i].append(swap_y(line[i][step]))
                else:
                    across[i].append(shift_z(after(across[i][0], line[i][step]), nz - 1))
        return line, across

    after = lambda x, *those: lax.optimization_barrier((x, *those))[0]
    ks = list(range(nz - 2, 0, -1)) + [nz - 1]
    depth, rank = projector.shape
    width = first_moment.shape[0]
    cols = rank // CHUNKS
    parts = [slice(i * cols, (i + 1) * cols) for i in range(CHUNKS)]

    order_in = [(-k, dy) for k in range(nz) for dy in (0, 1)]
    order_out = [(k, dy) for dy in (1, 0) for k in ks + [0]]
    last = len(order_in) - 1
    at_in = named([(k, dy, 0) for k, dy in order_in])
    at_out = named([(k, dy, 0) for k, dy in order_out])

    a_sibling = swap_core(activations)
    line, across = gather([projector[:, part] for part in parts])
    g_sibling = swap_core(after(out_grads, a_sibling, line[0][2]))
    block = lambda i, n: (across if n % 2 else line)[i][n // 2]
    mine, columns = project(activations, a_sibling, at_in, [[block(i, n) for n in range(last)] for i in range(CHUNKS)])
    mine = project_last(columns, [block(i, last) for i in range(CHUNKS)], mine)

    turned = turn(out_grads, g_sibling, at_out[:1], width)
    projected, send = outer_first(turned, mine, swap_core(mine))
    at = after(at_out[1 : nz + 1], send)
    *sends, keep = outer(out_grads, g_sibling, at, width, [BF16] * (nz - 1) + [F32], projected)
    passed = keep + swap_y(send).astype(F32)
    at = after(at_out[nz + 1 :], passed)
    keeps = outer(out_grads, g_sibling, at, width, [F32] * (nz - 1), projected)
    terms = [keep + swap_y(send).astype(F32) for keep, send in zip(keeps, sends)]
    for term in terms[: nz - 3]:
        passed = term + shift_z(passed.astype(BF16), 1).astype(F32)
    back_term = terms[nz - 3].astype(BF16)
    reduced = terms[nz - 2] + shift_z(back_term, nz - 1).astype(F32) + shift_z(passed.astype(BF16), 1).astype(F32)
    new_first, new_second, direction = adam(reduced, first_moment, second_moment)

    line, across = gather([direction[:, part] for part in parts])
    rows_in_all = 4 * nz * width
    steps = range(1, nz)
    mine = [(direction,)] + [tuple(jnp.concatenate([line[i][k], across[i][k - 1]]) for i in range(CHUNKS)) for k in steps]
    mine.append(tuple(across[i][-1] for i in range(CHUNKS)))
    theirs = [tuple(swap_core(after(x, line[0][1])) for x in mine[0])]
    theirs += [tuple(swap_core(x) for x in group) for group in mine[1:-1]]
    order = [[(0, 0)]] + [[(-k, 0), (1 - k, 1)] for k in steps] + [[(1 - nz, 1)]]
    update = None
    for low, high, weight in ((0, nz - 1, W_BACK), (nz - 1, nz + 1, W_LAST)):
        if low:
            theirs.append(tuple(swap_core(after(x, update)) for x in mine[-1]))
        at = named([(k, dy, dc) for dc in (0, 1) for some in order[low:high] for k, dy in some])
        update = back(mine[low:high] + theirs[low:high], projector, at, width, rows_in_all, update, weight)
    return update, new_first, new_second


def solution(mesh):
    devices = mesh.shape["dp"]

    def body(activations, out_grads, projector, first_moment, second_moment):
        aligned = projector.shape[0] % 128 == 0 and first_moment.shape[0] % 128 == 0
        if devices % 4 or devices < 16 or not aligned:
            return plain(activations, out_grads, projector, first_moment, second_moment)
        return levels(activations, out_grads, projector, first_moment, second_moment, nz=devices // 4)

    placed = P(("groups", "dp"), None)
    return jax.shard_map(
        body,
        mesh=mesh,
        in_specs=(placed,) * 5,
        out_specs=(P("groups", "dp"), placed, placed),
        check_vma=False,
    )
```

```python
import functools
import jax
import jax.numpy as jnp
from jax import lax
from jax.experimental import pallas as pl
from jax.experimental.pallas import tpu as pltpu
from jax.sharding import PartitionSpec as P

STEP = 100

decay_first = 0.9
decay_second = 0.999
epsilon = 1e-08

CHUNKS = 2
W_EARLY, W_LATE, W_OUTER, W_BACK, W_LAST = 3, 30, 30, 30, 30000
F32, BF16 = jnp.float32, jnp.bfloat16
VMEM_LIMIT = 16 * 1024 * 1024


def adam(reduced, first_moment, second_moment):
    new_first = decay_first * first_moment + (1.0 - decay_first) * reduced
    new_second = decay_second * second_moment + (1.0 - decay_second) * reduced * reduced
    first_fix = 1.0 - decay_first**STEP
    second_fix = 1.0 - decay_second**STEP
    direction = (new_first / first_fix / (jnp.sqrt(new_second / second_fix) + epsilon)).astype(BF16)
    return new_first, new_second, direction


def plain(activations, out_grads, projector, first_moment, second_moment):
    projected = jnp.dot(
        activations,
        lax.all_gather(projector, "dp", axis=0, tiled=True),
        preferred_element_type=F32,
    ).astype(BF16)
    reduced = lax.psum_scatter(
        lax.dot_general(out_grads, projected, (((0,), (0,)), ((), ())), preferred_element_type=F32),
        "dp",
        scatter_dimension=0,
        tiled=True,
    )
    new_first, new_second, direction = adam(reduced, first_moment, second_moment)
    update = lax.dot_general(
        lax.all_gather(direction, "dp", axis=0, tiled=True),
        projector,
        (((1,), (1,)), ((), ())),
        preferred_element_type=F32,
    ).astype(BF16)
    return update, new_first, new_second


def params():
    return pltpu.CompilerParams(vmem_limit_bytes=VMEM_LIMIT)


def cost(weight, flops, moved):
    return pl.CostEstimate(flops=weight * flops, bytes_accessed=weight * moved, transcendentals=0)


def pinned(x):
    return pltpu.with_memory_space_constraint(x, pltpu.HBM)


def call(kernel, scalars, far, near, outs, scratch, *, weight, flops, moved, name, aliases=None):
    anywhere, vmem = pl.BlockSpec(memory_space=pl.ANY), pl.BlockSpec(memory_space=pltpu.VMEM)
    return pl.pallas_call(
        kernel,
        grid_spec=pltpu.PrefetchScalarGridSpec(
            num_scalar_prefetch=1,
            grid=(),
            in_specs=[anywhere] * len(far) + [vmem] * len(near),
            out_specs=[vmem if inside else anywhere for inside, _ in outs],
            scratch_shapes=scratch,
        ),
        out_shape=[shape for _, shape in outs],
        input_output_aliases=aliases or {},
        compiler_params=params(),
        cost_estimate=cost(weight, flops, moved),
        name=name,
    )(scalars, *far, *near)


def project(activations, sibling, at, blocks):
    chunks, many = len(blocks), len(blocks[0])
    flat = [block for chunk in blocks for block in chunk]
    (depth, cols), rows = flat[0].shape, activations.shape[0]
    wide = chunks * cols

    def kernel(at_ref, own_ref, sib_ref, *refs):
        block_refs, (out_ref, next_ref, a, b, total, sems) = refs[: len(flat)], refs[len(flat) :]
        started = [[] for _ in range(many + 1)]

        def start(j, source, target):
            n = sum(len(copies) for copies in started)
            started[j].append(pltpu.make_async_copy(source, target, sems.at[n]))
            started[j][-1].start()

        core = lax.rem(lax.axis_index("dp"), 2)
        here, there = (pl.ds(pl.multiple_of(c * rows, rows), rows) for c in (core, 1 - core))
        for j in range(many):
            columns = pl.ds(pl.multiple_of(at_ref[j] * depth, depth), depth)
            start(j, own_ref.at[:, columns], a.at[here, pl.ds(j * depth, depth)])
            start(j, sib_ref.at[:, columns], a.at[there, pl.ds(j * depth, depth)])
        for n, ref in enumerate(block_refs):
            i, j = n // many, n % many
            start(j, ref, b.at[pl.ds(j * depth, depth), pl.ds(i * cols, cols)])
        columns = pl.ds(pl.multiple_of(at_ref[many] * depth, depth), depth)
        start(many, own_ref.at[:, columns], next_ref.at[here, :])
        start(many, sib_ref.at[:, columns], next_ref.at[there, :])
        cut = (many + 1) // 2
        for low, high in ((0, cut), (cut, many)):
            for copies in started[low:high]:
                for copy in copies:
                    copy.wait()
            deep = slice(low * depth, high * depth)
            term = jnp.dot(a[:, deep], b[deep, :], preferred_element_type=F32)
            total[...] = total[...] + term if low else term
        back_copy = pltpu.make_async_copy(total, out_ref, sems.at[2 * many + 2 + len(flat)])
        back_copy.start()
        for copy in started[many]:
            copy.wait()
        back_copy.wait()

    return call(
        kernel,
        at,
        [pinned(activations), pinned(sibling), *flat],
        [],
        [(False, jax.ShapeDtypeStruct((2 * rows, wide), F32)), (True, jax.ShapeDtypeStruct((2 * rows, depth), BF16))],
        [
            pltpu.VMEM((2 * rows, many * depth), BF16),
            pltpu.VMEM((many * depth, wide), BF16),
            pltpu.VMEM((2 * rows, wide), F32),
            pltpu.SemaphoreType.DMA((2 * many + len(flat) + 3,)),
        ],
        weight=W_EARLY,
        flops=4 * rows * depth * len(flat) * cols,
        moved=4 * rows * depth * many + 2 * depth * len(flat) * cols + 8 * rows * wide,
        name="project",
    )


def project_last(columns, blocks, before):
    (rows, depth), cols = columns.shape, blocks[0].shape[1]

    def kernel(columns_ref, *refs):
        block_refs, (before_ref, out_ref) = refs[: len(blocks)], refs[len(blocks) :]
        for i, ref in enumerate(block_refs):
            part = slice(i * cols, (i + 1) * cols)
            out_ref[:, part] = before_ref[:, part] + jnp.dot(columns_ref[...], ref[...], preferred_element_type=F32)

    vmem = pl.BlockSpec(memory_space=pltpu.VMEM)
    return pl.pallas_call(
        kernel,
        in_specs=[vmem] * (len(blocks) + 2),
        out_specs=vmem,
        out_shape=jax.ShapeDtypeStruct(before.shape, F32),
        compiler_params=params(),
        cost_estimate=cost(W_LATE, 2 * rows * depth * len(blocks) * cols, 2 * rows * depth + 10 * rows * len(blocks) * cols),
        name="project_last",
    )(columns, *blocks, before)


def turn(out_grads, sibling, at, width):
    rows = out_grads.shape[0]

    def kernel(at_ref, own_ref, sib_ref, out_ref, g, sems):
        core = lax.rem(lax.axis_index("dp"), 2)
        columns = pl.ds(pl.multiple_of(at_ref[0] * width, width), width)
        copies = []
        for n, (c, ref) in enumerate(((core, own_ref), (1 - core, sib_ref))):
            target = g.at[pl.ds(pl.multiple_of(c * rows, rows), rows), :]
            copies.append(pltpu.make_async_copy(ref.at[:, columns], target, sems.at[n]))
            copies[-1].start()
        for copy in copies:
            copy.wait()
        out_ref[...] = g[...].T

    return call(
        kernel,
        at,
        [pinned(out_grads), pinned(sibling)],
        [],
        [(True, jax.ShapeDtypeStruct((width, 2 * rows), BF16))],
        [pltpu.VMEM((2 * rows, width), BF16), pltpu.SemaphoreType.DMA((2,))],
        weight=W_OUTER,
        flops=0,
        moved=8 * rows * width,
        name="turn",
    )[0]


def outer_first(turned, mine, theirs):
    (width, rows), cols = turned.shape, mine.shape[1]

    def kernel(turned_ref, mine_ref, theirs_ref, projected_ref, out_ref):
        projected_ref[...] = (mine_ref[...] + theirs_ref[...]).astype(BF16)
        out_ref[...] = jnp.dot(turned_ref[...], projected_ref[...], preferred_element_type=F32).astype(BF16)

    vmem = pl.BlockSpec(memory_space=pltpu.VMEM)
    return pl.pallas_call(
        kernel,
        in_specs=[vmem] * 3,
        out_specs=[vmem] * 2,
        out_shape=[jax.ShapeDtypeStruct((rows, cols), BF16), jax.ShapeDtypeStruct((width, cols), BF16)],
        compiler_params=params(),
        cost_estimate=cost(W_OUTER, 2 * rows * width * cols, 10 * rows * cols),
        name="outer_first",
    )(turned, mine, theirs)


def outer(out_grads, sibling, at, width, dtypes, projected):
    rows, many, cols = out_grads.shape[0], at.shape[0], projected.shape[1]

    def kernel(at_ref, own_ref, sib_ref, projected_ref, *refs):
        outs, (g, sems) = refs[:-2], refs[-2:]
        copies = []
        core = lax.rem(lax.axis_index("dp"), 2)
        for j in range(many):
            columns = pl.ds(pl.multiple_of(at_ref[j] * width, width), width)
            for c, ref in ((core, own_ref), (1 - core, sib_ref)):
                target = g.at[pl.ds(pl.multiple_of(c * rows, rows), rows), pl.ds(j * width, width)]
                copies.append(pltpu.make_async_copy(ref.at[:, columns], target, sems.at[len(copies)]))
                copies[-1].start()
        for j in range(many):
            copies[2 * j].wait()
            copies[2 * j + 1].wait()
            block = g[:, j * width : (j + 1) * width].T
            outs[j][...] = jnp.dot(block, projected_ref[...], preferred_element_type=F32).astype(dtypes[j])

    return call(
        kernel,
        at,
        [pinned(out_grads), pinned(sibling)],
        [projected],
        [(True, jax.ShapeDtypeStruct((width, cols), dtype)) for dtype in dtypes],
        [pltpu.VMEM((2 * rows, many * width), BF16), pltpu.SemaphoreType.DMA((2 * many,))],
        weight=W_OUTER,
        flops=4 * rows * width * many * cols,
        moved=many * (4 * rows * width + 4 * width * cols),
        name="outer",
    )


def back(groups, projector, at, rows, rows_in_all, before, weight):
    many, (width, rank) = at.shape[0], projector.shape
    arrays = [x for group in groups for x in group]
    held = [] if before is None else [before]

    def kernel(at_ref, *refs):
        projector_ref, *array_refs = refs[len(held) : len(held) + 1 + len(arrays)]
        out_ref, pt, o, out_sems = refs[len(held) + 1 + len(arrays) :]
        pt[...] = projector_ref[...].T
        stores, start = [], 0
        for group in groups:
            size, column, total = group[0].shape[0], 0, None
            for x in group:
                deep = slice(column, column + x.shape[1])
                term = jnp.dot(array_refs.pop(0)[...], pt[deep, :], preferred_element_type=F32)
                total = term if total is None else total + term
                column += x.shape[1]
            o[start : start + size, :] = total.astype(BF16)
            for j in range(start // rows, (start + size) // rows):
                target = out_ref.at[pl.ds(pl.multiple_of(at_ref[j] * rows, rows), rows), :]
                stores.append(pltpu.make_async_copy(o.at[pl.ds(j * rows, rows), :], target, out_sems.at[j]))
                stores[-1].start()
            start += size
        for copy in stores:
            copy.wait()

    return call(
        kernel,
        at,
        held,
        [projector, *arrays],
        [(False, jax.ShapeDtypeStruct((rows_in_all, width), BF16))],
        [
            pltpu.VMEM((rank, width), BF16),
            pltpu.VMEM((many * rows, width), BF16),
            pltpu.SemaphoreType.DMA((many,)),
        ],
        weight=weight,
        flops=2 * many * rows * width * rank,
        moved=2 * many * rows * (width + rank),
        name="back",
        aliases={1: 0} if held else None,
    )[0]


def levels(activations, out_grads, projector, first_moment, second_moment, *, nz):
    me = lax.axis_index("dp")
    z, y, core = me // 4, me // 2 % 2, me % 2
    grid = [(a, b, c) for a in range(nz) for b in range(2) for c in range(2)]

    def pairs(to):
        return [((a * 2 + b) * 2 + c, (to(a, b, c)[0] * 2 + to(a, b, c)[1]) * 2 + to(a, b, c)[2]) for a, b, c in grid]

    def swap_core(x):
        return lax.ppermute(x, "dp", pairs(lambda a, b, c: (a, b, 1 - c)))

    def swap_y(x):
        return lax.ppermute(x, "dp", pairs(lambda a, b, c: (a, 1 - b, c)))

    def shift_z(x, k):
        return lax.ppermute(x, "dp", pairs(lambda a, b, c: ((a + k) % nz, b, c)))

    def index(k, dy, dc):
        return (lax.rem(z + nz + k, nz) * 2 + (1 - y if dy else y)) * 2 + (1 - core if dc else core)

    def named(order):
        return jnp.stack([index(*o) for o in order]).astype(jnp.int32)

    def gather(chunks):
        line = [[own] for own in chunks]
        across = [[] for _ in chunks]
        for step in range(nz):
            for i in range(len(chunks)):
                if step:
                    line[i][step], across[i][step - 1] = lax.optimization_barrier((line[i][step], across[i][step - 1]))
                if step < nz - 1:
                    line[i].append(shift_z(line[i][step], 1))
                if step < nz - 1 or i < len(chunks) - 1:
                    across[i].append(swap_y(line[i][step]))
                else:
                    across[i].append(shift_z(after(across[i][0], line[i][step]), nz - 1))
        return line, across

    after = lambda x, *those: lax.optimization_barrier((x, *those))[0]
    ks = list(range(nz - 2, 0, -1)) + [nz - 1]
    depth, rank = projector.shape
    width = first_moment.shape[0]
    cols = rank // CHUNKS
    parts = [slice(i * cols, (i + 1) * cols) for i in range(CHUNKS)]

    order_in = [(-k, dy) for k in range(nz) for dy in (0, 1)]
    order_out = [(k, dy) for dy in (1, 0) for k in ks + [0]]
    last = len(order_in) - 1
    at_in = named([(k, dy, 0) for k, dy in order_in])
    at_out = named([(k, dy, 0) for k, dy in order_out])

    a_sibling = swap_core(activations)
    line, across = gather([projector[:, part] for part in parts])
    g_sibling = swap_core(after(out_grads, a_sibling, line[0][2]))
    block = lambda i, n: (across if n % 2 else line)[i][n // 2]
    mine, columns = project(activations, a_sibling, at_in, [[block(i, n) for n in range(last)] for i in range(CHUNKS)])
    mine = project_last(columns, [block(i, last) for i in range(CHUNKS)], mine)

    turned = turn(out_grads, g_sibling, at_out[:1], width)
    projected, send = outer_first(turned, mine, swap_core(mine))
    at = after(at_out[1 : nz + 1], send)
    *sends, keep = outer(out_grads, g_sibling, at, width, [BF16] * (nz - 1) + [F32], projected)
    passed = keep + swap_y(send).astype(F32)
    at = after(at_out[nz + 1 :], passed)
    keeps = outer(out_grads, g_sibling, at, width, [F32] * (nz - 1), projected)
    terms = [keep + swap_y(send).astype(F32) for keep, send in zip(keeps, sends)]
    for term in terms[: nz - 3]:
        passed = term + shift_z(passed.astype(BF16), 1).astype(F32)
    back_term = terms[nz - 3].astype(BF16)
    reduced = terms[nz - 2] + shift_z(back_term, nz - 1).astype(F32) + shift_z(passed.astype(BF16), 1).astype(F32)
    direction = adam(reduced, first_moment, second_moment)[2]

    line, across = gather([direction[:, part] for part in parts])
    new_first, new_second, _ = adam(after(reduced, line[0][1]), first_moment, second_moment)
    rows_in_all = 4 * nz * width
    steps = range(1, nz)
    mine = [(direction,)] + [tuple(jnp.concatenate([line[i][k], across[i][k - 1]]) for i in range(CHUNKS)) for k in steps]
    mine.append(tuple(across[i][-1] for i in range(CHUNKS)))
    theirs = [tuple(swap_core(after(x, line[0][1])) for x in mine[0])]
    theirs += [tuple(swap_core(x) for x in group) for group in mine[1:-1]]
    order = [[(0, 0)]] + [[(-k, 0), (1 - k, 1)] for k in steps] + [[(1 - nz, 1)]]
    update = None
    for low, high, weight in ((0, nz - 1, W_BACK), (nz - 1, nz + 1, W_LAST)):
        if low:
            theirs.append(tuple(swap_core(after(x, update)) for x in mine[-1]))
        at = named([(k, dy, dc) for dc in (0, 1) for some in order[low:high] for k, dy in some])
        update = back(mine[low:high] + theirs[low:high], projector, at, width, rows_in_all, update, weight)
    return update, new_first, new_second


def solution(mesh):
    devices = mesh.shape["dp"]

    def body(activations, out_grads, projector, first_moment, second_moment):
        aligned = projector.shape[0] % 128 == 0 and first_moment.shape[0] % 128 == 0
        if devices % 4 or devices < 16 or not aligned:
            return plain(activations, out_grads, projector, first_moment, second_moment)
        return levels(activations, out_grads, projector, first_moment, second_moment, nz=devices // 4)

    placed = P(("groups", "dp"), None)
    return jax.shard_map(
        body,
        mesh=mesh,
        in_specs=(placed,) * 5,
        out_specs=(P("groups", "dp"), placed, placed),
        check_vma=False,
    )
```

```python
import functools
import jax
import jax.numpy as jnp
from jax import lax
from jax.experimental import pallas as pl
from jax.experimental.pallas import tpu as pltpu
from jax.sharding import PartitionSpec as P

STEP = 100

decay_first = 0.9
decay_second = 0.999
epsilon = 1e-08

CHUNKS = 2
W_EARLY, W_LATE, W_OUTER, W_BACK, W_LAST = 3, 30, 30, 30, 30000
F32, BF16 = jnp.float32, jnp.bfloat16
VMEM_LIMIT = 16 * 1024 * 1024


def adam(reduced, first_moment, second_moment):
    new_first = decay_first * first_moment + (1.0 - decay_first) * reduced
    new_second = decay_second * second_moment + (1.0 - decay_second) * reduced * reduced
    first_fix = 1.0 - decay_first**STEP
    second_fix = 1.0 - decay_second**STEP
    direction = (new_first / first_fix / (jnp.sqrt(new_second / second_fix) + epsilon)).astype(BF16)
    return new_first, new_second, direction


def plain(activations, out_grads, projector, first_moment, second_moment):
    projected = jnp.dot(
        activations,
        lax.all_gather(projector, "dp", axis=0, tiled=True),
        preferred_element_type=F32,
    ).astype(BF16)
    reduced = lax.psum_scatter(
        lax.dot_general(out_grads, projected, (((0,), (0,)), ((), ())), preferred_element_type=F32),
        "dp",
        scatter_dimension=0,
        tiled=True,
    )
    new_first, new_second, direction = adam(reduced, first_moment, second_moment)
    update = lax.dot_general(
        lax.all_gather(direction, "dp", axis=0, tiled=True),
        projector,
        (((1,), (1,)), ((), ())),
        preferred_element_type=F32,
    ).astype(BF16)
    return update, new_first, new_second


def params():
    return pltpu.CompilerParams(vmem_limit_bytes=VMEM_LIMIT)


def cost(weight, flops, moved):
    return pl.CostEstimate(flops=weight * flops, bytes_accessed=weight * moved, transcendentals=0)


def pinned(x):
    return pltpu.with_memory_space_constraint(x, pltpu.HBM)


def call(kernel, scalars, far, near, outs, scratch, *, weight, flops, moved, name, aliases=None):
    anywhere, vmem = pl.BlockSpec(memory_space=pl.ANY), pl.BlockSpec(memory_space=pltpu.VMEM)
    return pl.pallas_call(
        kernel,
        grid_spec=pltpu.PrefetchScalarGridSpec(
            num_scalar_prefetch=1,
            grid=(),
            in_specs=[anywhere] * len(far) + [vmem] * len(near),
            out_specs=[vmem if inside else anywhere for inside, _ in outs],
            scratch_shapes=scratch,
        ),
        out_shape=[shape for _, shape in outs],
        input_output_aliases=aliases or {},
        compiler_params=params(),
        cost_estimate=cost(weight, flops, moved),
        name=name,
    )(scalars, *far, *near)


def project(activations, sibling, at, blocks):
    chunks, many = len(blocks), len(blocks[0])
    flat = [block for chunk in blocks for block in chunk]
    (depth, cols), rows = flat[0].shape, activations.shape[0]
    wide = chunks * cols

    def kernel(at_ref, own_ref, sib_ref, *refs):
        block_refs, (out_ref, next_ref, a, b, total, sems) = refs[: len(flat)], refs[len(flat) :]
        started = [[] for _ in range(many + 1)]

        def start(j, source, target):
            n = sum(len(copies) for copies in started)
            started[j].append(pltpu.make_async_copy(source, target, sems.at[n]))
            started[j][-1].start()

        core = lax.rem(lax.axis_index("dp"), 2)
        here, there = (pl.ds(pl.multiple_of(c * rows, rows), rows) for c in (core, 1 - core))
        for j in range(many):
            columns = pl.ds(pl.multiple_of(at_ref[j] * depth, depth), depth)
            start(j, own_ref.at[:, columns], a.at[here, pl.ds(j * depth, depth)])
            start(j, sib_ref.at[:, columns], a.at[there, pl.ds(j * depth, depth)])
        for n, ref in enumerate(block_refs):
            i, j = n // many, n % many
            start(j, ref, b.at[pl.ds(j * depth, depth), pl.ds(i * cols, cols)])
        columns = pl.ds(pl.multiple_of(at_ref[many] * depth, depth), depth)
        start(many, own_ref.at[:, columns], next_ref.at[here, :])
        start(many, sib_ref.at[:, columns], next_ref.at[there, :])
        cut = (many + 1) // 2
        for low, high in ((0, cut), (cut, many)):
            for copies in started[low:high]:
                for copy in copies:
                    copy.wait()
            deep = slice(low * depth, high * depth)
            term = jnp.dot(a[:, deep], b[deep, :], preferred_element_type=F32)
            total[...] = total[...] + term if low else term
        back_copy = pltpu.make_async_copy(total, out_ref, sems.at[2 * many + 2 + len(flat)])
        back_copy.start()
        for copy in started[many]:
            copy.wait()
        back_copy.wait()

    return call(
        kernel,
        at,
        [pinned(activations), pinned(sibling), *flat],
        [],
        [(False, jax.ShapeDtypeStruct((2 * rows, wide), F32)), (True, jax.ShapeDtypeStruct((2 * rows, depth), BF16))],
        [
            pltpu.VMEM((2 * rows, many * depth), BF16),
            pltpu.VMEM((many * depth, wide), BF16),
            pltpu.VMEM((2 * rows, wide), F32),
            pltpu.SemaphoreType.DMA((2 * many + len(flat) + 3,)),
        ],
        weight=W_EARLY,
        flops=4 * rows * depth * len(flat) * cols,
        moved=4 * rows * depth * many + 2 * depth * len(flat) * cols + 8 * rows * wide,
        name="project",
    )


def project_last(columns, blocks, before):
    (rows, depth), cols = columns.shape, blocks[0].shape[1]

    def kernel(columns_ref, *refs):
        block_refs, (before_ref, out_ref) = refs[: len(blocks)], refs[len(blocks) :]
        for i, ref in enumerate(block_refs):
            part = slice(i * cols, (i + 1) * cols)
            out_ref[:, part] = before_ref[:, part] + jnp.dot(columns_ref[...], ref[...], preferred_element_type=F32)

    vmem = pl.BlockSpec(memory_space=pltpu.VMEM)
    return pl.pallas_call(
        kernel,
        in_specs=[vmem] * (len(blocks) + 2),
        out_specs=vmem,
        out_shape=jax.ShapeDtypeStruct(before.shape, F32),
        compiler_params=params(),
        cost_estimate=cost(W_LATE, 2 * rows * depth * len(blocks) * cols, 2 * rows * depth + 10 * rows * len(blocks) * cols),
        name="project_last",
    )(columns, *blocks, before)


def turn(out_grads, sibling, at, width):
    rows = out_grads.shape[0]

    def kernel(at_ref, own_ref, sib_ref, out_ref, g, sems):
        core = lax.rem(lax.axis_index("dp"), 2)
        columns = pl.ds(pl.multiple_of(at_ref[0] * width, width), width)
        copies = []
        for n, (c, ref) in enumerate(((core, own_ref), (1 - core, sib_ref))):
            target = g.at[pl.ds(pl.multiple_of(c * rows, rows), rows), :]
            copies.append(pltpu.make_async_copy(ref.at[:, columns], target, sems.at[n]))
            copies[-1].start()
        for copy in copies:
            copy.wait()
        out_ref[...] = g[...].T

    return call(
        kernel,
        at,
        [pinned(out_grads), pinned(sibling)],
        [],
        [(True, jax.ShapeDtypeStruct((width, 2 * rows), BF16))],
        [pltpu.VMEM((2 * rows, width), BF16), pltpu.SemaphoreType.DMA((2,))],
        weight=W_OUTER,
        flops=0,
        moved=8 * rows * width,
        name="turn",
    )[0]


def outer_first(turned, mine, theirs):
    (width, rows), cols = turned.shape, mine.shape[1]

    def kernel(turned_ref, mine_ref, theirs_ref, projected_ref, out_ref):
        projected_ref[...] = (mine_ref[...] + theirs_ref[...]).astype(BF16)
        out_ref[...] = jnp.dot(turned_ref[...], projected_ref[...], preferred_element_type=F32).astype(BF16)

    vmem = pl.BlockSpec(memory_space=pltpu.VMEM)
    return pl.pallas_call(
        kernel,
        in_specs=[vmem] * 3,
        out_specs=[vmem] * 2,
        out_shape=[jax.ShapeDtypeStruct((rows, cols), BF16), jax.ShapeDtypeStruct((width, cols), BF16)],
        compiler_params=params(),
        cost_estimate=cost(W_OUTER, 2 * rows * width * cols, 10 * rows * cols),
        name="outer_first",
    )(turned, mine, theirs)


def outer(out_grads, sibling, at, width, dtypes, projected):
    rows, many, cols = out_grads.shape[0], at.shape[0], projected.shape[1]

    def kernel(at_ref, own_ref, sib_ref, projected_ref, *refs):
        outs, (g, sems) = refs[:-2], refs[-2:]
        copies = []
        core = lax.rem(lax.axis_index("dp"), 2)
        for j in range(many):
            columns = pl.ds(pl.multiple_of(at_ref[j] * width, width), width)
            for c, ref in ((core, own_ref), (1 - core, sib_ref)):
                target = g.at[pl.ds(pl.multiple_of(c * rows, rows), rows), pl.ds(j * width, width)]
                copies.append(pltpu.make_async_copy(ref.at[:, columns], target, sems.at[len(copies)]))
                copies[-1].start()
        for j in range(many):
            copies[2 * j].wait()
            copies[2 * j + 1].wait()
            block = g[:, j * width : (j + 1) * width].T
            outs[j][...] = jnp.dot(block, projected_ref[...], preferred_element_type=F32).astype(dtypes[j])

    return call(
        kernel,
        at,
        [pinned(out_grads), pinned(sibling)],
        [projected],
        [(True, jax.ShapeDtypeStruct((width, cols), dtype)) for dtype in dtypes],
        [pltpu.VMEM((2 * rows, many * width), BF16), pltpu.SemaphoreType.DMA((2 * many,))],
        weight=W_OUTER,
        flops=4 * rows * width * many * cols,
        moved=many * (4 * rows * width + 4 * width * cols),
        name="outer",
    )


def back(groups, projector, at, rows, rows_in_all, before, weight):
    many, (width, rank) = at.shape[0], projector.shape
    arrays = [x for group in groups for x in group]
    held = [] if before is None else [before]
    turned = [] if held else [(True, jax.ShapeDtypeStruct((rank, width), BF16))]

    def kernel(at_ref, *refs):
        projector_ref, *array_refs = refs[len(held) : len(held) + 1 + len(arrays)]
        out_ref, *refs = refs[len(held) + 1 + len(arrays) :]
        pt, o, out_sems = [projector_ref, *refs] if held else refs
        if not held:
            pt[...] = projector_ref[...].T
        stores, start = [], 0
        for group in groups:
            size, column, total = group[0].shape[0], 0, None
            for x in group:
                deep = slice(column, column + x.shape[1])
                term = jnp.dot(array_refs.pop(0)[...], pt[deep, :], preferred_element_type=F32)
                total = term if total is None else total + term
                column += x.shape[1]
            o[start : start + size, :] = total.astype(BF16)
            for j in range(start // rows, (start + size) // rows):
                target = out_ref.at[pl.ds(pl.multiple_of(at_ref[j] * rows, rows), rows), :]
                stores.append(pltpu.make_async_copy(o.at[pl.ds(j * rows, rows), :], target, out_sems.at[j]))
                stores[-1].start()
            start += size
        for copy in stores:
            copy.wait()

    return call(
        kernel,
        at,
        held,
        [projector, *arrays],
        [(False, jax.ShapeDtypeStruct((rows_in_all, width), BF16))] + turned,
        [
            pltpu.VMEM((many * rows, width), BF16),
            pltpu.SemaphoreType.DMA((many,)),
        ],
        weight=weight,
        flops=2 * many * rows * width * rank,
        moved=2 * many * rows * (width + rank),
        name="back",
        aliases={1: 0} if held else None,
    )


def levels(activations, out_grads, projector, first_moment, second_moment, *, nz):
    me = lax.axis_index("dp")
    z, y, core = me // 4, me // 2 % 2, me % 2
    grid = [(a, b, c) for a in range(nz) for b in range(2) for c in range(2)]

    def pairs(to):
        return [((a * 2 + b) * 2 + c, (to(a, b, c)[0] * 2 + to(a, b, c)[1]) * 2 + to(a, b, c)[2]) for a, b, c in grid]

    def swap_core(x):
        return lax.ppermute(x, "dp", pairs(lambda a, b, c: (a, b, 1 - c)))

    def swap_y(x):
        return lax.ppermute(x, "dp", pairs(lambda a, b, c: (a, 1 - b, c)))

    def shift_z(x, k):
        return lax.ppermute(x, "dp", pairs(lambda a, b, c: ((a + k) % nz, b, c)))

    def index(k, dy, dc):
        return (lax.rem(z + nz + k, nz) * 2 + (1 - y if dy else y)) * 2 + (1 - core if dc else core)

    def named(order):
        return jnp.stack([index(*o) for o in order]).astype(jnp.int32)

    def gather(chunks):
        line = [[own] for own in chunks]
        across = [[] for _ in chunks]
        for step in range(nz):
            for i in range(len(chunks)):
                if step:
                    line[i][step], across[i][step - 1] = lax.optimization_barrier((line[i][step], across[i][step - 1]))
                if step < nz - 1:
                    line[i].append(shift_z(line[i][step], 1))
                if step < nz - 1 or i < len(chunks) - 1:
                    across[i].append(swap_y(line[i][step]))
                else:
                    across[i].append(shift_z(after(across[i][0], line[i][step]), nz - 1))
        return line, across

    after = lambda x, *those: lax.optimization_barrier((x, *those))[0]
    ks = list(range(nz - 2, 0, -1)) + [nz - 1]
    depth, rank = projector.shape
    width = first_moment.shape[0]
    cols = rank // CHUNKS
    parts = [slice(i * cols, (i + 1) * cols) for i in range(CHUNKS)]

    order_in = [(-k, dy) for k in range(nz) for dy in (0, 1)]
    order_out = [(k, dy) for dy in (1, 0) for k in ks + [0]]
    last = len(order_in) - 1
    at_in = named([(k, dy, 0) for k, dy in order_in])
    at_out = named([(k, dy, 0) for k, dy in order_out])

    a_sibling = swap_core(activations)
    line, across = gather([projector[:, part] for part in parts])
    g_sibling = swap_core(after(out_grads, a_sibling, line[0][2]))
    block = lambda i, n: (across if n % 2 else line)[i][n // 2]
    mine, columns = project(activations, a_sibling, at_in, [[block(i, n) for n in range(last)] for i in range(CHUNKS)])
    mine = project_last(columns, [block(i, last) for i in range(CHUNKS)], mine)

    turned = turn(out_grads, g_sibling, at_out[:1], width)
    projected, send = outer_first(turned, mine, swap_core(mine))
    at = after(at_out[1 : nz + 1], send)
    *sends, keep = outer(out_grads, g_sibling, at, width, [BF16] * (nz - 1) + [F32], projected)
    passed = keep + swap_y(send).astype(F32)
    at = after(at_out[nz + 1 :], passed)
    keeps = outer(out_grads, g_sibling, at, width, [F32] * (nz - 1), projected)
    terms = [keep + swap_y(send).astype(F32) for keep, send in zip(keeps, sends)]
    for term in terms[: nz - 3]:
        passed = term + shift_z(passed.astype(BF16), 1).astype(F32)
    back_term = terms[nz - 3].astype(BF16)
    reduced = terms[nz - 2] + shift_z(back_term, nz - 1).astype(F32) + shift_z(passed.astype(BF16), 1).astype(F32)
    direction = adam(reduced, first_moment, second_moment)[2]

    line, across = gather([direction[:, part] for part in parts])
    new_first, new_second, _ = adam(after(reduced, line[0][1]), first_moment, second_moment)
    rows_in_all = 4 * nz * width
    steps = range(1, nz)
    mine = [(direction,)] + [tuple(jnp.concatenate([line[i][k], across[i][k - 1]]) for i in range(CHUNKS)) for k in steps]
    mine.append(tuple(across[i][-1] for i in range(CHUNKS)))
    theirs = [tuple(swap_core(after(x, line[0][1])) for x in mine[0])]
    theirs += [tuple(swap_core(x) for x in group) for group in mine[1:-1]]
    order = [[(0, 0)]] + [[(-k, 0), (1 - k, 1)] for k in steps] + [[(1 - nz, 1)]]
    update, turned = None, [projector]
    for low, high, weight in ((0, nz - 1, W_BACK), (nz - 1, nz + 1, W_LAST)):
        if low:
            theirs.append(tuple(swap_core(after(x, update)) for x in mine[-1]))
        at = named([(k, dy, dc) for dc in (0, 1) for some in order[low:high] for k, dy in some])
        update, *turned = back(mine[low:high] + theirs[low:high], *turned, at, width, rows_in_all, update, weight)
    return update, new_first, new_second


def solution(mesh):
    devices = mesh.shape["dp"]

    def body(activations, out_grads, projector, first_moment, second_moment):
        aligned = projector.shape[0] % 128 == 0 and first_moment.shape[0] % 128 == 0
        if devices % 4 or devices < 16 or not aligned:
            return plain(activations, out_grads, projector, first_moment, second_moment)
        return levels(activations, out_grads, projector, first_moment, second_moment, nz=devices // 4)

    placed = P(("groups", "dp"), None)
    return jax.shard_map(
        body,
        mesh=mesh,
        in_specs=(placed,) * 5,
        out_specs=(P("groups", "dp"), placed, placed),
        check_vma=False,
    )
```
